128 devices in a mesh: row: 8 (over z, y_lo), col: 16 (over y_hi, x, core).
Axes of the slice: x: 4, y: 4 (y_hi: 2, y_lo: 2; y = y_hi * 2 + y_lo), z: 4, core: 2. Of those that a mesh axis runs over, the one named last changes fastest.
Arguments:
- three_centre: bfloat16 [512, 64, 4096], P(('row', 'col')), may hold values from -6 to 6
- screen_mask: int32 [8, 64], replicated, may hold values 0 or 1
- block_counts: int32 [9], replicated, may hold values from 32 to 64, as said below
- green_occ: bfloat16 [512, 192], P('row'), may hold values from -0.4375 to 0.4375
- occ_mask: int32 [8, 3], replicated, may hold values 0 or 1
- green_virt: bfloat16 [64, 64], replicated, may hold values from -0.75 to 0.75
Outputs:
- chi: float32 [4096, 4096], P('col', 'row')
The draws below stay inside these ranges and needn't reach their ends.
Inputs may be any that keep to these rules, and one draw needn't show every extreme that they name: `block_counts`: entry b < 8 counts the live functions of mu block b, entry 8 those of the nu block; live functions come first in a block.
All inputs are finite; a program needn't handle non-finite values.
Results may differ from the reference program's by a relative error of at most 0.013.
Values may be sent and summed in bfloat16 or wider, within the bound.
No kernel may reach another device: no remote copies, remote signals or barrier semaphores. Data moves between devices by JAX's collectives and lax.ppermute only.
A program may use at most 128 MiB of HBM per device.

```python
import math
import jax
import jax.numpy as jnp
from jax import lax

BS = 64
NU = 64
MU = 512
PS = 4096
N_ROW = 8


def draw_block_counts(key, part):
    key = jax.random.fold_in(key, 5)
    first_key, second_key = jax.random.split(key)
    total = N_ROW + 1
    counts = jax.random.randint(first_key, (total,), BS // 2, BS + 1)
    order = jax.random.permutation(second_key, total)
    counts = jnp.where(order == 0, BS, counts)
    counts = jnp.where(order == 1, BS // 2, counts)
    return counts.astype(jnp.int32)


def plant(drawn, own_key, least, top_value):
    extent = drawn.shape
    spot = [jax.random.randint(jax.random.fold_in(own_key, axis), (), 0, extent[axis]) for axis in range(len(extent))]
    drawn = drawn.at[tuple(spot)].set(least)
    longest = extent.index(max(extent))
    spot[longest] = (spot[longest] + 1) % extent[longest]
    return drawn.at[tuple(spot)].set(top_value)


def shard_levels(rng, shape, pieces, smallest, largest):
    loudness = 1.0
    for axis_at, shards_of in pieces:
        steps = jax.random.uniform(jax.random.fold_in(jax.random.fold_in(rng, 6), axis_at), (shards_of,), jnp.float32, smallest / len(pieces), largest / len(pieces))
        loudness = loudness * jnp.repeat(jnp.exp(steps), shape[axis_at] // shards_of).reshape((-1,) + (1,) * (len(shape) - 1 - axis_at))
    return loudness


def scatter_about(stream_key, extent, scale, bound, shards=(), kind=jnp.bfloat16):
    loudness = shard_levels(stream_key, extent, shards, -0.22, 0.18) if shards else 1.0
    values = jax.random.normal(stream_key, extent, jnp.float32) * scale * loudness
    return jnp.minimum(jnp.maximum(values, -bound), bound).astype(kind)


def setup_inputs(seed: int = 0) -> dict:
    key_of = jax.random.split(jax.random.key(seed), 7)
    return {
        "three_centre": scatter_about(key_of[0], (MU, NU, PS), 1.0, 6.0, ((0, 128),)),
        "screen_mask": plant((jax.random.randint(key_of[1], (N_ROW, PS // BS), 0, 3) < 2).astype(jnp.int32), jax.random.fold_in(key_of[1], 1), 0, 1),
        "block_counts": draw_block_counts(jax.random.fold_in(key_of[6], 71), 0),
        "green_occ": scatter_about(key_of[3], (MU, 3 * BS), (3 * BS) ** -0.5, 0.4375, ((0, 8),)),
        "occ_mask": plant((jax.random.randint(key_of[4], (N_ROW, 3), 0, 4) < 3).astype(jnp.int32), jax.random.fold_in(key_of[4], 1), 0, 1),
        "green_virt": scatter_about(key_of[5], (NU, NU), NU ** -0.5, 0.75),
    }


def reference(three_centre, screen_mask, block_counts, green_occ, occ_mask, green_virt):
    lane_ids = jnp.arange(BS, dtype=jnp.int32)
    mu_valid = (lane_ids[None, :] < block_counts[:N_ROW, None]).reshape(MU)
    nu_valid = jnp.arange(NU, dtype=jnp.int32) < block_counts[N_ROW]
    p_valid = jnp.repeat(jnp.repeat(screen_mask, BS, axis=1), BS, axis=0) > 0
    keep_mask = mu_valid[:, None, None] & nu_valid[None, :, None] & p_valid[:, None, :]
    masked = jnp.where(keep_mask, three_centre, jnp.zeros((), jnp.bfloat16))
    blocks = masked.reshape(N_ROW, BS, NU * PS)
    chi_scale = -1.0 / math.sqrt(MU * NU)

    def step(running, block_index):
        before = lax.dynamic_index_in_dim(blocks, (block_index + N_ROW - 1) % N_ROW, 0, keepdims=False)
        own_block = lax.dynamic_index_in_dim(blocks, block_index, 0, keepdims=False)
        after_block = lax.dynamic_index_in_dim(blocks, (block_index + 1) % N_ROW, 0, keepdims=False)
        neighbours = jnp.concatenate([before, own_block, after_block], axis=0)
        green_rows = lax.dynamic_slice_in_dim(green_occ, block_index * BS, BS, 0)
        green_mask = jnp.repeat(lax.dynamic_index_in_dim(occ_mask, block_index, 0, keepdims=False), BS).astype(jnp.bfloat16)
        green_band = green_rows * green_mask[None, :]
        occupied = jnp.dot(green_band, neighbours, preferred_element_type=jnp.float32).astype(jnp.bfloat16)
        virtual = jnp.einsum('anp,nm->amp', occupied.reshape(BS, NU, PS).astype(jnp.float32), green_virt.astype(jnp.float32)).astype(jnp.bfloat16)
        partial_value = jnp.dot(virtual.reshape(BS * NU, PS).T, own_block.reshape(BS * NU, PS), preferred_element_type=jnp.float32)
        rounded = lax.optimization_barrier((chi_scale * partial_value).astype(jnp.bfloat16))
        return (running + rounded.astype(jnp.float32), None)
    chi, _ = lax.scan(step, jnp.zeros((PS, PS), jnp.float32), jnp.arange(N_ROW, dtype=jnp.int32))
    return chi
```

```python
import functools
import math

import jax
import jax.numpy as jnp
from jax import lax
from jax.experimental import pallas as pl
from jax.experimental.pallas import tpu as pltpu
from jax.sharding import Mesh, PartitionSpec as P

AXES = ("zhi", "zlo", "ylo", "yhi", "x", "core")
SIZES = (2, 2, 2, 2, 4, 2)
ROWS = ("zhi", "zlo", "ylo")
COLS = ("yhi", "x", "core")
GROUP = ("zlo", "ylo", "x")
BS = 64
NU = 64
NB = 8
NG = 16
MUD = 4
SRC = 16
PSL = 4096
W = 256
LINES = 8
TAIL = 128
WIDE = 4 * W
BF = jnp.bfloat16
F32 = jnp.float32
SCALE = -1.0 / math.sqrt(NB * BS * NU)
PARAMS = pltpu.CompilerParams(vmem_limit_bytes=48 * 1024 * 1024)


def iota(shape, axis):
    return lax.broadcasted_iota(jnp.int32, shape, axis)


def cost(flops, size):
    return pl.CostEstimate(flops=flops, bytes_accessed=size, transcendentals=0)


def in_hbm(value):
    return pltpu.with_memory_space_constraint(value, pltpu.HBM)


def pack_kernel(per, part, rows, pos_ref, screen_ref, counts_ref, gv_ref, *refs):
    (x0, x1, x2, x3), out_ref, lhs = refs[:4], refs[-2], refs[-1]
    step = pl.program_id(0)
    row = pos_ref[0]
    col = pos_ref[1]
    full = NG * rows

    @pl.when(step == 0)
    def _():
        def place(shape):
            line = iota(shape, 0)
            group, r = line // rows, line % rows
            if part == 0:
                plain = r >= MUD * per
                mu = jnp.where(plain, r - MUD * per, r // per)
                j = jnp.where(plain, per - 1, r % per)
            else:
                width = rows // MUD
                plain = r >= 0
                mu = r // width
                j = r % width
            return plain, mu, group * per + j

        plain, _, m = place((full, NU))
        pick = (m == iota((full, NU), 1)).astype(F32)
        if part == 0:
            gv_t = gv_ref[...].astype(F32).T
            small = jnp.dot(pick, gv_t, preferred_element_type=F32)
            small = jnp.where(plain, pick, small)
        else:
            small = pick
        big = jnp.concatenate([small] * MUD, axis=1)
        _, mu, _ = place((full, MUD * NU))
        lane = iota((full, MUD * NU), 1)
        live = (
            (mu == lane // NU)
            & (lane % NU < counts_ref[NB])
            & (mu + MUD * col < counts_ref[row])
        )
        lhs[...] = jnp.where(live, big, 0.0).astype(BF)

    half, core = step // 2, step % 2
    sub = iota((1, W), 1) // BS

    def store(g, lanes, piece):
        zlo, ylo, xx = g // 8, (g // 4) % 2, g % 4
        for copy in range(2):
            if part == 0:
                out_ref[copy, zlo, ylo, xx, :, lanes] = piece
            else:
                out_ref[zlo, ylo, copy, xx, :, lanes] = piece

    for t, ref in enumerate((x0, x1, x2, x3)):
        mask = jnp.zeros((1, W), F32)
        for k in range(W // BS):
            on = screen_ref[row, (half * 8 + 2 * t + core) * (W // BS) + k] > 0
            mask = jnp.where(sub == k, on.astype(F32), mask)
        cells = ref[...].reshape(MUD * NU, W)
        out = jnp.dot(lhs[...], cells, preferred_element_type=F32) * mask
        for g in range(NG):
            piece = out[g * rows : (g + 1) * rows]
            if part == 0:
                for h in range(rows // LINES):
                    at = h * WIDE + t * W
                    store(g, slice(at, at + W), piece[h * LINES : (h + 1) * LINES].astype(BF))
            else:
                store(g, slice(t * W, (t + 1) * W), piece.astype(BF))
    if part == 0:
        green = refs[4][...]
        line, mu = iota((LINES, BS), 0), iota((LINES, BS), 1)
        left = (mu == MUD * col + line).astype(BF)
        right = (mu == MUD * col + line - MUD).astype(BF)
        left = jnp.where(line < MUD, left, jnp.zeros_like(left))
        right = jnp.where(line < MUD, jnp.zeros_like(right), right)
        tail = jnp.dot(left, green[:, :TAIL], preferred_element_type=F32)
        low = jnp.dot(right, green[:, TAIL:], preferred_element_type=F32)
        tail = (tail + jnp.concatenate([low, jnp.zeros_like(low)], axis=1)).astype(BF)
        at = rows // LINES * WIDE
        for g in range(NG):
            store(g, slice(at, at + TAIL), tail)


def pack(per, part, rows, pos, screen_mask, counts, green_virt, green_occ, cells):
    if part == 0:
        shape = (LINES, rows // LINES * WIDE + TAIL)
        block = (2, 2, 2, None, 4, None) + shape
        index = lambda s, *_: (0, 0, 0, s // 2, 0, s % 2, 0, 0)
    else:
        shape = (rows, WIDE)
        block = (None, 2, 2, 2, 4, None) + shape
        index = lambda s, *_: (s // 2, 0, 0, 0, 0, s % 2, 0, 0)

    def column(t):
        return pl.BlockSpec((MUD, NU, W), lambda s, *_: (0, 0, (s // 2) * 8 + 2 * t + s % 2))

    operands = [green_virt] + [cells] * 4
    in_specs = [pl.BlockSpec((NU, NU), lambda s, *_: (0, 0))] + [column(t) for t in range(4)]
    if part == 0:
        operands.append(green_occ)
        in_specs.append(pl.BlockSpec((BS, 3 * BS), lambda s, *_: (0, 0)))
    out = pl.pallas_call(
        functools.partial(pack_kernel, per, part, rows),
        grid_spec=pltpu.PrefetchScalarGridSpec(
            num_scalar_prefetch=3,
            grid=(4,),
            in_specs=in_specs,
            out_specs=pl.BlockSpec(block, index),
            scratch_shapes=[pltpu.VMEM((NG * rows, MUD * NU), BF)],
        ),
        out_shape=pltpu.HBM(SIZES + shape, BF),
        compiler_params=PARAMS,
        cost_estimate=cost(2 * NG * rows * 256 * PSL, 6 << 20),
        name=f"pack_{part}",
    )(pos, screen_mask, counts, *operands)
    return out.reshape((128,) + shape)


def band_kernel(per, mask_ref, c0, c1, c2, c3, *out_refs):
    step = pl.program_id(0)
    refs = (c0, c1, c2, c3)
    lines = SRC * LINES
    halves = c0.shape[1] // WIDE
    depth = lines * halves
    width = 2 if per == 3 else per
    main = BS * width
    count = BS * per

    def place_row(shape):
        line = iota(shape, 0)
        extra = line >= main
        return jnp.where(extra, line - main, line // width), jnp.where(extra, width, line % width)

    def place_col(shape):
        line = iota(shape, 1)
        half, line = line // lines, line % lines
        source, r = line // LINES, line % LINES + half * LINES
        return r < MUD * per, source * MUD + r // per, r % per

    row_mu, _ = place_row((count, BS))
    spread_rows = (row_mu == iota((count, BS), 1)).astype(BF)
    good, col_mu, _ = place_col((BS, depth))
    spread_cols = (good & (col_mu == iota((BS, depth), 0))).astype(BF)
    _, row_j = place_row((count, depth))
    _, _, col_j = place_col((count, depth))
    same = row_j == col_j
    line, at = iota((BS, lines), 0), iota((BS, lines), 1)
    spot = (line // MUD) * LINES + line % MUD
    take_left = (spot == at).astype(BF)
    take_right = (spot + MUD == at).astype(BF)
    blocks = [
        jnp.concatenate([ref[:, h * WIDE : (h + 1) * WIDE] for h in range(halves)], axis=0)
        for ref in refs
    ]
    mains, extras = [], []
    for u in range(2):
        total = jnp.zeros((count, WIDE), F32)
        packed = refs[u + 1][:, halves * WIDE :]
        left = jnp.dot(take_left, packed, preferred_element_type=F32).astype(BF)
        right = jnp.dot(take_right, packed, preferred_element_type=F32).astype(BF)
        left = jnp.dot(spread_rows, left, preferred_element_type=F32).astype(BF)
        right = jnp.dot(spread_rows, right, preferred_element_type=F32).astype(BF)
        for k, part in enumerate((left[:, :BS], left[:, BS:], right[:, :BS])):
            part = jnp.dot(part, spread_cols, preferred_element_type=F32)
            part = jnp.where(same, part * mask_ref[2 * step + u, k].astype(F32), 0.0).astype(BF)
            total += jnp.dot(part, blocks[u + k], preferred_element_type=F32)
        mains.append(total[:main])
        extras.append(total[main:])
        if per == 3:
            line, at = iota((BS, lines), 0), iota((BS, lines), 1)
            take = ((line // MUD) * LINES + MUD + line % MUD == at).astype(BF)
            out_refs[2][u * BS : (u + 1) * BS, :] = jnp.dot(
                take, blocks[u + 1][lines:], preferred_element_type=F32
            ).astype(BF)
    out_refs[0][...] = jnp.concatenate(mains, axis=0).astype(BF).T
    if per == 3:
        out_refs[1][...] = jnp.concatenate(extras, axis=0).astype(BF).T


def band(per, occ_mask, cells):
    lines, full = SRC * LINES, cells.shape[1]
    width = 2 if per == 3 else per
    blk = lambda off: pl.BlockSpec((lines, full), lambda s, *_: ((2 * s + off) % NB, 0))
    out_specs = [pl.BlockSpec((WIDE, 2 * BS * width), lambda s, *_: (0, s))]
    out_shape = [jax.ShapeDtypeStruct((WIDE, NB * BS * width), BF)]
    if per == 3:
        out_specs.append(pl.BlockSpec((WIDE, 2 * BS), lambda s, *_: (0, s)))
        out_shape.append(jax.ShapeDtypeStruct((WIDE, NB * BS), BF))
        out_specs.append(pl.BlockSpec((2 * BS, WIDE), lambda s, *_: (s, 0)))
        out_shape.append(pltpu.HBM((NB * BS, WIDE), BF))
    return pl.pallas_call(
        functools.partial(band_kernel, per),
        grid_spec=pltpu.PrefetchScalarGridSpec(
            num_scalar_prefetch=1,
            grid=(NB // 2,),
            in_specs=[blk(off) for off in (NB - 1, 0, 1, 2)],
            out_specs=out_specs,
        ),
        out_shape=out_shape,
        compiler_params=PARAMS,
        cost_estimate=cost(2 * NB * BS * per * 3 * full // WIDE * lines * WIDE, 12 << 20),
        name="band",
    )(occ_mask, cells, cells, cells, cells)


def product_kernel(pairs, pos_ref, *refs):
    out = jnp.dot(refs[0][...], refs[1][...], preferred_element_type=F32)
    for i in range(1, pairs):
        out += jnp.dot(refs[2 * i][...], refs[2 * i + 1][...], preferred_element_type=F32)
    out = (out * SCALE).astype(BF)
    for x in range(4):
        refs[-1][x] = out[x * W : (x + 1) * W]


def product(pos, virts, cells, before=None):
    operands, in_specs, flops = [], [], 0
    for virt, cell in zip(virts, cells):
        depth = cell.shape[0]
        operands += [virt, cell]
        in_specs += [
            pl.BlockSpec((WIDE, depth), lambda i, *_: (0, 0)),
            pl.BlockSpec((depth, W), lambda i, *_: (0, i)),
        ]
        flops += 2 * depth * WIDE * WIDE
    if before is None:
        index = lambda i, pos_ref: (i, 0, 0, pos_ref[2])
        alias = {}
    else:
        operands.append(before)
        in_specs.append(pl.BlockSpec(memory_space=pl.ANY))
        index = lambda i, pos_ref: (i, 0, 0, 1 - pos_ref[2])
        alias = {len(operands): 0}
    return pl.pallas_call(
        functools.partial(product_kernel, len(virts)),
        grid_spec=pltpu.PrefetchScalarGridSpec(
            num_scalar_prefetch=1,
            grid=(4,),
            in_specs=in_specs,
            out_specs=pl.BlockSpec((None, 4, W, W), index),
        ),
        out_shape=pltpu.HBM((4, 4, W, 2 * W), BF),
        input_output_aliases=alias,
        compiler_params=PARAMS,
        cost_estimate=cost(flops, 10 << 20),
        name="product",
    )(pos, *operands)


def total_kernel(ref, out_ref):
    acc = ref[0].astype(F32)
    for k in range(1, NG):
        acc += ref[k].astype(F32)
    out_ref[...] = acc


def total(value):
    tile = 64
    return pl.pallas_call(
        total_kernel,
        grid=(W // tile,),
        in_specs=[pl.BlockSpec((NG, tile, 2 * W), lambda i: (0, i, 0))],
        out_specs=pl.BlockSpec((tile, 2 * W), lambda i: (i, 0)),
        out_shape=jax.ShapeDtypeStruct((W, 2 * W), F32),
        compiler_params=PARAMS,
        cost_estimate=cost(2 << 20, 5 << 20),
        name="total",
    )(value)


def exchange(value, axes):
    return lax.all_to_all(value, axes, split_axis=0, concat_axis=0, tiled=True)


def run(per, pos, cells, screen_mask, counts, green_occ, occ_mask, green_virt):
    rows = (8 if per == 2 else 16, 16 if per == 4 else 8)
    first = pack(per, 0, rows[0], pos, screen_mask, counts, green_virt, green_occ, cells)
    second = pack(per, 1, rows[1], pos, screen_mask, counts, green_virt, green_occ, cells)
    first = exchange(first, AXES)
    second, first = lax.optimization_barrier((second, first))
    second = exchange(second, AXES).reshape(128 * rows[1], WIDE)
    outs = band(per, occ_mask, first.reshape(128 * LINES, first.shape[-1]))
    second, outs = lax.optimization_barrier((second, outs))
    virts = outs[:2]
    own = [second] + list(outs[2:])
    other = [lax.ppermute(v, "core", [(0, 1), (1, 0)]) for v in own]
    part = product(pos, virts, own)
    part = product(pos, virts, other, part)
    return total(exchange(part.reshape(NG, W, 2 * W), GROUP))


def local(three_centre, screen_mask, block_counts, green_occ, occ_mask, green_virt):
    row = lax.axis_index(ROWS)
    col = lax.axis_index(COLS)
    pos = jnp.stack([row, col, lax.axis_index("core")]).astype(jnp.int32)
    return run(
        4, pos, in_hbm(three_centre), screen_mask, block_counts, green_occ, occ_mask, in_hbm(green_virt)
    )


def solution(mesh):
    fine = Mesh(mesh.devices.reshape(SIZES), AXES)
    in_specs = (P(ROWS + COLS, None, None), P(), P(), P(ROWS, None), P(), P())
    return jax.shard_map(
        local, mesh=fine, in_specs=in_specs, out_specs=P(COLS, ROWS), check_vma=False
    )
```

```python
import functools
import math

import jax
import jax.numpy as jnp
from jax import lax
from jax.experimental import pallas as pl
from jax.experimental.pallas import tpu as pltpu
from jax.sharding import Mesh, PartitionSpec as P

AXES = ("zhi", "zlo", "ylo", "yhi", "x", "core")
SIZES = (2, 2, 2, 2, 4, 2)
ROWS = ("zhi", "zlo", "ylo")
COLS = ("yhi", "x", "core")
GROUP = ("zlo", "ylo", "x")
BS = 64
NU = 64
NB = 8
NG = 16
MUD = 4
SRC = 16
PSL = 4096
W = 256
LINES = 8
TAIL = 128
WIDE = 4 * W
BF = jnp.bfloat16
F32 = jnp.float32
SCALE = -1.0 / math.sqrt(NB * BS * NU)
PARAMS = pltpu.CompilerParams(vmem_limit_bytes=48 * 1024 * 1024)


def iota(shape, axis):
    return lax.broadcasted_iota(jnp.int32, shape, axis)


def cost(flops, size):
    return pl.CostEstimate(flops=flops, bytes_accessed=size, transcendentals=0)


def in_hbm(value):
    return pltpu.with_memory_space_constraint(value, pltpu.HBM)


def pack_kernel(per, part, rows, pos_ref, screen_ref, counts_ref, gv_ref, *refs):
    green_ref, out_ref, lhs = refs[-3:]
    step = pl.program_id(0)
    row = pos_ref[0]
    col = pos_ref[1]
    full = NG * rows

    @pl.when(step == 0)
    def _():
        def place(shape):
            line = iota(shape, 0)
            group, r = line // rows, line % rows
            if part == 0:
                plain = r >= MUD * per
                mu = jnp.where(plain, r - MUD * per, r // per)
                j = jnp.where(plain, per - 1, r % per)
            else:
                width = rows // MUD
                plain = r >= 0
                mu = r // width
                j = r % width
            return plain, mu, group * per + j

        plain, _, m = place((full, NU))
        pick = (m == iota((full, NU), 1)).astype(F32)
        if part == 0:
            gv_t = gv_ref[...].astype(F32).T
            small = jnp.dot(pick, gv_t, preferred_element_type=F32)
            small = jnp.where(plain, pick, small)
        else:
            small = pick
        big = jnp.concatenate([small] * MUD, axis=1)
        _, mu, _ = place((full, MUD * NU))
        lane = iota((full, MUD * NU), 1)
        live = (
            (mu == lane // NU)
            & (lane % NU < counts_ref[NB])
            & (mu + MUD * col < counts_ref[row])
        )
        lhs[...] = jnp.where(live, big, 0.0).astype(BF)

    half, core = step // 2, step % 2
    sub = iota((1, W), 1) // BS

    def store(g, lanes, pieces):
        zlo, ylo, xx = g // 8, (g // 4) % 2, g % 4
        for copy in range(2):
            if part == 0:
                out_ref[copy, zlo, ylo, xx, :, lanes] = pieces[copy]
            else:
                out_ref[zlo, ylo, copy, xx, :, lanes] = pieces[copy]

    def column(ref, which, t):
        mask = jnp.zeros((1, W), F32)
        for k in range(W // BS):
            on = screen_ref[row, (which * 8 + 2 * t + core) * (W // BS) + k] > 0
            mask = jnp.where(sub == k, on.astype(F32), mask)
        cells = ref[...].reshape(MUD * NU, W)
        return jnp.dot(lhs[...], cells, preferred_element_type=F32) * mask

    for t in range(4):
        out = column(refs[t], half, t)
        if part == 0 and per == 3:
            swap = column(refs[4 + t], 1 - half, t)
        for g in range(NG):
            piece = out[g * rows : (g + 1) * rows]
            if part == 1:
                store(g, slice(t * W, (t + 1) * W), [piece.astype(BF)] * 2)
                continue
            for h in range(rows // LINES):
                at = h * WIDE + t * W
                part_h = piece[h * LINES : (h + 1) * LINES]
                pieces = [part_h, part_h]
                if per == 3 and h == 1:
                    other = swap[g * rows + LINES : (g + 1) * rows]
                    plain = iota((LINES, W), 0) >= MUD
                    pieces = [
                        jnp.where(plain & (half != copy), other, part_h) for copy in range(2)
                    ]
                store(g, slice(at, at + W), [p.astype(BF) for p in pieces])
    if part == 0:
        green = green_ref[...]
        line, mu = iota((LINES, BS), 0), iota((LINES, BS), 1)
        left = (mu == MUD * col + line).astype(BF)
        right = (mu == MUD * col + line - MUD).astype(BF)
        left = jnp.where(line < MUD, left, jnp.zeros_like(left))
        right = jnp.where(line < MUD, jnp.zeros_like(right), right)
        tail = jnp.dot(left, green[:, :TAIL], preferred_element_type=F32)
        low = jnp.dot(right, green[:, TAIL:], preferred_element_type=F32)
        tail = (tail + jnp.concatenate([low, jnp.zeros_like(low)], axis=1)).astype(BF)
        at = rows // LINES * WIDE
        for g in range(NG):
            store(g, slice(at, at + TAIL), [tail, tail])


def pack(per, part, rows, pos, screen_mask, counts, green_virt, green_occ, cells):
    if part == 0:
        shape = (LINES, rows // LINES * WIDE + TAIL)
        block = (2, 2, 2, None, 4, None) + shape
        index = lambda s, *_: (0, 0, 0, s // 2, 0, s % 2, 0, 0)
    else:
        shape = (rows, WIDE)
        block = (None, 2, 2, 2, 4, None) + shape
        index = lambda s, *_: (s // 2, 0, 0, 0, 0, s % 2, 0, 0)

    def column(t, flip):
        def place(s, *_):
            half = 1 - s // 2 if flip else s // 2
            return 0, 0, half * 8 + 2 * t + s % 2

        return pl.BlockSpec((MUD, NU, W), place)

    operands = [green_virt] + [cells] * 4
    in_specs = [pl.BlockSpec((NU, NU), lambda s, *_: (0, 0))] + [column(t, False) for t in range(4)]
    if part == 0 and per == 3:
        operands += [cells] * 4
        in_specs += [column(t, True) for t in range(4)]
    operands.append(green_occ)
    in_specs.append(pl.BlockSpec((BS, 3 * BS), lambda s, *_: (0, 0)))
    out = pl.pallas_call(
        functools.partial(pack_kernel, per, part, rows),
        grid_spec=pltpu.PrefetchScalarGridSpec(
            num_scalar_prefetch=3,
            grid=(4,),
            in_specs=in_specs,
            out_specs=pl.BlockSpec(block, index),
            scratch_shapes=[pltpu.VMEM((NG * rows, MUD * NU), BF)],
        ),
        out_shape=pltpu.HBM(SIZES + shape, BF),
        compiler_params=PARAMS,
        cost_estimate=cost(2 * NG * rows * 256 * PSL, 6 << 20),
        name=f"pack_{part}",
    )(pos, screen_mask, counts, *operands)
    return out.reshape((128,) + shape)


def band_kernel(per, mask_ref, c0, c1, c2, c3, *out_refs):
    step = pl.program_id(0)
    refs = (c0, c1, c2, c3)
    lines = SRC * LINES
    halves = c0.shape[1] // WIDE
    depth = lines * halves
    width = 2 if per == 3 else per
    main = BS * width
    count = BS * per

    def place_row(shape):
        line = iota(shape, 0)
        extra = line >= main
        return jnp.where(extra, line - main, line // width), jnp.where(extra, width, line % width)

    def place_col(shape):
        line = iota(shape, 1)
        half, line = line // lines, line % lines
        source, r = line // LINES, line % LINES + half * LINES
        return r < MUD * per, source * MUD + r // per, r % per

    row_mu, _ = place_row((count, BS))
    spread_rows = (row_mu == iota((count, BS), 1)).astype(BF)
    good, col_mu, _ = place_col((BS, depth))
    spread_cols = (good & (col_mu == iota((BS, depth), 0))).astype(BF)
    _, row_j = place_row((count, depth))
    _, _, col_j = place_col((count, depth))
    same = row_j == col_j
    line, at = iota((BS, lines), 0), iota((BS, lines), 1)
    spot = (line // MUD) * LINES + line % MUD
    take_left = (spot == at).astype(BF)
    take_right = (spot + MUD == at).astype(BF)
    blocks = [
        jnp.concatenate([ref[:, h * WIDE : (h + 1) * WIDE] for h in range(halves)], axis=0)
        for ref in refs
    ]
    mains, extras = [], []
    for u in range(2):
        total = jnp.zeros((count, WIDE), F32)
        packed = refs[u + 1][:, halves * WIDE :]
        left = jnp.dot(take_left, packed, preferred_element_type=F32).astype(BF)
        right = jnp.dot(take_right, packed, preferred_element_type=F32).astype(BF)
        left = jnp.dot(spread_rows, left, preferred_element_type=F32).astype(BF)
        right = jnp.dot(spread_rows, right, preferred_element_type=F32).astype(BF)
        for k, part in enumerate((left[:, :BS], left[:, BS:], right[:, :BS])):
            part = jnp.dot(part, spread_cols, preferred_element_type=F32)
            part = jnp.where(same, part * mask_ref[2 * step + u, k].astype(F32), 0.0).astype(BF)
            total += jnp.dot(part, blocks[u + k], preferred_element_type=F32)
        mains.append(total[:main])
        extras.append(total[main:])
        if per == 3:
            line, at = iota((BS, lines), 0), iota((BS, lines), 1)
            take = ((line // MUD) * LINES + MUD + line % MUD == at).astype(BF)
            out_refs[2][u * BS : (u + 1) * BS, :] = jnp.dot(
                take, blocks[u + 1][lines:], preferred_element_type=F32
            ).astype(BF)
    out_refs[0][...] = jnp.concatenate(mains, axis=0).astype(BF).T
    if per == 3:
        out_refs[1][...] = jnp.concatenate(extras, axis=0).astype(BF).T


def band(per, occ_mask, cells):
    lines, full = SRC * LINES, cells.shape[1]
    width = 2 if per == 3 else per
    blk = lambda off: pl.BlockSpec((lines, full), lambda s, *_: ((2 * s + off) % NB, 0))
    out_specs = [pl.BlockSpec((WIDE, 2 * BS * width), lambda s, *_: (0, s))]
    out_shape = [pltpu.HBM((WIDE, NB * BS * width), BF)]
    if per == 3:
        out_specs.append(pl.BlockSpec((WIDE, 2 * BS), lambda s, *_: (0, s)))
        out_shape.append(pltpu.HBM((WIDE, NB * BS), BF))
        out_specs.append(pl.BlockSpec((2 * BS, WIDE), lambda s, *_: (s, 0)))
        out_shape.append(pltpu.HBM((NB * BS, WIDE), BF))
    return pl.pallas_call(
        functools.partial(band_kernel, per),
        grid_spec=pltpu.PrefetchScalarGridSpec(
            num_scalar_prefetch=1,
            grid=(NB // 2,),
            in_specs=[blk(off) for off in (NB - 1, 0, 1, 2)],
            out_specs=out_specs,
        ),
        out_shape=out_shape,
        compiler_params=PARAMS,
        cost_estimate=cost(2 * NB * BS * per * 3 * full // WIDE * lines * WIDE, 12 << 20),
        name="band",
    )(occ_mask, cells, cells, cells, cells)


def product_kernel(pairs, pos_ref, *refs):
    out = jnp.dot(refs[0][...], refs[1][...], preferred_element_type=F32)
    for i in range(1, pairs):
        out += jnp.dot(refs[2 * i][...], refs[2 * i + 1][...], preferred_element_type=F32)
    out = (out * SCALE).astype(BF)
    for x in range(4):
        refs[-1][x] = out[x * W : (x + 1) * W]


def product(pos, virts, cells, before=None):
    operands, in_specs, flops = [], [], 0
    for virt, cell in zip(virts, cells):
        depth = cell.shape[0]
        operands += [virt, cell]
        in_specs += [
            pl.BlockSpec((WIDE, depth), lambda i, *_: (0, 0)),
            pl.BlockSpec((depth, W), lambda i, *_: (0, i)),
        ]
        flops += 2 * depth * WIDE * WIDE
    if before is None:
        index = lambda i, pos_ref: (i, 0, 0, pos_ref[2])
        alias = {}
    else:
        operands.append(before)
        in_specs.append(pl.BlockSpec(memory_space=pl.ANY))
        index = lambda i, pos_ref: (i, 0, 0, 1 - pos_ref[2])
        alias = {len(operands): 0}
    return pl.pallas_call(
        functools.partial(product_kernel, len(virts)),
        grid_spec=pltpu.PrefetchScalarGridSpec(
            num_scalar_prefetch=1,
            grid=(4,),
            in_specs=in_specs,
            out_specs=pl.BlockSpec((None, 4, W, W), index),
        ),
        out_shape=pltpu.HBM((4, 4, W, 2 * W), BF),
        input_output_aliases=alias,
        compiler_params=PARAMS,
        cost_estimate=cost(flops, 10 << 20),
        name="product",
    )(pos, *operands)


def total_kernel(ref, out_ref):
    acc = ref[0].astype(F32)
    for k in range(1, NG):
        acc += ref[k].astype(F32)
    out_ref[...] = acc


def total(value):
    tile = 64
    return pl.pallas_call(
        total_kernel,
        grid=(W // tile,),
        in_specs=[pl.BlockSpec((NG, tile, 2 * W), lambda i: (0, i, 0))],
        out_specs=pl.BlockSpec((tile, 2 * W), lambda i: (i, 0)),
        out_shape=jax.ShapeDtypeStruct((W, 2 * W), F32),
        compiler_params=PARAMS,
        cost_estimate=cost(2 << 20, 5 << 20),
        name="total",
    )(value)


def exchange(value, axes):
    return lax.all_to_all(value, axes, split_axis=0, concat_axis=0, tiled=True)


def run(per, pos, cells, screen_mask, counts, green_occ, occ_mask, green_virt):
    rows = (8 if per == 2 else 16, 16 if per == 4 else 8)
    cells, green_virt = in_hbm(cells), in_hbm(green_virt)
    first = pack(per, 0, rows[0], pos, screen_mask, counts, green_virt, green_occ, cells)
    second = pack(per, 1, rows[1], pos, screen_mask, counts, green_virt, green_occ, cells)
    first = exchange(first, AXES)
    second, first = lax.optimization_barrier((second, first))
    second = exchange(second, AXES).reshape(128 * rows[1], WIDE)
    outs = band(per, occ_mask, first.reshape(128 * LINES, first.shape[-1]))
    second, outs = lax.optimization_barrier((second, outs))
    virts = [in_hbm(v) for v in outs[:2]]
    own = [second] + list(outs[2:])
    other = [in_hbm(lax.ppermute(v, "core", [(0, 1), (1, 0)])) for v in own]
    part = product(pos, virts, own)
    part = product(pos, virts, other, part)
    return total(exchange(part.reshape(NG, W, 2 * W), GROUP))


def local(three_centre, screen_mask, block_counts, green_occ, occ_mask, green_virt):
    row = lax.axis_index(ROWS)
    col = lax.axis_index(COLS)
    pos = jnp.stack([row, col, lax.axis_index("core")]).astype(jnp.int32)
    live = block_counts[NB]
    branch = (live > 2 * NG).astype(jnp.int32) + (live > 3 * NG).astype(jnp.int32)
    return lax.switch(
        branch,
        [functools.partial(run, per) for per in (2, 3, 4)],
        pos,
        three_centre,
        screen_mask,
        block_counts,
        green_occ,
        occ_mask,
        green_virt,
    )


def solution(mesh):
    fine = Mesh(mesh.devices.reshape(SIZES), AXES)
    in_specs = (P(ROWS + COLS, None, None), P(), P(), P(ROWS, None), P(), P())
    return jax.shard_map(
        local, mesh=fine, in_specs=in_specs, out_specs=P(COLS, ROWS), check_vma=False
    )
```

```python
import functools
import math

import jax
import jax.numpy as jnp
from jax import lax
from jax.experimental import pallas as pl
from jax.experimental.pallas import tpu as pltpu
from jax.sharding import Mesh, PartitionSpec as P

AXES = ("zhi", "zlo", "ylo", "yhi", "x", "core")
SIZES = (2, 2, 2, 2, 4, 2)
ROWS = ("zhi", "zlo", "ylo")
COLS = ("yhi", "x", "core")
GROUP = ("zlo", "ylo", "x")
BS = 64
NU = 64
NB = 8
NG = 16
MUD = 4
SRC = 16
PSL = 4096
W = 256
LINES = 8
TAIL = 128
WIDE = 4 * W
BF = jnp.bfloat16
F32 = jnp.float32
SCALE = -1.0 / math.sqrt(NB * BS * NU)
PARAMS = pltpu.CompilerParams(vmem_limit_bytes=48 * 1024 * 1024)


def iota(shape, axis):
    return lax.broadcasted_iota(jnp.int32, shape, axis)


def cost(flops, size):
    return pl.CostEstimate(flops=flops, bytes_accessed=size, transcendentals=0)


def in_hbm(value):
    return pltpu.with_memory_space_constraint(value, pltpu.HBM)


def halves_of(per):
    return 1 if per == 2 else 2


def rest_of(per, width):
    return {2: 0, 3: width // 2, 4: width}[per]


def row_of(per, half, line):
    return line + LINES * half if per != 3 else jnp.where(half > 0, LINES + line % MUD, line)


def pack_kernel(per, part, pos_ref, screen_ref, counts_ref, gv_ref, *refs):
    out_ref, lhs = refs[-2:]
    step = pl.program_id(0)
    row = pos_ref[0]
    col = pos_ref[1]
    halves = halves_of(per)
    rows = LINES * halves
    full = NG * rows

    @pl.when(step == 0)
    def _():
        def place(shape):
            line = iota(shape, 0)
            group, half, line = line // rows, (line % rows) // LINES, line % LINES
            r = row_of(per, half, line)
            return r // per, group * per + r % per

        _, m = place((full, NU))
        pick = (m == iota((full, NU), 1)).astype(F32)
        smalls = [pick]
        if part == 0:
            gv_t = gv_ref[...].astype(F32).T
            smalls.append(jnp.dot(pick, gv_t, preferred_element_type=F32))
        mu, _ = place((full, MUD * NU))
        lane = iota((full, MUD * NU), 1)
        live = (
            (mu == lane // NU)
            & (lane % NU < counts_ref[NB])
            & (mu + MUD * col < counts_ref[row])
        )
        for i, small in enumerate(smalls):
            big = jnp.concatenate([small] * MUD, axis=1)
            lhs[i] = jnp.where(live, big, 0.0).astype(BF)

    half, core = step // 2, step % 2
    sub = iota((1, W), 1) // BS
    low = iota((LINES, W), 0) < MUD

    def column(kind, ref, which, t):
        mask = jnp.zeros((1, W), F32)
        for k in range(W // BS):
            on = screen_ref[row, (which * 8 + 2 * t + core) * (W // BS) + k] > 0
            mask = jnp.where(sub == k, on.astype(F32), mask)
        cells = ref[...].reshape(MUD * NU, W)
        return jnp.dot(lhs[kind], cells, preferred_element_type=F32) * mask

    def pieces(outs, at):
        wide = len(outs) * W
        for g in range(NG):
            for t, out in enumerate(outs):
                yield g, at + t * W, out[g * rows : g * rows + LINES].astype(BF)
            if per == 2:
                continue
            rest = [out[g * rows + LINES : (g + 1) * rows] for out in outs]
            if per == 3:
                count = len(outs) // 2
                rest = [jnp.where(low, rest[t], rest[t + count]) for t in range(count)]
            for t, piece in enumerate(rest):
                yield g, at + wide + t * W, piece.astype(BF)

    def spot(g):
        return g // 8, (g // 4) % 2, g % 4

    if part == 1:
        outs = [column(0, refs[i], half, 2 + i) for i in range(2)]
        for g, at, piece in pieces(outs, 0):
            zlo, ylo, xx = spot(g)
            for copy in range(2):
                out_ref[zlo, ylo, copy, xx, :, at : at + W] = piece
        return

    outs = [column(1, refs[t], half, t) for t in range(4)]
    for g, at, piece in pieces(outs, 0):
        for copy in range(2):
            out_ref[(copy,) + spot(g) + (slice(None), slice(at, at + W))] = piece
    base = WIDE + rest_of(per, WIDE)
    for copy in range(2):
        outs = [column(0, refs[4 + 2 * copy + t], copy, t) for t in range(2)]
        for g, at, piece in pieces(outs, base):
            out_ref[(copy,) + spot(g) + (slice(None), slice(at, at + W))] = piece
    base += 2 * W + rest_of(per, 2 * W)
    green = refs[8][...]
    line, mu = iota((LINES, BS), 0), iota((LINES, BS), 1)
    left = ((mu == MUD * col + line) & (line < MUD)).astype(BF)
    right = ((mu == MUD * col + line - MUD) & (line >= MUD)).astype(BF)
    tail = jnp.dot(left, green[:, :TAIL], preferred_element_type=F32)
    lower = jnp.dot(right, green[:, TAIL:], preferred_element_type=F32)
    tail = (tail + jnp.concatenate([lower, jnp.zeros_like(lower)], axis=1)).astype(BF)
    for g in range(NG):
        for copy in range(2):
            out_ref[(copy,) + spot(g) + (slice(None), slice(base, base + TAIL))] = tail


def pack(per, part, pos, screen_mask, counts, green_virt, green_occ, cells):
    screened = 2 * W + rest_of(per, 2 * W)

    def column(place):
        return pl.BlockSpec((MUD, NU, W), lambda s, *_: (0, 0, place(s // 2) + s % 2))

    in_specs = [pl.BlockSpec((NU, NU), lambda s, *_: (0, 0))]
    if part == 0:
        shape = (LINES, WIDE + rest_of(per, WIDE) + screened + TAIL)
        block = (2, 2, 2, None, 4, None) + shape
        index = lambda s, *_: (0, 0, 0, s // 2, 0, s % 2, 0, 0)
        in_specs += [column(lambda half, t=t: half * 8 + 2 * t) for t in range(4)]
        in_specs += [column(lambda half, c=c, t=t: c * 8 + 2 * t) for c in range(2) for t in range(2)]
        in_specs.append(pl.BlockSpec((BS, 3 * BS), lambda s, *_: (0, 0)))
        operands = [green_virt] + [cells] * 8 + [green_occ]
    else:
        shape = (LINES, screened)
        block = (None, 2, 2, 2, 4, None) + shape
        index = lambda s, *_: (s // 2, 0, 0, 0, 0, s % 2, 0, 0)
        in_specs += [column(lambda half, t=t: half * 8 + 2 * t) for t in (2, 3)]
        operands = [green_virt] + [cells] * 2
    rows = NG * LINES * halves_of(per)
    out = pl.pallas_call(
        functools.partial(pack_kernel, per, part),
        grid_spec=pltpu.PrefetchScalarGridSpec(
            num_scalar_prefetch=3,
            grid=(4,),
            in_specs=in_specs,
            out_specs=pl.BlockSpec(block, index),
            scratch_shapes=[pltpu.VMEM((2 - part, rows, MUD * NU), BF)],
        ),
        out_shape=pltpu.HBM(SIZES + shape, BF),
        compiler_params=PARAMS,
        cost_estimate=cost(2 * rows * 256 * PSL, 6 << 20),
        name=f"pack_{part}",
    )(pos, screen_mask, counts, *operands)
    return out.reshape((128,) + shape)


def band_kernel(per, mask_ref, c0, c1, c2, c3, out_ref):
    step = pl.program_id(0)
    refs = (c0, c1, c2, c3)
    lines = SRC * LINES
    halves = halves_of(per)
    count = lines * halves

    def place(shape, axis):
        at = iota(shape, axis)
        half, at = at // lines, at % lines
        line = at % LINES
        r = row_of(per, half, line)
        return half, line, (at // LINES) * MUD + r // per, r % per

    _, _, mu, _ = place((count, BS), 0)
    spread_rows = (mu == iota((count, BS), 1)).astype(BF)
    _, _, mu, _ = place((BS, count), 1)
    spread_cols = (mu == iota((BS, count), 0)).astype(BF)
    _, _, _, row_j = place((count, count), 0)
    col_half, col_line, _, col_j = place((count, count), 1)
    same = row_j == col_j
    cuts = 2 if per == 3 else 1
    wide = WIDE // cuts
    keeps = [same]
    if per == 3:
        keeps = [same & ((col_half == 0) | (col_line // MUD == cut)) for cut in range(cuts)]
    blocks = []
    for ref in refs:
        cells = []
        for cut in range(cuts):
            parts = [ref[:, cut * wide : (cut + 1) * wide]]
            if halves == 2:
                parts.append(ref[:, WIDE : WIDE + wide])
            cells.append(jnp.concatenate(parts, axis=0))
        blocks.append(cells)
    line, at = iota((BS, lines), 0), iota((BS, lines), 1)
    spot = (line // MUD) * LINES + line % MUD
    take_left = (spot == at).astype(BF)
    take_right = (spot + MUD == at).astype(BF)
    for u in range(2):
        packed = refs[u + 1][:, refs[u + 1].shape[1] - TAIL :]
        left = jnp.dot(take_left, packed, preferred_element_type=F32).astype(BF)
        right = jnp.dot(take_right, packed, preferred_element_type=F32).astype(BF)
        left = jnp.dot(spread_rows, left, preferred_element_type=F32).astype(BF)
        right = jnp.dot(spread_rows, right, preferred_element_type=F32).astype(BF)
        totals = [jnp.zeros((count, wide), F32) for _ in range(cuts)]
        for k, part in enumerate((left[:, :BS], left[:, BS:], right[:, :BS])):
            part = jnp.dot(part, spread_cols, preferred_element_type=F32)
            part = part * mask_ref[2 * step + u, k].astype(F32)
            for cut in range(cuts):
                used = jnp.where(keeps[cut], part, 0.0).astype(BF)
                totals[cut] += jnp.dot(used, blocks[u + k][cut], preferred_element_type=F32)
        for cut in range(cuts):
            virt = totals[cut].astype(BF)
            for h in range(halves):
                out_ref[h, cut * wide : (cut + 1) * wide, u * lines : (u + 1) * lines] = virt[
                    h * lines : (h + 1) * lines
                ].T


def band(per, occ_mask, cells):
    lines, full = SRC * LINES, cells.shape[1]
    halves = halves_of(per)
    blk = lambda off: pl.BlockSpec((lines, full), lambda s, *_: ((2 * s + off) % NB, 0))
    return pl.pallas_call(
        functools.partial(band_kernel, per),
        grid_spec=pltpu.PrefetchScalarGridSpec(
            num_scalar_prefetch=1,
            grid=(NB // 2,),
            in_specs=[blk(off) for off in (NB - 1, 0, 1, 2)],
            out_specs=pl.BlockSpec((halves, WIDE, 2 * lines), lambda s, *_: (0, 0, s)),
        ),
        out_shape=pltpu.HBM((halves, WIDE, NB * lines), BF),
        compiler_params=PARAMS,
        cost_estimate=cost(2 * NB * 3 * (lines * halves) ** 2 * WIDE, 12 << 20),
        name="band",
    )(occ_mask, cells, cells, cells, cells)


def product_kernel(per, pos_ref, v_ref, *refs):
    out_ref, acc = refs[-2:]
    step = pl.program_id(0)
    last = halves_of(per) - 1

    def finish(value):
        value = (value * SCALE).astype(BF)
        for t in range(2):
            for x in range(4):
                out_ref[t, x] = value[x * W : (x + 1) * W, t * W : (t + 1) * W]

    @pl.when(step == 0)
    def _():
        value = jnp.dot(v_ref[...], refs[0][...], preferred_element_type=F32)
        if last == 0:
            finish(value)
        else:
            acc[...] = value

    if last == 1:

        @pl.when(step == 1)
        def _():
            cells = refs[1][...]
            if per == 3:
                low = iota(cells.shape, 0) % LINES < MUD
                none = jnp.zeros_like(cells)
                cells = jnp.concatenate(
                    [jnp.where(low, cells, none), jnp.where(low, none, cells)], axis=1
                )
            finish(acc[...] + jnp.dot(v_ref[...], cells, preferred_element_type=F32))


def product(per, group, mine, pos, virt, cells, at, before):
    wide = 2 * W
    halves = halves_of(per)
    rest = rest_of(per, wide)
    depth = virt.shape[2]
    operands = [virt, cells]
    in_specs = [
        pl.BlockSpec((None, WIDE, depth), lambda h, *_: (h, 0, 0)),
        pl.BlockSpec((depth, wide), lambda h, *_: (0, at // wide)),
    ]
    if rest:
        operands.append(cells)
        in_specs.append(pl.BlockSpec((depth, rest), lambda h, *_: (0, (at + wide) // rest)))
    alias = {}
    if before is not None:
        operands.append(before)
        in_specs.append(pl.BlockSpec(memory_space=pl.ANY))
        alias = {len(operands): 0}

    def index(h, pos_ref):
        return group, 0, 0, 0, pos_ref[2] if mine else 1 - pos_ref[2]

    return pl.pallas_call(
        functools.partial(product_kernel, per),
        grid_spec=pltpu.PrefetchScalarGridSpec(
            num_scalar_prefetch=1,
            grid=(halves,),
            in_specs=in_specs,
            out_specs=pl.BlockSpec((None, 2, 4, W, W), index),
            scratch_shapes=[pltpu.VMEM((WIDE, wide), F32)],
        ),
        out_shape=pltpu.HBM((2, 2, 4, W, 2 * W), BF),
        input_output_aliases=alias,
        compiler_params=PARAMS,
        cost_estimate=cost(2 * halves * depth * WIDE * wide, 7 << 20),
        name="product",
    )(pos, *operands)


def total_kernel(ref, out_ref):
    acc = ref[0].astype(F32)
    for k in range(1, NG):
        acc += ref[k].astype(F32)
    out_ref[...] = acc


def total(value):
    tile = 64
    return pl.pallas_call(
        total_kernel,
        grid=(W // tile,),
        in_specs=[pl.BlockSpec((NG, tile, 2 * W), lambda i: (0, i, 0))],
        out_specs=pl.BlockSpec((tile, 2 * W), lambda i: (i, 0)),
        out_shape=pltpu.HBM((W, 2 * W), F32),
        compiler_params=PARAMS,
        cost_estimate=cost(2 << 20, 5 << 20),
        name="total",
    )(value)


def exchange(value, axes):
    return lax.all_to_all(value, axes, split_axis=0, concat_axis=0, tiled=True)


def swapped(value):
    return in_hbm(lax.ppermute(value, "core", [(0, 1), (1, 0)]))


def run(per, pos, cells, screen_mask, counts, green_occ, occ_mask, green_virt):
    cells, green_virt = in_hbm(cells), in_hbm(green_virt)
    first = pack(per, 0, pos, screen_mask, counts, green_virt, green_occ, cells)
    second = pack(per, 1, pos, screen_mask, counts, green_virt, green_occ, cells)
    first = exchange(first, AXES)
    second, first = lax.optimization_barrier((second, first))
    second = exchange(second, AXES)
    second = second.reshape(128 * LINES, second.shape[-1])
    first = first.reshape(128 * LINES, first.shape[-1])
    at = WIDE + rest_of(per, WIDE)
    size = 2 * W + rest_of(per, 2 * W)
    virt = band(per, occ_mask, first)
    part = product(per, 0, True, pos, virt, first, at, None)
    part = product(per, 0, False, pos, virt, swapped(first[:, at : at + size]), 0, part)
    second, part = lax.optimization_barrier((second, part))
    part = product(per, 1, True, pos, virt, second, 0, part)
    part = product(per, 1, False, pos, virt, swapped(second), 0, part)
    return total(exchange(part.reshape(NG, W, 2 * W), GROUP))


def local(three_centre, screen_mask, block_counts, green_occ, occ_mask, green_virt):
    row = lax.axis_index(ROWS)
    col = lax.axis_index(COLS)
    pos = jnp.stack([row, col, lax.axis_index("core")]).astype(jnp.int32)
    live = block_counts[NB]
    branch = (live > 2 * NG).astype(jnp.int32) + (live > 3 * NG).astype(jnp.int32)
    return lax.switch(
        branch,
        [functools.partial(run, per) for per in (2, 3, 4)],
        pos,
        three_centre,
        screen_mask,
        block_counts,
        green_occ,
        occ_mask,
        green_virt,
    )


def solution(mesh):
    fine = Mesh(mesh.devices.reshape(SIZES), AXES)
    in_specs = (P(ROWS + COLS, None, None), P(), P(), P(ROWS, None), P(), P())
    return jax.shard_map(
        local, mesh=fine, in_specs=in_specs, out_specs=P(COLS, ROWS), check_vma=False
    )
```

```python
import functools
import math

import jax
import jax.numpy as jnp
from jax import lax
from jax.experimental import pallas as pl
from jax.experimental.pallas import tpu as pltpu
from jax.sharding import Mesh, PartitionSpec as P

AXES = ("zhi", "zlo", "ylo", "yhi", "x", "core")
SIZES = (2, 2, 2, 2, 4, 2)
ROWS = ("zhi", "zlo", "ylo")
COLS = ("yhi", "x", "core")
GROUP = ("zlo", "ylo", "x")
BS = 64
NU = 64
NB = 8
NG = 16
MUD = 4
SRC = 16
PSL = 4096
W = 256
LINES = 8
TAIL = 128
WIDE = 4 * W
BF = jnp.bfloat16
F32 = jnp.float32
SCALE = -1.0 / math.sqrt(NB * BS * NU)
PARAMS = pltpu.CompilerParams(vmem_limit_bytes=48 * 1024 * 1024)
SMALL = pltpu.CompilerParams(vmem_limit_bytes=28 * 1024 * 1024)


def iota(shape, axis):
    return lax.broadcasted_iota(jnp.int32, shape, axis)


def cost(flops, size):
    return pl.CostEstimate(flops=flops, bytes_accessed=size, transcendentals=0)


def in_hbm(value):
    return pltpu.with_memory_space_constraint(value, pltpu.HBM)


def halves_of(per):
    return 1 if per == 2 else 2


def rest_of(per, width):
    return {2: 0, 3: width // 2, 4: width}[per]


def row_of(per, half, line):
    return line + LINES * half if per != 3 else jnp.where(half > 0, LINES + line % MUD, line)


def pack_kernel(per, part, pos_ref, screen_ref, counts_ref, gv_ref, *refs):
    out_ref, lhs = refs[-2:]
    step = pl.program_id(0)
    row = pos_ref[0]
    col = pos_ref[1]
    halves = halves_of(per)
    rows = LINES * halves
    full = NG * rows

    @pl.when(step == 0)
    def _():
        def place(shape):
            line = iota(shape, 0)
            group, half, line = line // rows, (line % rows) // LINES, line % LINES
            r = row_of(per, half, line)
            return r // per, group * per + r % per

        _, m = place((full, NU))
        pick = (m == iota((full, NU), 1)).astype(F32)
        smalls = [pick]
        if part == 0:
            gv_t = gv_ref[...].astype(F32).T
            smalls.append(jnp.dot(pick, gv_t, preferred_element_type=F32))
        mu, _ = place((full, MUD * NU))
        lane = iota((full, MUD * NU), 1)
        live = (
            (mu == lane // NU)
            & (lane % NU < counts_ref[NB])
            & (mu + MUD * col < counts_ref[row])
        )
        for i, small in enumerate(smalls):
            big = jnp.concatenate([small] * MUD, axis=1)
            lhs[i] = jnp.where(live, big, 0.0).astype(BF)

    half, core = step // 2, step % 2
    sub = iota((1, W), 1) // BS
    low = iota((LINES, W), 0) < MUD

    def column(kind, which, t):
        place = which * 8 + 2 * t + core
        mask = jnp.zeros((1, W), F32)
        for k in range(W // BS):
            on = screen_ref[row, place * (W // BS) + k] > 0
            mask = jnp.where(sub == k, on.astype(F32), mask)
        lanes = pl.ds(pl.multiple_of(place * W, W), W)
        cells = refs[0][:, :, lanes].reshape(MUD * NU, W)
        return jnp.dot(lhs[kind], cells, preferred_element_type=F32) * mask

    def pieces(outs, at):
        wide = len(outs) * W
        for g in range(NG):
            for t, out in enumerate(outs):
                yield g, at + t * W, out[g * rows : g * rows + LINES].astype(BF)
            if per == 2:
                continue
            rest = [out[g * rows + LINES : (g + 1) * rows] for out in outs]
            if per == 3:
                count = len(outs) // 2
                rest = [jnp.where(low, rest[t], rest[t + count]) for t in range(count)]
            for t, piece in enumerate(rest):
                yield g, at + wide + t * W, piece.astype(BF)

    def spot(g):
        return g // 8, (g // 4) % 2, g % 4

    if part == 1:
        outs = [column(0, half, 2 + i) for i in range(2)]
        for g, at, piece in pieces(outs, 0):
            zlo, ylo, xx = spot(g)
            for copy in range(2):
                out_ref[zlo, ylo, copy, xx, :, at : at + W] = piece
        return

    outs = [column(1, half, t) for t in range(4)]
    for g, at, piece in pieces(outs, 0):
        for copy in range(2):
            out_ref[(copy,) + spot(g) + (slice(None), slice(at, at + W))] = piece
    base = WIDE + rest_of(per, WIDE)
    for copy in range(2):
        outs = [column(0, copy, t) for t in range(2)]
        for g, at, piece in pieces(outs, base):
            out_ref[(copy,) + spot(g) + (slice(None), slice(at, at + W))] = piece
    base += 2 * W + rest_of(per, 2 * W)
    green = refs[1][...]
    line, mu = iota((LINES, BS), 0), iota((LINES, BS), 1)
    left = ((mu == MUD * col + line) & (line < MUD)).astype(BF)
    right = ((mu == MUD * col + line - MUD) & (line >= MUD)).astype(BF)
    tail = jnp.dot(left, green[:, :TAIL], preferred_element_type=F32)
    lower = jnp.dot(right, green[:, TAIL:], preferred_element_type=F32)
    tail = (tail + jnp.concatenate([lower, jnp.zeros_like(lower)], axis=1)).astype(BF)
    for g in range(NG):
        for copy in range(2):
            out_ref[(copy,) + spot(g) + (slice(None), slice(base, base + TAIL))] = tail


def pack(per, part, pos, screen_mask, counts, green_virt, green_occ, cells):
    screened = 2 * W + rest_of(per, 2 * W)

    in_specs = [
        pl.BlockSpec((NU, NU), lambda s, *_: (0, 0)),
        pl.BlockSpec((MUD, NU, PSL), lambda s, *_: (0, 0, 0)),
    ]
    operands = [green_virt, cells]
    if part == 0:
        shape = (LINES, WIDE + rest_of(per, WIDE) + screened + TAIL)
        block = (2, 2, 2, None, 4, None) + shape
        index = lambda s, *_: (0, 0, 0, s // 2, 0, s % 2, 0, 0)
        in_specs.append(pl.BlockSpec((BS, 3 * BS), lambda s, *_: (0, 0)))
        operands.append(green_occ)
    else:
        shape = (LINES, screened)
        block = (None, 2, 2, 2, 4, None) + shape
        index = lambda s, *_: (s // 2, 0, 0, 0, 0, s % 2, 0, 0)
    rows = NG * LINES * halves_of(per)
    out = pl.pallas_call(
        functools.partial(pack_kernel, per, part),
        grid_spec=pltpu.PrefetchScalarGridSpec(
            num_scalar_prefetch=3,
            grid=(4,),
            in_specs=in_specs,
            out_specs=pl.BlockSpec(block, index),
            scratch_shapes=[pltpu.VMEM((2 - part, rows, MUD * NU), BF)],
        ),
        out_shape=pltpu.HBM(SIZES + shape, BF),
        compiler_params=PARAMS,
        cost_estimate=cost(2 * rows * 256 * PSL, 6 << 20),
        name=f"pack_{part}",
    )(pos, screen_mask, counts, *operands)
    return out.reshape((128,) + shape)


def band_kernel(per, mask_ref, c0, c1, c2, c3, out_ref, copy_ref):
    step = pl.program_id(0)
    refs = (c0, c1, c2, c3)
    lines = SRC * LINES
    halves = halves_of(per)
    count = lines * halves

    def place(shape, axis):
        at = iota(shape, axis)
        half, at = at // lines, at % lines
        line = at % LINES
        r = row_of(per, half, line)
        return half, line, (at // LINES) * MUD + r // per, r % per

    _, _, mu, _ = place((count, BS), 0)
    spread_rows = (mu == iota((count, BS), 1)).astype(BF)
    _, _, mu, _ = place((BS, count), 1)
    spread_cols = (mu == iota((BS, count), 0)).astype(BF)
    _, _, _, row_j = place((count, count), 0)
    col_half, col_line, _, col_j = place((count, count), 1)
    same = row_j == col_j
    cuts = 2 if per == 3 else 1
    wide = WIDE // cuts
    keeps = [same]
    if per == 3:
        keeps = [same & ((col_half == 0) | (col_line // MUD == cut)) for cut in range(cuts)]
    blocks = []
    for ref in refs:
        cells = []
        for cut in range(cuts):
            parts = [ref[:, cut * wide : (cut + 1) * wide]]
            if halves == 2:
                parts.append(ref[:, WIDE : WIDE + wide])
            cells.append(jnp.concatenate(parts, axis=0))
        blocks.append(cells)
    line, at = iota((BS, lines), 0), iota((BS, lines), 1)
    spot = (line // MUD) * LINES + line % MUD
    take_left = (spot == at).astype(BF)
    take_right = (spot + MUD == at).astype(BF)
    end = c0.shape[1] - TAIL
    for u in range(2):
        copy_ref[u * lines : (u + 1) * lines] = refs[u + 1][:, end - copy_ref.shape[1] : end]
        packed = refs[u + 1][:, end:]
        left = jnp.dot(take_left, packed, preferred_element_type=F32).astype(BF)
        right = jnp.dot(take_right, packed, preferred_element_type=F32).astype(BF)
        left = jnp.dot(spread_rows, left, preferred_element_type=F32).astype(BF)
        right = jnp.dot(spread_rows, right, preferred_element_type=F32).astype(BF)
        totals = [jnp.zeros((count, wide), F32) for _ in range(cuts)]
        for k, part in enumerate((left[:, :BS], left[:, BS:], right[:, :BS])):
            part = jnp.dot(part, spread_cols, preferred_element_type=F32)
            part = part * mask_ref[2 * step + u, k].astype(F32)
            for cut in range(cuts):
                used = jnp.where(keeps[cut], part, 0.0).astype(BF)
                totals[cut] += jnp.dot(used, blocks[u + k][cut], preferred_element_type=F32)
        for cut in range(cuts):
            virt = totals[cut].astype(BF)
            for h in range(halves):
                out_ref[h, cut * wide : (cut + 1) * wide, u * lines : (u + 1) * lines] = virt[
                    h * lines : (h + 1) * lines
                ].T


def band(per, occ_mask, cells):
    lines, full = SRC * LINES, cells.shape[1]
    halves = halves_of(per)
    size = 2 * W + rest_of(per, 2 * W)
    blk = lambda off: pl.BlockSpec((lines, full), lambda s, *_: ((2 * s + off) % NB, 0))
    return pl.pallas_call(
        functools.partial(band_kernel, per),
        grid_spec=pltpu.PrefetchScalarGridSpec(
            num_scalar_prefetch=1,
            grid=(NB // 2,),
            in_specs=[blk(off) for off in (NB - 1, 0, 1, 2)],
            out_specs=[
                pl.BlockSpec((halves, WIDE, 2 * lines), lambda s, *_: (0, 0, s)),
                pl.BlockSpec((2 * lines, size), lambda s, *_: (s, 0)),
            ],
        ),
        out_shape=[
            pltpu.HBM((halves, WIDE, NB * lines), BF),
            pltpu.HBM((NB * lines, size), BF),
        ],
        compiler_params=PARAMS,
        cost_estimate=cost(2 * NB * 3 * (lines * halves) ** 2 * WIDE, 12 << 20),
        name="band",
    )(occ_mask, cells, cells, cells, cells)


def product_kernel(per, pos_ref, v_ref, *refs):
    out_ref, acc = refs[-2:]
    step = pl.program_id(0)
    last = halves_of(per) - 1

    def finish(value):
        value = (value * SCALE).astype(BF)
        for t in range(2):
            for x in range(4):
                out_ref[t, x] = value[x * W : (x + 1) * W, t * W : (t + 1) * W]

    @pl.when(step == 0)
    def _():
        value = jnp.dot(v_ref[...], refs[0][...], preferred_element_type=F32)
        if last == 0:
            finish(value)
        else:
            acc[...] = value

    if last == 1:

        @pl.when(step == 1)
        def _():
            cells = refs[1][...]
            if per == 3:
                low = iota(cells.shape, 0) % LINES < MUD
                none = jnp.zeros_like(cells)
                cells = jnp.concatenate(
                    [jnp.where(low, cells, none), jnp.where(low, none, cells)], axis=1
                )
            finish(acc[...] + jnp.dot(v_ref[...], cells, preferred_element_type=F32))


def product(per, group, mine, pos, virt, cells, at, before):
    wide = 2 * W
    halves = halves_of(per)
    rest = rest_of(per, wide)
    depth = virt.shape[2]
    operands = [virt, cells]
    in_specs = [
        pl.BlockSpec((None, WIDE, depth), lambda h, *_: (h, 0, 0)),
        pl.BlockSpec((depth, wide), lambda h, *_: (0, at // wide)),
    ]
    if rest:
        operands.append(cells)
        in_specs.append(pl.BlockSpec((depth, rest), lambda h, *_: (0, (at + wide) // rest)))
    alias = {}
    if before is not None:
        operands.append(before)
        in_specs.append(pl.BlockSpec(memory_space=pl.ANY))
        alias = {len(operands): 0}

    def index(h, pos_ref):
        return group, 0, 0, 0, pos_ref[2] if mine else 1 - pos_ref[2]

    return pl.pallas_call(
        functools.partial(product_kernel, per),
        grid_spec=pltpu.PrefetchScalarGridSpec(
            num_scalar_prefetch=1,
            grid=(halves,),
            in_specs=in_specs,
            out_specs=pl.BlockSpec((None, 2, 4, W, W), index),
            scratch_shapes=[pltpu.VMEM((WIDE, wide), F32)],
        ),
        out_shape=pltpu.HBM((2, 2, 4, W, 2 * W), BF),
        input_output_aliases=alias,
        compiler_params=SMALL,
        cost_estimate=cost(2 * halves * depth * WIDE * wide, 7 << 20),
        name="product",
    )(pos, *operands)


def total_kernel(ref, out_ref):
    acc = ref[0].astype(F32)
    for k in range(1, NG):
        acc += ref[k].astype(F32)
    out_ref[...] = acc


def total(value):
    tile = 64
    return pl.pallas_call(
        total_kernel,
        grid=(W // tile,),
        in_specs=[pl.BlockSpec((NG, tile, 2 * W), lambda i: (0, i, 0))],
        out_specs=pl.BlockSpec((tile, 2 * W), lambda i: (i, 0)),
        out_shape=pltpu.HBM((W, 2 * W), F32),
        compiler_params=PARAMS,
        cost_estimate=cost(2 << 20, 5 << 20),
        name="total",
    )(value)


def exchange(value, axes):
    return lax.all_to_all(value, axes, split_axis=0, concat_axis=0, tiled=True)


def swapped(value):
    return lax.ppermute(value, "core", [(0, 1), (1, 0)])


def run(per, pos, cells, screen_mask, counts, green_occ, occ_mask, green_virt):
    cells, green_virt = in_hbm(cells), in_hbm(green_virt)
    first = pack(per, 0, pos, screen_mask, counts, green_virt, green_occ, cells)
    second = pack(per, 1, pos, screen_mask, counts, green_virt, green_occ, cells)
    first = exchange(first, AXES)
    second, first = lax.optimization_barrier((second, first))
    second = exchange(second, AXES)
    second = second.reshape(128 * LINES, second.shape[-1])
    first = first.reshape(128 * LINES, first.shape[-1])
    at = WIDE + rest_of(per, WIDE)
    virt, copied = band(per, occ_mask, first)
    virt = in_hbm(virt)
    part = product(per, 0, True, pos, virt, first, at, None)
    part = product(per, 0, False, pos, virt, swapped(copied), 0, part)
    second, part = lax.optimization_barrier((second, part))
    part = product(per, 1, True, pos, virt, second, 0, part)
    part = product(per, 1, False, pos, virt, swapped(second), 0, part)
    return total(exchange(part.reshape(NG, W, 2 * W), GROUP))


def local(three_centre, screen_mask, block_counts, green_occ, occ_mask, green_virt):
    row = lax.axis_index(ROWS)
    col = lax.axis_index(COLS)
    pos = jnp.stack([row, col, lax.axis_index("core")]).astype(jnp.int32)
    live = block_counts[NB]
    branch = (live > 2 * NG).astype(jnp.int32) + (live > 3 * NG).astype(jnp.int32)
    return lax.switch(
        branch,
        [functools.partial(run, per) for per in (2, 3, 4)],
        pos,
        three_centre,
        screen_mask,
        block_counts,
        green_occ,
        occ_mask,
        green_virt,
    )


def solution(mesh):
    fine = Mesh(mesh.devices.reshape(SIZES), AXES)
    in_specs = (P(ROWS + COLS, None, None), P(), P(), P(ROWS, None), P(), P())
    return jax.shard_map(
        local, mesh=fine, in_specs=in_specs, out_specs=P(COLS, ROWS), check_vma=False
    )
```

```python
import functools
import math

import jax
import jax.numpy as jnp
from jax import lax
from jax.experimental import pallas as pl
from jax.experimental.pallas import tpu as pltpu
from jax.sharding import Mesh, PartitionSpec as P

AXES = ("zhi", "zlo", "ylo", "yhi", "x", "core")
SIZES = (2, 2, 2, 2, 4, 2)
ROWS = ("zhi", "zlo", "ylo")
COLS = ("yhi", "x", "core")
GROUP = ("zlo", "ylo", "x")
BS = 64
NU = 64
NB = 8
NG = 16
MUD = 4
SRC = 16
PSL = 4096
W = 256
LINES = 8
TAIL = 128
WIDE = 4 * W
BF = jnp.bfloat16
F32 = jnp.float32
SCALE = -1.0 / math.sqrt(NB * BS * NU)
PARAMS = pltpu.CompilerParams(vmem_limit_bytes=48 * 1024 * 1024)
SMALL = pltpu.CompilerParams(vmem_limit_bytes=28 * 1024 * 1024)


def iota(shape, axis):
    return lax.broadcasted_iota(jnp.int32, shape, axis)


def cost(flops, size):
    return pl.CostEstimate(flops=flops, bytes_accessed=size, transcendentals=0)


def in_hbm(value):
    return pltpu.with_memory_space_constraint(value, pltpu.HBM)


def halves_of(per):
    return 1 if per == 2 else 2


def rest_of(per, width):
    return {2: 0, 3: width // 2, 4: width}[per]


def row_of(per, half, line):
    return line + LINES * half if per != 3 else jnp.where(half > 0, LINES + line % MUD, line)


def pack_kernel(per, part, pos_ref, screen_ref, counts_ref, gv_ref, *refs):
    out_ref, lhs = refs[-2:]
    step = pl.program_id(0)
    row = pos_ref[0]
    col = pos_ref[1]
    halves = halves_of(per)
    rows = LINES * halves
    full = NG * rows

    @pl.when(step == 0)
    def _():
        def place(shape):
            line = iota(shape, 0)
            group, half, line = line // rows, (line % rows) // LINES, line % LINES
            r = row_of(per, half, line)
            return r // per, group * per + r % per

        _, m = place((full, NU))
        pick = (m == iota((full, NU), 1)).astype(F32)
        smalls = [pick]
        if part == 0:
            gv_t = gv_ref[...].astype(F32).T
            smalls.append(jnp.dot(pick, gv_t, preferred_element_type=F32))
        mu, _ = place((full, MUD * NU))
        lane = iota((full, MUD * NU), 1)
        live = (
            (mu == lane // NU)
            & (lane % NU < counts_ref[NB])
            & (mu + MUD * col < counts_ref[row])
        )
        for i, small in enumerate(smalls):
            big = jnp.concatenate([small] * MUD, axis=1)
            lhs[i] = jnp.where(live, big, 0.0).astype(BF)

    half, core = step // 2, step % 2
    sub = iota((1, W), 1) // BS
    low = iota((LINES, W), 0) < MUD

    def column(kind, which, t):
        place = which * 8 + 2 * t + core
        mask = jnp.zeros((1, W), F32)
        for k in range(W // BS):
            on = screen_ref[row, place * (W // BS) + k] > 0
            mask = jnp.where(sub == k, on.astype(F32), mask)
        lanes = pl.ds(pl.multiple_of(place * W, W), W)
        cells = refs[0][:, :, lanes].reshape(MUD * NU, W)
        return jnp.dot(lhs[kind], cells, preferred_element_type=F32) * mask

    def pieces(outs, at):
        wide = len(outs) * W
        for g in range(NG):
            for t, out in enumerate(outs):
                yield g, at + t * W, out[g * rows : g * rows + LINES].astype(BF)
            if per == 2:
                continue
            rest = [out[g * rows + LINES : (g + 1) * rows] for out in outs]
            if per == 3:
                count = len(outs) // 2
                rest = [jnp.where(low, rest[t], rest[t + count]) for t in range(count)]
            for t, piece in enumerate(rest):
                yield g, at + wide + t * W, piece.astype(BF)

    def spot(g):
        return g // 8, (g // 4) % 2, g % 4

    if part == 1:
        outs = [column(0, half, 2 + i) for i in range(2)]
        for g, at, piece in pieces(outs, 0):
            zlo, ylo, xx = spot(g)
            for copy in range(2):
                out_ref[zlo, ylo, copy, xx, :, at : at + W] = piece
        return

    outs = [column(1, half, t) for t in range(4)]
    for g, at, piece in pieces(outs, 0):
        for copy in range(2):
            out_ref[(copy,) + spot(g) + (slice(None), slice(at, at + W))] = piece
    base = WIDE + rest_of(per, WIDE)
    for copy in range(2):
        outs = [column(0, copy, t) for t in range(2)]
        for g, at, piece in pieces(outs, base):
            out_ref[(copy,) + spot(g) + (slice(None), slice(at, at + W))] = piece
    base += 2 * W + rest_of(per, 2 * W)
    green = refs[1][...]
    line, mu = iota((LINES, BS), 0), iota((LINES, BS), 1)
    left = ((mu == MUD * col + line) & (line < MUD)).astype(BF)
    right = ((mu == MUD * col + line - MUD) & (line >= MUD)).astype(BF)
    tail = jnp.dot(left, green[:, :TAIL], preferred_element_type=F32)
    lower = jnp.dot(right, green[:, TAIL:], preferred_element_type=F32)
    tail = (tail + jnp.concatenate([lower, jnp.zeros_like(lower)], axis=1)).astype(BF)
    for g in range(NG):
        for copy in range(2):
            out_ref[(copy,) + spot(g) + (slice(None), slice(base, base + TAIL))] = tail


def pack(per, part, pos, screen_mask, counts, green_virt, green_occ, cells):
    screened = 2 * W + rest_of(per, 2 * W)

    in_specs = [
        pl.BlockSpec((NU, NU), lambda s, *_: (0, 0)),
        pl.BlockSpec((MUD, NU, PSL), lambda s, *_: (0, 0, 0)),
    ]
    operands = [green_virt, cells]
    if part == 0:
        shape = (LINES, WIDE + rest_of(per, WIDE) + screened + TAIL)
        block = (2, 2, 2, None, 4, None) + shape
        index = lambda s, *_: (0, 0, 0, s // 2, 0, s % 2, 0, 0)
        in_specs.append(pl.BlockSpec((BS, 3 * BS), lambda s, *_: (0, 0)))
        operands.append(green_occ)
    else:
        shape = (LINES, screened)
        block = (None, 2, 2, 2, 4, None) + shape
        index = lambda s, *_: (s // 2, 0, 0, 0, 0, s % 2, 0, 0)
    rows = NG * LINES * halves_of(per)
    out = pl.pallas_call(
        functools.partial(pack_kernel, per, part),
        grid_spec=pltpu.PrefetchScalarGridSpec(
            num_scalar_prefetch=3,
            grid=(4,),
            in_specs=in_specs,
            out_specs=pl.BlockSpec(block, index),
            scratch_shapes=[pltpu.VMEM((2 - part, rows, MUD * NU), BF)],
        ),
        out_shape=pltpu.HBM(SIZES + shape, BF),
        compiler_params=PARAMS,
        cost_estimate=cost(2 * rows * 256 * PSL, 6 << 20),
        name=f"pack_{part}",
    )(pos, screen_mask, counts, *operands)
    return out.reshape((128,) + shape)


def band_kernel(per, mask_ref, c0, c1, c2, c3, out_ref, copy_ref):
    step = pl.program_id(0)
    refs = (c0, c1, c2, c3)
    lines = SRC * LINES
    halves = halves_of(per)
    count = lines * halves

    def place(shape, axis):
        at = iota(shape, axis)
        half, at = at // lines, at % lines
        line = at % LINES
        r = row_of(per, half, line)
        return half, line, (at // LINES) * MUD + r // per, r % per

    _, _, mu, _ = place((count, BS), 0)
    spread_rows = (mu == iota((count, BS), 1)).astype(BF)
    _, _, mu, _ = place((BS, count), 1)
    spread_cols = (mu == iota((BS, count), 0)).astype(BF)
    _, _, _, row_j = place((count, count), 0)
    col_half, col_line, _, col_j = place((count, count), 1)
    same = row_j == col_j
    cuts = 2 if per == 3 else 1
    wide = WIDE // cuts
    keeps = [same]
    if per == 3:
        keeps = [same & ((col_half == 0) | (col_line // MUD == cut)) for cut in range(cuts)]
    blocks = []
    for ref in refs:
        cells = []
        for cut in range(cuts):
            parts = [ref[:, cut * wide : (cut + 1) * wide]]
            if halves == 2:
                parts.append(ref[:, WIDE : WIDE + wide])
            cells.append(jnp.concatenate(parts, axis=0))
        blocks.append(cells)
    line, at = iota((BS, lines), 0), iota((BS, lines), 1)
    spot = (line // MUD) * LINES + line % MUD
    take_left = (spot == at).astype(BF)
    take_right = (spot + MUD == at).astype(BF)
    end = c0.shape[1] - TAIL
    for u in range(2):
        copy_ref[u * lines : (u + 1) * lines] = refs[u + 1][:, end - copy_ref.shape[1] : end]
        packed = refs[u + 1][:, end:]
        left = jnp.dot(take_left, packed, preferred_element_type=F32).astype(BF)
        right = jnp.dot(take_right, packed, preferred_element_type=F32).astype(BF)
        left = jnp.dot(spread_rows, left, preferred_element_type=F32).astype(BF)
        right = jnp.dot(spread_rows, right, preferred_element_type=F32).astype(BF)
        totals = [jnp.zeros((count, wide), F32) for _ in range(cuts)]
        for k, part in enumerate((left[:, :BS], left[:, BS:], right[:, :BS])):
            part = jnp.dot(part, spread_cols, preferred_element_type=F32)
            part = part * mask_ref[2 * step + u, k].astype(F32)
            for cut in range(cuts):
                used = jnp.where(keeps[cut], part, 0.0).astype(BF)
                totals[cut] += jnp.dot(used, blocks[u + k][cut], preferred_element_type=F32)
        for cut in range(cuts):
            virt = totals[cut].astype(BF)
            for h in range(halves):
                out_ref[h, cut * wide : (cut + 1) * wide, u * lines : (u + 1) * lines] = virt[
                    h * lines : (h + 1) * lines
                ].T


def band(per, occ_mask, cells):
    lines, full = SRC * LINES, cells.shape[1]
    halves = halves_of(per)
    size = 2 * W + rest_of(per, 2 * W)
    blk = lambda off: pl.BlockSpec((lines, full), lambda s, *_: ((2 * s + off) % NB, 0))
    return pl.pallas_call(
        functools.partial(band_kernel, per),
        grid_spec=pltpu.PrefetchScalarGridSpec(
            num_scalar_prefetch=1,
            grid=(NB // 2,),
            in_specs=[blk(off) for off in (NB - 1, 0, 1, 2)],
            out_specs=[
                pl.BlockSpec((halves, WIDE, 2 * lines), lambda s, *_: (0, 0, s)),
                pl.BlockSpec((2 * lines, size), lambda s, *_: (s, 0)),
            ],
        ),
        out_shape=[
            pltpu.HBM((halves, WIDE, NB * lines), BF),
            pltpu.HBM((NB * lines, size), BF),
        ],
        compiler_params=PARAMS,
        cost_estimate=cost(1 << 20, 1 << 16),
        name="band",
    )(occ_mask, cells, cells, cells, cells)


def product_kernel(per, pos_ref, v_ref, *refs):
    out_ref, acc = refs[-2:]
    step = pl.program_id(0)
    last = halves_of(per) - 1

    def finish(value):
        value = (value * SCALE).astype(BF)
        for t in range(2):
            for x in range(4):
                out_ref[t, x] = value[x * W : (x + 1) * W, t * W : (t + 1) * W]

    @pl.when(step == 0)
    def _():
        value = jnp.dot(v_ref[...], refs[0][...], preferred_element_type=F32)
        if last == 0:
            finish(value)
        else:
            acc[...] = value

    if last == 1:

        @pl.when(step == 1)
        def _():
            cells = refs[1][...]
            if per == 3:
                low = iota(cells.shape, 0) % LINES < MUD
                none = jnp.zeros_like(cells)
                cells = jnp.concatenate(
                    [jnp.where(low, cells, none), jnp.where(low, none, cells)], axis=1
                )
            finish(acc[...] + jnp.dot(v_ref[...], cells, preferred_element_type=F32))


def product(per, group, mine, pos, virt, cells, at, before):
    wide = 2 * W
    halves = halves_of(per)
    rest = rest_of(per, wide)
    depth = virt.shape[2]
    operands = [virt, cells]
    in_specs = [
        pl.BlockSpec((None, WIDE, depth), lambda h, *_: (h, 0, 0)),
        pl.BlockSpec((depth, wide), lambda h, *_: (0, at // wide)),
    ]
    if rest:
        operands.append(cells)
        in_specs.append(pl.BlockSpec((depth, rest), lambda h, *_: (0, (at + wide) // rest)))
    alias = {}
    if before is not None:
        operands.append(before)
        in_specs.append(pl.BlockSpec(memory_space=pl.ANY))
        alias = {len(operands): 0}

    def index(h, pos_ref):
        return group, 0, 0, 0, pos_ref[2] if mine else 1 - pos_ref[2]

    return pl.pallas_call(
        functools.partial(product_kernel, per),
        grid_spec=pltpu.PrefetchScalarGridSpec(
            num_scalar_prefetch=1,
            grid=(halves,),
            in_specs=in_specs,
            out_specs=pl.BlockSpec((None, 2, 4, W, W), index),
            scratch_shapes=[pltpu.VMEM((WIDE, wide), F32)],
        ),
        out_shape=pltpu.HBM((2, 2, 4, W, 2 * W), BF),
        input_output_aliases=alias,
        compiler_params=SMALL,
        cost_estimate=cost(1 << 20, 1 << 16),
        name="product",
    )(pos, *operands)


def total_kernel(ref, out_ref):
    acc = ref[0].astype(F32)
    for k in range(1, NG):
        acc += ref[k].astype(F32)
    out_ref[...] = acc


def total(value):
    tile = 64
    return pl.pallas_call(
        total_kernel,
        grid=(W // tile,),
        in_specs=[pl.BlockSpec((NG, tile, 2 * W), lambda i: (0, i, 0))],
        out_specs=pl.BlockSpec((tile, 2 * W), lambda i: (i, 0)),
        out_shape=pltpu.HBM((W, 2 * W), F32),
        compiler_params=PARAMS,
        cost_estimate=cost(2 << 20, 5 << 20),
        name="total",
    )(value)


def exchange(value, axes):
    return lax.all_to_all(value, axes, split_axis=0, concat_axis=0, tiled=True)


def swapped(value):
    return lax.ppermute(value, "core", [(0, 1), (1, 0)])


def run(per, pos, cells, screen_mask, counts, green_occ, occ_mask, green_virt):
    cells, green_virt = in_hbm(cells), in_hbm(green_virt)
    first = pack(per, 0, pos, screen_mask, counts, green_virt, green_occ, cells)
    second = pack(per, 1, pos, screen_mask, counts, green_virt, green_occ, cells)
    first = exchange(first, AXES)
    second, first = lax.optimization_barrier((second, first))
    second = exchange(second, AXES)
    second = second.reshape(128 * LINES, second.shape[-1])
    first = first.reshape(128 * LINES, first.shape[-1])
    at = WIDE + rest_of(per, WIDE)
    virt, copied = band(per, occ_mask, first)
    virt = in_hbm(virt)
    part = product(per, 0, True, pos, virt, first, at, None)
    part = product(per, 0, False, pos, virt, swapped(copied), 0, part)
    second, part = lax.optimization_barrier((second, part))
    part = product(per, 1, True, pos, virt, second, 0, part)
    part = product(per, 1, False, pos, virt, swapped(second), 0, part)
    return total(exchange(part.reshape(NG, W, 2 * W), GROUP))


def local(three_centre, screen_mask, block_counts, green_occ, occ_mask, green_virt):
    row = lax.axis_index(ROWS)
    col = lax.axis_index(COLS)
    pos = jnp.stack([row, col, lax.axis_index("core")]).astype(jnp.int32)
    live = block_counts[NB]
    branch = (live > 2 * NG).astype(jnp.int32) + (live > 3 * NG).astype(jnp.int32)
    return lax.switch(
        branch,
        [functools.partial(run, per) for per in (2, 3, 4)],
        pos,
        three_centre,
        screen_mask,
        block_counts,
        green_occ,
        occ_mask,
        green_virt,
    )


def solution(mesh):
    fine = Mesh(mesh.devices.reshape(SIZES), AXES)
    in_specs = (P(ROWS + COLS, None, None), P(), P(), P(ROWS, None), P(), P())
    return jax.shard_map(
        local, mesh=fine, in_specs=in_specs, out_specs=P(COLS, ROWS), check_vma=False
    )
```

```python
import functools
import math

import jax
import jax.numpy as jnp
from jax import lax
from jax.experimental import pallas as pl
from jax.experimental.pallas import tpu as pltpu
from jax.sharding import Mesh, PartitionSpec as P

AXES = ("zhi", "zlo", "ylo", "yhi", "x", "core")
SIZES = (2, 2, 2, 2, 4, 2)
ROWS = ("zhi", "zlo", "ylo")
COLS = ("yhi", "x", "core")
GROUP = ("zlo", "ylo", "x")
BS = 64
NU = 64
NB = 8
NG = 16
MUD = 4
SRC = 16
PSL = 4096
W = 256
LINES = 8
TAIL = 128
WIDE = 4 * W
BF = jnp.bfloat16
F32 = jnp.float32
SCALE = -1.0 / math.sqrt(NB * BS * NU)
PARAMS = pltpu.CompilerParams(vmem_limit_bytes=48 * 1024 * 1024)
SMALL = pltpu.CompilerParams(vmem_limit_bytes=28 * 1024 * 1024)


def iota(shape, axis):
    return lax.broadcasted_iota(jnp.int32, shape, axis)


def cost(flops, size):
    return pl.CostEstimate(flops=flops, bytes_accessed=size, transcendentals=0)


def in_hbm(value):
    return pltpu.with_memory_space_constraint(value, pltpu.HBM)


def halves_of(per):
    return 1 if per == 2 else 2


def rest_of(per, width):
    return {2: 0, 3: width // 2, 4: width}[per]


def row_of(per, half, line):
    return line + LINES * half if per != 3 else jnp.where(half > 0, LINES + line % MUD, line)


def pack_kernel(per, part, pos_ref, screen_ref, counts_ref, gv_ref, *refs):
    out_ref, lhs = refs[-2:]
    step = pl.program_id(0)
    row = pos_ref[0]
    col = pos_ref[1]
    halves = halves_of(per)
    rows = LINES * halves
    full = NG * rows

    @pl.when(step == 0)
    def _():
        def place(shape):
            line = iota(shape, 0)
            group, half, line = line // rows, (line % rows) // LINES, line % LINES
            r = row_of(per, half, line)
            return r // per, group * per + r % per

        _, m = place((full, NU))
        pick = (m == iota((full, NU), 1)).astype(F32)
        smalls = [pick]
        if part == 0:
            gv_t = gv_ref[...].astype(F32).T
            smalls.append(jnp.dot(pick, gv_t, preferred_element_type=F32))
        mu, _ = place((full, MUD * NU))
        lane = iota((full, MUD * NU), 1)
        live = (
            (mu == lane // NU)
            & (lane % NU < counts_ref[NB])
            & (mu + MUD * col < counts_ref[row])
        )
        for i, small in enumerate(smalls):
            big = jnp.concatenate([small] * MUD, axis=1)
            lhs[i] = jnp.where(live, big, 0.0).astype(BF)

    half, core = step // 2, step % 2
    sub = iota((1, W), 1) // BS
    low = iota((LINES, W), 0) < MUD

    def column(kind, which, t):
        place = which * 8 + 2 * t + core
        mask = jnp.zeros((1, W), F32)
        for k in range(W // BS):
            on = screen_ref[row, place * (W // BS) + k] > 0
            mask = jnp.where(sub == k, on.astype(F32), mask)
        lanes = pl.ds(pl.multiple_of(place * W, W), W)
        cells = refs[0][:, :, lanes].reshape(MUD * NU, W)
        return jnp.dot(lhs[kind], cells, preferred_element_type=F32) * mask

    def pieces(outs, at):
        wide = len(outs) * W
        for g in range(NG):
            for t, out in enumerate(outs):
                yield g, at + t * W, out[g * rows : g * rows + LINES].astype(BF)
            if per == 2:
                continue
            rest = [out[g * rows + LINES : (g + 1) * rows] for out in outs]
            if per == 3:
                count = len(outs) // 2
                rest = [jnp.where(low, rest[t], rest[t + count]) for t in range(count)]
            for t, piece in enumerate(rest):
                yield g, at + wide + t * W, piece.astype(BF)

    def spot(g):
        return g // 8, (g // 4) % 2, g % 4

    if part == 1:
        outs = [column(0, half, 2 + i) for i in range(2)]
        for g, at, piece in pieces(outs, 0):
            zlo, ylo, xx = spot(g)
            for copy in range(2):
                out_ref[zlo, ylo, copy, xx, :, at : at + W] = piece
        return

    outs = [column(1, half, t) for t in range(4)]
    for g, at, piece in pieces(outs, 0):
        for copy in range(2):
            out_ref[(copy,) + spot(g) + (slice(None), slice(at, at + W))] = piece
    base = WIDE + rest_of(per, WIDE)
    for copy in range(2):
        outs = [column(0, copy, t) for t in range(2)]
        for g, at, piece in pieces(outs, base):
            out_ref[(copy,) + spot(g) + (slice(None), slice(at, at + W))] = piece
    base += 2 * W + rest_of(per, 2 * W)
    green = refs[1][...]
    line, mu = iota((LINES, BS), 0), iota((LINES, BS), 1)
    left = ((mu == MUD * col + line) & (line < MUD)).astype(BF)
    right = ((mu == MUD * col + line - MUD) & (line >= MUD)).astype(BF)
    tail = jnp.dot(left, green[:, :TAIL], preferred_element_type=F32)
    lower = jnp.dot(right, green[:, TAIL:], preferred_element_type=F32)
    tail = (tail + jnp.concatenate([lower, jnp.zeros_like(lower)], axis=1)).astype(BF)
    for g in range(NG):
        for copy in range(2):
            out_ref[(copy,) + spot(g) + (slice(None), slice(base, base + TAIL))] = tail


def pack(per, part, pos, screen_mask, counts, green_virt, green_occ, cells):
    screened = 2 * W + rest_of(per, 2 * W)

    in_specs = [
        pl.BlockSpec((NU, NU), lambda s, *_: (0, 0)),
        pl.BlockSpec((MUD, NU, PSL), lambda s, *_: (0, 0, 0)),
    ]
    operands = [green_virt, cells]
    if part == 0:
        shape = (LINES, WIDE + rest_of(per, WIDE) + screened + TAIL)
        block = (2, 2, 2, None, 4, None) + shape
        index = lambda s, *_: (0, 0, 0, s // 2, 0, s % 2, 0, 0)
        in_specs.append(pl.BlockSpec((BS, 3 * BS), lambda s, *_: (0, 0)))
        operands.append(green_occ)
    else:
        shape = (LINES, screened)
        block = (None, 2, 2, 2, 4, None) + shape
        index = lambda s, *_: (s // 2, 0, 0, 0, 0, s % 2, 0, 0)
    rows = NG * LINES * halves_of(per)
    out = pl.pallas_call(
        functools.partial(pack_kernel, per, part),
        grid_spec=pltpu.PrefetchScalarGridSpec(
            num_scalar_prefetch=3,
            grid=(4,),
            in_specs=in_specs,
            out_specs=pl.BlockSpec(block, index),
            scratch_shapes=[pltpu.VMEM((2 - part, rows, MUD * NU), BF)],
        ),
        out_shape=pltpu.HBM(SIZES + shape, BF),
        compiler_params=PARAMS,
        cost_estimate=cost(2 * rows * 256 * PSL, 6 << 20),
        name=f"pack_{part}",
    )(pos, screen_mask, counts, *operands)
    return out.reshape((128,) + shape)


def band_kernel(per, mask_ref, c0, c1, c2, c3, out_ref, copy_ref):
    step = pl.program_id(0)
    refs = (c0, c1, c2, c3)
    lines = SRC * LINES
    halves = halves_of(per)
    count = lines * halves

    def place(shape, axis):
        at = iota(shape, axis)
        half, at = at // lines, at % lines
        line = at % LINES
        r = row_of(per, half, line)
        return half, line, (at // LINES) * MUD + r // per, r % per

    _, _, mu, _ = place((count, BS), 0)
    spread_rows = (mu == iota((count, BS), 1)).astype(BF)
    _, _, mu, _ = place((BS, count), 1)
    spread_cols = (mu == iota((BS, count), 0)).astype(BF)
    _, _, _, row_j = place((count, count), 0)
    col_half, col_line, _, col_j = place((count, count), 1)
    same = row_j == col_j
    cuts = 2 if per == 3 else 1
    wide = WIDE // cuts
    keeps = [same]
    if per == 3:
        keeps = [same & ((col_half == 0) | (col_line // MUD == cut)) for cut in range(cuts)]
    blocks = []
    for ref in refs:
        cells = []
        for cut in range(cuts):
            parts = [ref[:, cut * wide : (cut + 1) * wide]]
            if halves == 2:
                parts.append(ref[:, WIDE : WIDE + wide])
            cells.append(jnp.concatenate(parts, axis=0))
        blocks.append(cells)
    line, at = iota((BS, lines), 0), iota((BS, lines), 1)
    spot = (line // MUD) * LINES + line % MUD
    take_left = (spot == at).astype(BF)
    take_right = (spot + MUD == at).astype(BF)
    end = c0.shape[1] - TAIL
    for u in range(2):
        copy_ref[u * lines : (u + 1) * lines] = refs[u + 1][:, end - copy_ref.shape[1] : end]
        packed = refs[u + 1][:, end:]
        left = jnp.dot(take_left, packed, preferred_element_type=F32).astype(BF)
        right = jnp.dot(take_right, packed, preferred_element_type=F32).astype(BF)
        left = jnp.dot(spread_rows, left, preferred_element_type=F32).astype(BF)
        right = jnp.dot(spread_rows, right, preferred_element_type=F32).astype(BF)
        totals = [jnp.zeros((count, wide), F32) for _ in range(cuts)]
        for k, part in enumerate((left[:, :BS], left[:, BS:], right[:, :BS])):
            part = jnp.dot(part, spread_cols, preferred_element_type=F32)
            part = part * mask_ref[2 * step + u, k].astype(F32)
            for cut in range(cuts):
                used = jnp.where(keeps[cut], part, 0.0).astype(BF)
                totals[cut] += jnp.dot(used, blocks[u + k][cut], preferred_element_type=F32)
        for cut in range(cuts):
            virt = totals[cut].astype(BF)
            for h in range(halves):
                out_ref[h, cut * wide : (cut + 1) * wide, u * lines : (u + 1) * lines] = virt[
                    h * lines : (h + 1) * lines
                ].T


def band(per, occ_mask, cells):
    lines, full = SRC * LINES, cells.shape[1]
    halves = halves_of(per)
    size = 2 * W + rest_of(per, 2 * W)
    blk = lambda off: pl.BlockSpec((lines, full), lambda s, *_: ((2 * s + off) % NB, 0))
    return pl.pallas_call(
        functools.partial(band_kernel, per),
        grid_spec=pltpu.PrefetchScalarGridSpec(
            num_scalar_prefetch=1,
            grid=(NB // 2,),
            in_specs=[blk(off) for off in (NB - 1, 0, 1, 2)],
            out_specs=[
                pl.BlockSpec((halves, WIDE, 2 * lines), lambda s, *_: (0, 0, s)),
                pl.BlockSpec((2 * lines, size), lambda s, *_: (s, 0)),
            ],
        ),
        out_shape=[
            pltpu.HBM((halves, WIDE, NB * lines), BF),
            pltpu.HBM((NB * lines, size), BF),
        ],
        compiler_params=PARAMS,
        cost_estimate=cost(1 << 20, 1 << 16),
        name="band",
    )(occ_mask, cells, cells, cells, cells)


def product_kernel(per, pos_ref, v_ref, *refs):
    out_ref, acc = refs[-2:]
    step = pl.program_id(0)
    last = halves_of(per) - 1

    def finish(value):
        value = (value * SCALE).astype(BF)
        for t in range(2):
            for x in range(4):
                out_ref[t, x] = value[x * W : (x + 1) * W, t * W : (t + 1) * W]

    @pl.when(step == 0)
    def _():
        value = jnp.dot(v_ref[...], refs[0][...], preferred_element_type=F32)
        if last == 0:
            finish(value)
        else:
            acc[...] = value

    if last == 1:

        @pl.when(step == 1)
        def _():
            cells = refs[1][...]
            if per == 3:
                low = iota(cells.shape, 0) % LINES < MUD
                none = jnp.zeros_like(cells)
                cells = jnp.concatenate(
                    [jnp.where(low, cells, none), jnp.where(low, none, cells)], axis=1
                )
            finish(acc[...] + jnp.dot(v_ref[...], cells, preferred_element_type=F32))


def product(per, group, mine, pos, virt, cells, at, before):
    wide = 2 * W
    halves = halves_of(per)
    rest = rest_of(per, wide)
    depth = virt.shape[2]
    operands = [virt, cells]
    in_specs = [
        pl.BlockSpec((None, WIDE, depth), lambda h, *_: (h, 0, 0)),
        pl.BlockSpec((depth, wide), lambda h, *_: (0, at // wide)),
    ]
    if rest:
        operands.append(cells)
        in_specs.append(pl.BlockSpec((depth, rest), lambda h, *_: (0, (at + wide) // rest)))
    alias = {}
    if before is not None:
        operands.append(before)
        in_specs.append(pl.BlockSpec(memory_space=pl.ANY))
        alias = {len(operands): 0}

    def index(h, pos_ref):
        return group, 0, 0, 0, pos_ref[2] if mine else 1 - pos_ref[2]

    return pl.pallas_call(
        functools.partial(product_kernel, per),
        grid_spec=pltpu.PrefetchScalarGridSpec(
            num_scalar_prefetch=1,
            grid=(halves,),
            in_specs=in_specs,
            out_specs=pl.BlockSpec((None, 2, 4, W, W), index),
            scratch_shapes=[pltpu.VMEM((WIDE, wide), F32)],
        ),
        out_shape=pltpu.HBM((2, 2, 4, W, 2 * W), BF),
        input_output_aliases=alias,
        compiler_params=SMALL,
        cost_estimate=cost(1 << 20, 1 << 16),
        name="product",
    )(pos, *operands)


def total_kernel(ref, out_ref):
    acc = ref[0].astype(F32)
    for k in range(1, NG):
        acc += ref[k].astype(F32)
    out_ref[...] = acc


def total(value):
    tile = 64
    return pl.pallas_call(
        total_kernel,
        grid=(W // tile,),
        in_specs=[pl.BlockSpec((NG, tile, 2 * W), lambda i: (0, i, 0))],
        out_specs=pl.BlockSpec((tile, 2 * W), lambda i: (i, 0)),
        out_shape=pltpu.HBM((W, 2 * W), F32),
        compiler_params=PARAMS,
        cost_estimate=cost(2 << 20, 5 << 20),
        name="total",
    )(value)


def exchange(value, axes):
    return lax.all_to_all(value, axes, split_axis=0, concat_axis=0, tiled=True)


def swapped(value):
    return lax.ppermute(value, "core", [(0, 1), (1, 0)])


def run(per, pos, cells, screen_mask, counts, green_occ, occ_mask, green_virt):
    cells, green_virt = in_hbm(cells), in_hbm(green_virt)
    first = pack(per, 0, pos, screen_mask, counts, green_virt, green_occ, cells)
    second = pack(per, 1, pos, screen_mask, counts, green_virt, green_occ, cells)
    first = exchange(first, AXES)
    second, first = lax.optimization_barrier((second, first))
    second = exchange(second, AXES)
    second = second.reshape(128 * LINES, second.shape[-1])
    first = first.reshape(128 * LINES, first.shape[-1])
    at = WIDE + rest_of(per, WIDE)
    virt, copied = band(per, occ_mask, first)
    virt = in_hbm(virt)
    part = product(per, 0, True, pos, virt, first, at, None)
    part, copied = lax.optimization_barrier((part, copied))
    part = product(per, 0, False, pos, virt, swapped(copied), 0, part)
    second, part = lax.optimization_barrier((second, part))
    part = product(per, 1, True, pos, virt, second, 0, part)
    part = product(per, 1, False, pos, virt, swapped(second), 0, part)
    return total(exchange(part.reshape(NG, W, 2 * W), GROUP))


def local(three_centre, screen_mask, block_counts, green_occ, occ_mask, green_virt):
    row = lax.axis_index(ROWS)
    col = lax.axis_index(COLS)
    pos = jnp.stack([row, col, lax.axis_index("core")]).astype(jnp.int32)
    live = block_counts[NB]
    branch = (live > 2 * NG).astype(jnp.int32) + (live > 3 * NG).astype(jnp.int32)
    return lax.switch(
        branch,
        [functools.partial(run, per) for per in (2, 3, 4)],
        pos,
        three_centre,
        screen_mask,
        block_counts,
        green_occ,
        occ_mask,
        green_virt,
    )


def solution(mesh):
    fine = Mesh(mesh.devices.reshape(SIZES), AXES)
    in_specs = (P(ROWS + COLS, None, None), P(), P(), P(ROWS, None), P(), P())
    return jax.shard_map(
        local, mesh=fine, in_specs=in_specs, out_specs=P(COLS, ROWS), check_vma=False
    )
```

```python
import functools
import math

import jax
import jax.numpy as jnp
from jax import lax
from jax.experimental import pallas as pl
from jax.experimental.pallas import tpu as pltpu
from jax.sharding import Mesh, PartitionSpec as P

AXES = ("zhi", "zlo", "ylo", "yhi", "x", "core")
SIZES = (2, 2, 2, 2, 4, 2)
ROWS = ("zhi", "zlo", "ylo")
COLS = ("yhi", "x", "core")
GROUP = ("zlo", "ylo", "x")
BS = 64
NU = 64
NB = 8
NG = 16
MUD = 4
SRC = 16
PSL = 4096
W = 256
LINES = 8
TAIL = 128
WIDE = 4 * W
BF = jnp.bfloat16
F32 = jnp.float32
SCALE = -1.0 / math.sqrt(NB * BS * NU)
PARAMS = pltpu.CompilerParams(vmem_limit_bytes=48 * 1024 * 1024)
SMALL = pltpu.CompilerParams(vmem_limit_bytes=28 * 1024 * 1024)


def iota(shape, axis):
    return lax.broadcasted_iota(jnp.int32, shape, axis)


def cost(flops, size):
    return pl.CostEstimate(flops=flops, bytes_accessed=size, transcendentals=0)


def in_hbm(value):
    return pltpu.with_memory_space_constraint(value, pltpu.HBM)


def halves_of(per):
    return 1 if per == 2 else 2


def rest_of(per, width):
    return {2: 0, 3: width // 2, 4: width}[per]


def row_of(per, half, line):
    return line + LINES * half if per != 3 else jnp.where(half > 0, LINES + line % MUD, line)


def pack_kernel(per, part, pos_ref, screen_ref, counts_ref, gv_ref, *refs):
    out_ref, lhs = refs[-2:]
    step = pl.program_id(0)
    row = pos_ref[0]
    col = pos_ref[1]
    halves = halves_of(per)
    rows = LINES * halves
    full = NG * rows

    @pl.when(step == 0)
    def _():
        def place(shape):
            line = iota(shape, 0)
            group, half, line = line // rows, (line % rows) // LINES, line % LINES
            r = row_of(per, half, line)
            return r // per, group * per + r % per

        _, m = place((full, NU))
        pick = (m == iota((full, NU), 1)).astype(F32)
        smalls = [pick]
        if part == 0:
            gv_t = gv_ref[...].astype(F32).T
            smalls.append(jnp.dot(pick, gv_t, preferred_element_type=F32))
        mu, _ = place((full, MUD * NU))
        lane = iota((full, MUD * NU), 1)
        live = (
            (mu == lane // NU)
            & (lane % NU < counts_ref[NB])
            & (mu + MUD * col < counts_ref[row])
        )
        for i, small in enumerate(smalls):
            big = jnp.concatenate([small] * MUD, axis=1)
            lhs[i] = jnp.where(live, big, 0.0).astype(BF)

    half, core = step // 2, step % 2
    sub = iota((1, W), 1) // BS
    low = iota((LINES, W), 0) < MUD

    def column(kind, which, t):
        place = which * 8 + 2 * t + core
        mask = jnp.zeros((1, W), F32)
        for k in range(W // BS):
            on = screen_ref[row, place * (W // BS) + k] > 0
            mask = jnp.where(sub == k, on.astype(F32), mask)
        lanes = pl.ds(pl.multiple_of(place * W, W), W)
        cells = refs[0][:, :, lanes].reshape(MUD * NU, W)
        return jnp.dot(lhs[kind], cells, preferred_element_type=F32) * mask

    def pieces(outs, at):
        wide = len(outs) * W
        for g in range(NG):
            for t, out in enumerate(outs):
                yield g, at + t * W, out[g * rows : g * rows + LINES].astype(BF)
            if per == 2:
                continue
            rest = [out[g * rows + LINES : (g + 1) * rows] for out in outs]
            if per == 3:
                count = len(outs) // 2
                rest = [jnp.where(low, rest[t], rest[t + count]) for t in range(count)]
            for t, piece in enumerate(rest):
                yield g, at + wide + t * W, piece.astype(BF)

    def spot(g):
        return g // 8, (g // 4) % 2, g % 4

    if part == 1:
        outs = [column(0, half, 2 + i) for i in range(2)]
        for g, at, piece in pieces(outs, 0):
            zlo, ylo, xx = spot(g)
            for copy in range(2):
                out_ref[zlo, ylo, copy, xx, :, at : at + W] = piece
        return

    outs = [column(1, half, t) for t in range(4)]
    for g, at, piece in pieces(outs, 0):
        for copy in range(2):
            out_ref[(copy,) + spot(g) + (slice(None), slice(at, at + W))] = piece
    base = WIDE + rest_of(per, WIDE)
    for copy in range(2):
        outs = [column(0, copy, t) for t in range(2)]
        for g, at, piece in pieces(outs, base):
            out_ref[(copy,) + spot(g) + (slice(None), slice(at, at + W))] = piece
    base += 2 * W + rest_of(per, 2 * W)
    green = refs[1][...]
    line, mu = iota((LINES, BS), 0), iota((LINES, BS), 1)
    left = ((mu == MUD * col + line) & (line < MUD)).astype(BF)
    right = ((mu == MUD * col + line - MUD) & (line >= MUD)).astype(BF)
    tail = jnp.dot(left, green[:, :TAIL], preferred_element_type=F32)
    lower = jnp.dot(right, green[:, TAIL:], preferred_element_type=F32)
    tail = (tail + jnp.concatenate([lower, jnp.zeros_like(lower)], axis=1)).astype(BF)
    for g in range(NG):
        for copy in range(2):
            out_ref[(copy,) + spot(g) + (slice(None), slice(base, base + TAIL))] = tail


def pack(per, part, pos, screen_mask, counts, green_virt, green_occ, cells):
    screened = 2 * W + rest_of(per, 2 * W)

    in_specs = [
        pl.BlockSpec((NU, NU), lambda s, *_: (0, 0)),
        pl.BlockSpec((MUD, NU, PSL), lambda s, *_: (0, 0, 0)),
    ]
    operands = [green_virt, cells]
    if part == 0:
        shape = (LINES, WIDE + rest_of(per, WIDE) + screened + TAIL)
        block = (2, 2, 2, None, 4, None) + shape
        index = lambda s, *_: (0, 0, 0, s // 2, 0, s % 2, 0, 0)
        in_specs.append(pl.BlockSpec((BS, 3 * BS), lambda s, *_: (0, 0)))
        operands.append(green_occ)
    else:
        shape = (LINES, screened)
        block = (None, 2, 2, 2, 4, None) + shape
        index = lambda s, *_: (s // 2, 0, 0, 0, 0, s % 2, 0, 0)
    rows = NG * LINES * halves_of(per)
    out = pl.pallas_call(
        functools.partial(pack_kernel, per, part),
        grid_spec=pltpu.PrefetchScalarGridSpec(
            num_scalar_prefetch=3,
            grid=(4,),
            in_specs=in_specs,
            out_specs=pl.BlockSpec(block, index),
            scratch_shapes=[pltpu.VMEM((2 - part, rows, MUD * NU), BF)],
        ),
        out_shape=pltpu.HBM(SIZES + shape, BF),
        compiler_params=PARAMS,
        cost_estimate=cost(2 * rows * 256 * PSL, 6 << 20),
        name=f"pack_{part}",
    )(pos, screen_mask, counts, *operands)
    return out.reshape((128,) + shape)


def band_kernel(per, mask_ref, c0, c1, c2, c3, out_ref):
    step = pl.program_id(0)
    refs = (c0, c1, c2, c3)
    lines = SRC * LINES
    halves = halves_of(per)
    count = lines * halves

    def place(shape, axis):
        at = iota(shape, axis)
        half, at = at // lines, at % lines
        line = at % LINES
        r = row_of(per, half, line)
        return half, line, (at // LINES) * MUD + r // per, r % per

    _, _, mu, _ = place((count, BS), 0)
    spread_rows = (mu == iota((count, BS), 1)).astype(BF)
    _, _, mu, _ = place((BS, count), 1)
    spread_cols = (mu == iota((BS, count), 0)).astype(BF)
    _, _, _, row_j = place((count, count), 0)
    col_half, col_line, _, col_j = place((count, count), 1)
    same = row_j == col_j
    cuts = 2 if per == 3 else 1
    wide = WIDE // cuts
    keeps = [same]
    if per == 3:
        keeps = [same & ((col_half == 0) | (col_line // MUD == cut)) for cut in range(cuts)]
    blocks = []
    for ref in refs:
        cells = []
        for cut in range(cuts):
            parts = [ref[:, cut * wide : (cut + 1) * wide]]
            if halves == 2:
                parts.append(ref[:, WIDE : WIDE + wide])
            cells.append(jnp.concatenate(parts, axis=0))
        blocks.append(cells)
    line, at = iota((BS, lines), 0), iota((BS, lines), 1)
    spot = (line // MUD) * LINES + line % MUD
    take_left = (spot == at).astype(BF)
    take_right = (spot + MUD == at).astype(BF)
    end = c0.shape[1] - TAIL
    for u in range(2):
        packed = refs[u + 1][:, end:]
        left = jnp.dot(take_left, packed, preferred_element_type=F32).astype(BF)
        right = jnp.dot(take_right, packed, preferred_element_type=F32).astype(BF)
        left = jnp.dot(spread_rows, left, preferred_element_type=F32).astype(BF)
        right = jnp.dot(spread_rows, right, preferred_element_type=F32).astype(BF)
        totals = [jnp.zeros((count, wide), F32) for _ in range(cuts)]
        for k, part in enumerate((left[:, :BS], left[:, BS:], right[:, :BS])):
            part = jnp.dot(part, spread_cols, preferred_element_type=F32)
            part = part * mask_ref[2 * step + u, k].astype(F32)
            for cut in range(cuts):
                used = jnp.where(keeps[cut], part, 0.0).astype(BF)
                totals[cut] += jnp.dot(used, blocks[u + k][cut], preferred_element_type=F32)
        for cut in range(cuts):
            virt = totals[cut].astype(BF)
            for h in range(halves):
                out_ref[h, cut * wide : (cut + 1) * wide, u * lines : (u + 1) * lines] = virt[
                    h * lines : (h + 1) * lines
                ].T


def band(per, occ_mask, cells):
    lines, full = SRC * LINES, cells.shape[1]
    halves = halves_of(per)
    blk = lambda off: pl.BlockSpec((lines, full), lambda s, *_: ((2 * s + off) % NB, 0))
    return pl.pallas_call(
        functools.partial(band_kernel, per),
        grid_spec=pltpu.PrefetchScalarGridSpec(
            num_scalar_prefetch=1,
            grid=(NB // 2,),
            in_specs=[blk(off) for off in (NB - 1, 0, 1, 2)],
            out_specs=pl.BlockSpec((halves, WIDE, 2 * lines), lambda s, *_: (0, 0, s)),
        ),
        out_shape=pltpu.HBM((halves, WIDE, NB * lines), BF),
        compiler_params=PARAMS,
        cost_estimate=cost(1 << 20, 1 << 16),
        name="band",
    )(occ_mask, cells, cells, cells, cells)


def product_kernel(per, pos_ref, v_ref, *refs):
    out_ref, acc = refs[-2:]
    step = pl.program_id(0)
    last = halves_of(per) - 1

    def finish(value):
        value = (value * SCALE).astype(BF)
        for t in range(2):
            for x in range(4):
                out_ref[t, x] = value[x * W : (x + 1) * W, t * W : (t + 1) * W]

    @pl.when(step == 0)
    def _():
        value = jnp.dot(v_ref[...], refs[0][...], preferred_element_type=F32)
        if last == 0:
            finish(value)
        else:
            acc[...] = value

    if last == 1:

        @pl.when(step == 1)
        def _():
            cells = refs[1][...]
            if per == 3:
                low = iota(cells.shape, 0) % LINES < MUD
                none = jnp.zeros_like(cells)
                cells = jnp.concatenate(
                    [jnp.where(low, cells, none), jnp.where(low, none, cells)], axis=1
                )
            finish(acc[...] + jnp.dot(v_ref[...], cells, preferred_element_type=F32))


def product(per, group, mine, pos, virt, cells, at, before):
    wide = 2 * W
    halves = halves_of(per)
    rest = rest_of(per, wide)
    depth = virt.shape[2]
    operands = [virt, cells]
    in_specs = [
        pl.BlockSpec((None, WIDE, depth), lambda h, *_: (h, 0, 0)),
        pl.BlockSpec((depth, wide), lambda h, *_: (0, at // wide)),
    ]
    if rest:
        operands.append(cells)
        in_specs.append(pl.BlockSpec((depth, rest), lambda h, *_: (0, (at + wide) // rest)))
    alias = {}
    if before is not None:
        operands.append(before)
        in_specs.append(pl.BlockSpec(memory_space=pl.ANY))
        alias = {len(operands): 0}

    def index(h, pos_ref):
        return group, 0, 0, 0, pos_ref[2] if mine else 1 - pos_ref[2]

    return pl.pallas_call(
        functools.partial(product_kernel, per),
        grid_spec=pltpu.PrefetchScalarGridSpec(
            num_scalar_prefetch=1,
            grid=(halves,),
            in_specs=in_specs,
            out_specs=pl.BlockSpec((None, 2, 4, W, W), index),
            scratch_shapes=[pltpu.VMEM((WIDE, wide), F32)],
        ),
        out_shape=pltpu.HBM((2, 2, 4, W, 2 * W), BF),
        input_output_aliases=alias,
        compiler_params=SMALL,
        cost_estimate=cost(1 << 20, 1 << 16),
        name="product",
    )(pos, *operands)


def total_kernel(ref, out_ref):
    acc = ref[0].astype(F32)
    for k in range(1, NG):
        acc += ref[k].astype(F32)
    out_ref[...] = acc


def total(value):
    tile = 64
    return pl.pallas_call(
        total_kernel,
        grid=(W // tile,),
        in_specs=[pl.BlockSpec((NG, tile, 2 * W), lambda i: (0, i, 0))],
        out_specs=pl.BlockSpec((tile, 2 * W), lambda i: (i, 0)),
        out_shape=pltpu.HBM((W, 2 * W), F32),
        compiler_params=PARAMS,
        cost_estimate=cost(2 << 20, 5 << 20),
        name="total",
    )(value)


def exchange(value, axes):
    return lax.all_to_all(value, axes, split_axis=0, concat_axis=0, tiled=True)


def swapped(value):
    return lax.ppermute(value, "core", [(0, 1), (1, 0)])


def run(per, pos, cells, screen_mask, counts, green_occ, occ_mask, green_virt):
    cells, green_virt = in_hbm(cells), in_hbm(green_virt)
    first = pack(per, 0, pos, screen_mask, counts, green_virt, green_occ, cells)
    second = pack(per, 1, pos, screen_mask, counts, green_virt, green_occ, cells)
    first = exchange(first, AXES)
    second, first = lax.optimization_barrier((second, first))
    second = exchange(second, AXES)
    second = second.reshape(128 * LINES, second.shape[-1])
    first = first.reshape(128 * LINES, first.shape[-1])
    at = WIDE + rest_of(per, WIDE)
    virt = in_hbm(band(per, occ_mask, first))
    part = product(per, 0, True, pos, virt, first, at, None)
    part = product(per, 0, False, pos, virt, swapped(first), at, part)
    second, part = lax.optimization_barrier((second, part))
    part = product(per, 1, True, pos, virt, second, 0, part)
    part = product(per, 1, False, pos, virt, swapped(second), 0, part)
    return total(exchange(part.reshape(NG, W, 2 * W), GROUP))


def local(three_centre, screen_mask, block_counts, green_occ, occ_mask, green_virt):
    row = lax.axis_index(ROWS)
    col = lax.axis_index(COLS)
    pos = jnp.stack([row, col, lax.axis_index("core")]).astype(jnp.int32)
    live = block_counts[NB]
    branch = (live > 2 * NG).astype(jnp.int32) + (live > 3 * NG).astype(jnp.int32)
    return lax.switch(
        branch,
        [functools.partial(run, per) for per in (2, 3, 4)],
        pos,
        three_centre,
        screen_mask,
        block_counts,
        green_occ,
        occ_mask,
        green_virt,
    )


def solution(mesh):
    fine = Mesh(mesh.devices.reshape(SIZES), AXES)
    in_specs = (P(ROWS + COLS, None, None), P(), P(), P(ROWS, None), P(), P())
    return jax.shard_map(
        local, mesh=fine, in_specs=in_specs, out_specs=P(COLS, ROWS), check_vma=False
    )
```

```python
import functools
import math

import jax
import jax.numpy as jnp
from jax import lax
from jax.experimental import pallas as pl
from jax.experimental.pallas import tpu as pltpu
from jax.sharding import Mesh, PartitionSpec as P

AXES = ("zhi", "zlo", "ylo", "yhi", "x", "core")
SIZES = (2, 2, 2, 2, 4, 2)
ROWS = ("zhi", "zlo", "ylo")
COLS = ("yhi", "x", "core")
GROUP = ("zlo", "ylo", "x")
BS = 64
NU = 64
NB = 8
NG = 16
MUD = 4
SRC = 16
PSL = 4096
W = 256
H = W // 2
LINES = 8
TAIL = 128
WIDE = 4 * W
BF = jnp.bfloat16
F32 = jnp.float32
SCALE = -1.0 / math.sqrt(NB * BS * NU)
PARAMS = pltpu.CompilerParams(vmem_limit_bytes=48 * 1024 * 1024)
SMALL = pltpu.CompilerParams(vmem_limit_bytes=28 * 1024 * 1024)


def iota(shape, axis):
    return lax.broadcasted_iota(jnp.int32, shape, axis)


def cost(flops, size):
    return pl.CostEstimate(flops=flops, bytes_accessed=size, transcendentals=0)


def in_hbm(value):
    return pltpu.with_memory_space_constraint(value, pltpu.HBM)


def halves_of(per):
    return 1 if per == 2 else 2


def rest_of(per, width):
    return {2: 0, 3: width // 2, 4: width}[per]


def row_of(per, half, line):
    return line + LINES * half if per != 3 else jnp.where(half > 0, LINES + line % MUD, line)


def pack_kernel(per, part, pos_ref, screen_ref, counts_ref, gv_ref, *refs):
    out_ref, lhs = refs[-2:]
    step = pl.program_id(0)
    row = pos_ref[0]
    col = pos_ref[1]
    halves = halves_of(per)
    rows = LINES * halves
    full = NG * rows

    @pl.when(step == 0)
    def _():
        def place(shape):
            line = iota(shape, 0)
            group, half, line = line // rows, (line % rows) // LINES, line % LINES
            r = row_of(per, half, line)
            return r // per, group * per + r % per

        _, m = place((full, NU))
        pick = (m == iota((full, NU), 1)).astype(F32)
        smalls = [pick]
        if part == 0:
            gv_t = gv_ref[...].astype(F32).T
            smalls.append(jnp.dot(pick, gv_t, preferred_element_type=F32))
        mu, _ = place((full, MUD * NU))
        lane = iota((full, MUD * NU), 1)
        live = (
            (mu == lane // NU)
            & (lane % NU < counts_ref[NB])
            & (mu + MUD * col < counts_ref[row])
        )
        for i, small in enumerate(smalls):
            big = jnp.concatenate([small] * MUD, axis=1)
            lhs[i] = jnp.where(live, big, 0.0).astype(BF)

    half, core = step // 2, step % 2

    def column(kind, which, t, wide, at):
        place = (which * 8 + 2 * t + core) * W + at
        mask = jnp.zeros((1, wide), F32)
        for k in range(wide // BS):
            on = screen_ref[row, place // BS + k] > 0
            mask = jnp.where(iota((1, wide), 1) // BS == k, on.astype(F32), mask)
        lanes = pl.ds(pl.multiple_of(place, H), wide)
        cells = refs[0][:, :, lanes].reshape(MUD * NU, wide)
        return jnp.dot(lhs[kind], cells, preferred_element_type=F32) * mask

    def pieces(outs, at):
        size = outs[0].shape[1]
        wide = len(outs) * size
        low = iota((LINES, size), 0) < MUD

        def lanes(first):
            return slice(first, first + size)

        for g in range(NG):
            for t, out in enumerate(outs):
                yield g, lanes(at + t * size), out[g * rows : g * rows + LINES].astype(BF)
            if per == 2:
                continue
            rest = [out[g * rows + LINES : (g + 1) * rows] for out in outs]
            if per == 3:
                count = len(outs) // 2
                rest = [jnp.where(low, rest[t], rest[t + count]) for t in range(count)]
            for t, piece in enumerate(rest):
                yield g, lanes(at + wide + t * size), piece.astype(BF)

    def spot(g):
        return g // 8, (g // 4) % 2, g % 4

    if part == 1:
        outs = [column(0, half, t, H, H) for t in range(4)]
        for g, at, piece in pieces(outs, 0):
            zlo, ylo, xx = spot(g)
            for copy in range(2):
                out_ref[zlo, ylo, copy, xx, :, at] = piece
        return

    outs = [column(1, half, t, W, 0) for t in range(4)]
    for g, at, piece in pieces(outs, 0):
        for copy in range(2):
            out_ref[(copy,) + spot(g) + (slice(None), at)] = piece
    base = WIDE + rest_of(per, WIDE)
    for copy in range(2):
        outs = [column(0, copy, t, H, 0) for t in range(4)]
        for g, at, piece in pieces(outs, base):
            out_ref[(copy,) + spot(g) + (slice(None), at)] = piece
    base += 2 * W + rest_of(per, 2 * W)
    green = refs[1][...]
    line, mu = iota((LINES, BS), 0), iota((LINES, BS), 1)
    left = ((mu == MUD * col + line) & (line < MUD)).astype(BF)
    right = ((mu == MUD * col + line - MUD) & (line >= MUD)).astype(BF)
    tail = jnp.dot(left, green[:, :TAIL], preferred_element_type=F32)
    lower = jnp.dot(right, green[:, TAIL:], preferred_element_type=F32)
    tail = (tail + jnp.concatenate([lower, jnp.zeros_like(lower)], axis=1)).astype(BF)
    for g in range(NG):
        for copy in range(2):
            out_ref[(copy,) + spot(g) + (slice(None), slice(base, base + TAIL))] = tail


def pack(per, part, pos, screen_mask, counts, green_virt, green_occ, cells):
    screened = 2 * W + rest_of(per, 2 * W)

    in_specs = [
        pl.BlockSpec((NU, NU), lambda s, *_: (0, 0)),
        pl.BlockSpec((MUD, NU, PSL), lambda s, *_: (0, 0, 0)),
    ]
    operands = [green_virt, cells]
    if part == 0:
        shape = (LINES, WIDE + rest_of(per, WIDE) + screened + TAIL)
        block = (2, 2, 2, None, 4, None) + shape
        index = lambda s, *_: (0, 0, 0, s // 2, 0, s % 2, 0, 0)
        in_specs.append(pl.BlockSpec((BS, 3 * BS), lambda s, *_: (0, 0)))
        operands.append(green_occ)
    else:
        shape = (LINES, screened)
        block = (None, 2, 2, 2, 4, None) + shape
        index = lambda s, *_: (s // 2, 0, 0, 0, 0, s % 2, 0, 0)
    rows = NG * LINES * halves_of(per)
    out = pl.pallas_call(
        functools.partial(pack_kernel, per, part),
        grid_spec=pltpu.PrefetchScalarGridSpec(
            num_scalar_prefetch=3,
            grid=(4,),
            in_specs=in_specs,
            out_specs=pl.BlockSpec(block, index),
            scratch_shapes=[pltpu.VMEM((2 - part, rows, MUD * NU), BF)],
        ),
        out_shape=pltpu.HBM(SIZES + shape, BF),
        compiler_params=PARAMS,
        cost_estimate=cost(2 * rows * 256 * PSL, 6 << 20),
        name=f"pack_{part}",
    )(pos, screen_mask, counts, *operands)
    return out.reshape((128,) + shape)


def band_kernel(per, mask_ref, c0, c1, c2, c3, out_ref):
    step = pl.program_id(0)
    refs = (c0, c1, c2, c3)
    lines = SRC * LINES
    halves = halves_of(per)
    count = lines * halves

    def place(shape, axis):
        at = iota(shape, axis)
        half, at = at // lines, at % lines
        line = at % LINES
        r = row_of(per, half, line)
        return half, line, (at // LINES) * MUD + r // per, r % per

    _, _, mu, _ = place((count, BS), 0)
    spread_rows = (mu == iota((count, BS), 1)).astype(BF)
    _, _, mu, _ = place((BS, count), 1)
    spread_cols = (mu == iota((BS, count), 0)).astype(BF)
    _, _, _, row_j = place((count, count), 0)
    col_half, col_line, _, col_j = place((count, count), 1)
    same = row_j == col_j
    cuts = 2 if per == 3 else 1
    wide = WIDE // cuts
    keeps = [same]
    if per == 3:
        keeps = [same & ((col_half == 0) | (col_line // MUD == cut)) for cut in range(cuts)]
    blocks = []
    for ref in refs:
        cells = []
        for cut in range(cuts):
            parts = [ref[:, cut * wide : (cut + 1) * wide]]
            if halves == 2:
                parts.append(ref[:, WIDE : WIDE + wide])
            cells.append(jnp.concatenate(parts, axis=0))
        blocks.append(cells)
    line, at = iota((BS, lines), 0), iota((BS, lines), 1)
    spot = (line // MUD) * LINES + line % MUD
    take_left = (spot == at).astype(BF)
    take_right = (spot + MUD == at).astype(BF)
    end = c0.shape[1] - TAIL
    for u in range(2):
        packed = refs[u + 1][:, end:]
        left = jnp.dot(take_left, packed, preferred_element_type=F32).astype(BF)
        right = jnp.dot(take_right, packed, preferred_element_type=F32).astype(BF)
        left = jnp.dot(spread_rows, left, preferred_element_type=F32).astype(BF)
        right = jnp.dot(spread_rows, right, preferred_element_type=F32).astype(BF)
        totals = [jnp.zeros((count, wide), F32) for _ in range(cuts)]
        for k, part in enumerate((left[:, :BS], left[:, BS:], right[:, :BS])):
            part = jnp.dot(part, spread_cols, preferred_element_type=F32)
            part = part * mask_ref[2 * step + u, k].astype(F32)
            for cut in range(cuts):
                used = jnp.where(keeps[cut], part, 0.0).astype(BF)
                totals[cut] += jnp.dot(used, blocks[u + k][cut], preferred_element_type=F32)
        for cut in range(cuts):
            virt = totals[cut].astype(BF)
            for h in range(halves):
                out_ref[h, cut * wide : (cut + 1) * wide, u * lines : (u + 1) * lines] = virt[
                    h * lines : (h + 1) * lines
                ].T


def band(per, occ_mask, cells):
    lines, full = SRC * LINES, cells.shape[1]
    halves = halves_of(per)
    blk = lambda off: pl.BlockSpec((lines, full), lambda s, *_: ((2 * s + off) % NB, 0))
    return pl.pallas_call(
        functools.partial(band_kernel, per),
        grid_spec=pltpu.PrefetchScalarGridSpec(
            num_scalar_prefetch=1,
            grid=(NB // 2,),
            in_specs=[blk(off) for off in (NB - 1, 0, 1, 2)],
            out_specs=pl.BlockSpec((halves, WIDE, 2 * lines), lambda s, *_: (0, 0, s)),
        ),
        out_shape=pltpu.HBM((halves, WIDE, NB * lines), BF),
        compiler_params=PARAMS,
        cost_estimate=cost(1 << 20, 1 << 16),
        name="band",
    )(occ_mask, cells, cells, cells, cells)


def product_kernel(per, by_x, pos_ref, v_ref, *refs):
    out_refs, acc = refs[-5:-1], refs[-1]
    step = pl.program_id(0)
    last = halves_of(per) - 1

    def finish(value):
        acc[...] = value * SCALE
        for i, out_ref in enumerate(out_refs):
            if by_x:
                part = acc[pl.ds(pl.multiple_of(pos_ref[3 + i] * W, W), W), :].astype(BF)
                for t in range(4):
                    out_ref[t] = part[:, t * H : (t + 1) * H]
            else:
                part = acc[:, pl.ds(pl.multiple_of(pos_ref[7 + i] * H, H), H)].astype(BF)
                for x in range(4):
                    out_ref[x] = part[x * W : (x + 1) * W]

    @pl.when(step == 0)
    def _():
        value = jnp.dot(v_ref[...], refs[0][...], preferred_element_type=F32)
        if last == 0:
            finish(value)
        else:
            acc[...] = value

    if last == 1:

        @pl.when(step == 1)
        def _():
            cells = refs[1][...]
            if per == 3:
                low = iota(cells.shape, 0) % LINES < MUD
                none = jnp.zeros_like(cells)
                cells = jnp.concatenate(
                    [jnp.where(low, cells, none), jnp.where(low, none, cells)], axis=1
                )
            finish(acc[...] + jnp.dot(v_ref[...], cells, preferred_element_type=F32))


def product(per, by_x, mine, pos, virt, cells, at, before):
    wide = 4 * H
    halves = halves_of(per)
    rest = rest_of(per, wide)
    depth = virt.shape[2]
    operands = [virt, cells]
    in_specs = [
        pl.BlockSpec((None, WIDE, depth), lambda h, *_: (h, 0, 0)),
        pl.BlockSpec((depth, wide), lambda h, *_: (0, at // wide)),
    ]
    if rest:
        operands.append(cells)
        in_specs.append(pl.BlockSpec((depth, rest), lambda h, *_: (0, (at + wide) // rest)))
    alias = {}
    if before is not None:
        alias = {len(operands) + 1 + i: i for i in range(4)}
        operands += before
        in_specs += [pl.BlockSpec(memory_space=pl.ANY)] * 4

    def index(h, pos_ref):
        return 0, 0, pos_ref[2] if mine else 1 - pos_ref[2]

    return pl.pallas_call(
        functools.partial(product_kernel, per, by_x),
        grid_spec=pltpu.PrefetchScalarGridSpec(
            num_scalar_prefetch=1,
            grid=(halves,),
            in_specs=in_specs,
            out_specs=[pl.BlockSpec((4, W, H), index)] * 4,
            scratch_shapes=[pltpu.VMEM((WIDE, wide), F32)],
        ),
        out_shape=[pltpu.HBM((4, W, W), BF)] * 4,
        input_output_aliases=alias,
        compiler_params=SMALL,
        cost_estimate=cost(2 * halves * depth * WIDE * wide, 7 << 20),
        name="product",
    )(pos, *operands)


def middle_kernel(first, pos_ref, *refs):
    for i in range(4):
        at = pos_ref[first + i]
        value = refs[0][at].astype(F32)
        for ref in refs[1:4]:
            value += ref[at].astype(F32)
        refs[4 + i][...] = value.astype(refs[4 + i].dtype)


def middle(by_x, pos, parts):
    tile = W // 2
    return pl.pallas_call(
        functools.partial(middle_kernel, 7 if by_x else 3),
        grid_spec=pltpu.PrefetchScalarGridSpec(
            num_scalar_prefetch=1,
            grid=(W // tile,),
            in_specs=[pl.BlockSpec((4, tile, W), lambda i, *_: (0, i, 0))] * 4,
            out_specs=[pl.BlockSpec((tile, W), lambda i, *_: (i, 0))] * 4,
        ),
        out_shape=[jax.ShapeDtypeStruct((W, W), F32)] + [jax.ShapeDtypeStruct((W, W), BF)] * 3,
        compiler_params=SMALL,
        cost_estimate=cost(1 << 20, 3 << 20),
        name="middle",
    )(pos, *parts)


def total_kernel(*refs):
    for group in range(2):
        value = refs[4 * group][...]
        for ref in refs[4 * group + 1 : 4 * group + 4]:
            value += ref[...].astype(F32)
        for core in range(2):
            at = core * W + group * H
            refs[8][:, at : at + H] = value[:, core * H : (core + 1) * H]


def total(parts):
    tile = W // 2
    return pl.pallas_call(
        total_kernel,
        grid=(W // tile,),
        in_specs=[pl.BlockSpec((tile, W), lambda i: (i, 0))] * 8,
        out_specs=pl.BlockSpec((tile, 2 * W), lambda i: (i, 0)),
        out_shape=pltpu.HBM((W, 2 * W), F32),
        compiler_params=SMALL,
        cost_estimate=cost(1 << 20, 2 << 20),
        name="total",
    )(*parts)


def along_x(parts):
    moved = [
        lax.ppermute(parts[s], "x", [(i, (i + s) % 4) for i in range(4)]) for s in range(1, 4)
    ]
    return [parts[0]] + moved


def along_t(parts):
    moved = [
        lax.ppermute(parts[d], ("zlo", "ylo"), [(i, i ^ d) for i in range(4)]) for d in range(1, 4)
    ]
    return [parts[0]] + moved


def exchange(value, axes):
    return lax.all_to_all(value, axes, split_axis=0, concat_axis=0, tiled=True)


def swapped(value):
    return lax.ppermute(value, "core", [(0, 1), (1, 0)])


def run(per, pos, cells, screen_mask, counts, green_occ, occ_mask, green_virt):
    cells, green_virt = in_hbm(cells), in_hbm(green_virt)
    first = pack(per, 0, pos, screen_mask, counts, green_virt, green_occ, cells)
    second = pack(per, 1, pos, screen_mask, counts, green_virt, green_occ, cells)
    first = exchange(first, AXES)
    second, first = lax.optimization_barrier((second, first))
    second = exchange(second, AXES)
    second = second.reshape(128 * LINES, second.shape[-1])
    first = first.reshape(128 * LINES, first.shape[-1])
    at = WIDE + rest_of(per, WIDE)
    virt = in_hbm(band(per, occ_mask, first))
    part_a = product(per, True, True, pos, virt, first, at, None)
    part_a = product(per, True, False, pos, virt, swapped(first), at, part_a)
    second, part_a = lax.optimization_barrier((second, part_a))
    sent_a = along_x(part_a)
    part_b = product(per, False, True, pos, virt, second, 0, None)
    part_b = product(per, False, False, pos, virt, swapped(second), 0, part_b)
    sent_b = along_t(part_b)
    sent_a = along_t(middle(True, pos, sent_a))
    sent_b = along_x(middle(False, pos, sent_b))
    return total(sent_a + sent_b)


def positions(row, col):
    x, t = lax.axis_index("x"), lax.axis_index(("zlo", "ylo"))
    receivers = [(x + s) % 4 for s in range(4)] + [t ^ d for d in range(4)]
    return jnp.stack([row, col, lax.axis_index("core")] + receivers).astype(jnp.int32)


def local(three_centre, screen_mask, block_counts, green_occ, occ_mask, green_virt):
    row = lax.axis_index(ROWS)
    col = lax.axis_index(COLS)
    pos = positions(row, col)
    live = block_counts[NB]
    branch = (live > 2 * NG).astype(jnp.int32) + (live > 3 * NG).astype(jnp.int32)
    return lax.switch(
        branch,
        [functools.partial(run, per) for per in (2, 3, 4)],
        pos,
        three_centre,
        screen_mask,
        block_counts,
        green_occ,
        occ_mask,
        green_virt,
    )


def solution(mesh):
    fine = Mesh(mesh.devices.reshape(SIZES), AXES)
    in_specs = (P(ROWS + COLS, None, None), P(), P(), P(ROWS, None), P(), P())
    return jax.shard_map(
        local, mesh=fine, in_specs=in_specs, out_specs=P(COLS, ROWS), check_vma=False
    )
```

```python
import functools
import math

import jax
import jax.numpy as jnp
from jax import lax
from jax.experimental import pallas as pl
from jax.experimental.pallas import tpu as pltpu
from jax.sharding import Mesh, PartitionSpec as P

AXES = ("zhi", "zlo", "ylo", "yhi", "x", "core")
SIZES = (2, 2, 2, 2, 4, 2)
ROWS = ("zhi", "zlo", "ylo")
COLS = ("yhi", "x", "core")
GROUP = ("zlo", "ylo", "x")
BS = 64
NU = 64
NB = 8
NG = 16
MUD = 4
SRC = 16
PSL = 4096
W = 256
H = W // 2
LINES = 8
TAIL = 128
WIDE = 4 * W
BF = jnp.bfloat16
F32 = jnp.float32
SCALE = -1.0 / math.sqrt(NB * BS * NU)
PARAMS = pltpu.CompilerParams(vmem_limit_bytes=48 * 1024 * 1024)
SMALL = pltpu.CompilerParams(vmem_limit_bytes=28 * 1024 * 1024)


def iota(shape, axis):
    return lax.broadcasted_iota(jnp.int32, shape, axis)


def cost(flops, size):
    return pl.CostEstimate(flops=flops, bytes_accessed=size, transcendentals=0)


def in_hbm(value):
    return pltpu.with_memory_space_constraint(value, pltpu.HBM)


def halves_of(per):
    return 1 if per == 2 else 2


def rest_of(per, width):
    return {2: 0, 3: width // 2, 4: width}[per]


def row_of(per, half, line):
    return line + LINES * half if per != 3 else jnp.where(half > 0, LINES + line % MUD, line)


def pack_kernel(per, part, pos_ref, screen_ref, counts_ref, gv_ref, *refs):
    out_ref, lhs = refs[-2:]
    step = pl.program_id(0)
    row = pos_ref[0]
    col = pos_ref[1]
    halves = halves_of(per)
    rows = LINES * halves
    full = NG * rows

    @pl.when(step == 0)
    def _():
        def place(shape):
            line = iota(shape, 0)
            group, half, line = line // rows, (line % rows) // LINES, line % LINES
            r = row_of(per, half, line)
            return r // per, group * per + r % per

        _, m = place((full, NU))
        pick = (m == iota((full, NU), 1)).astype(F32)
        smalls = [pick]
        if part == 0:
            gv_t = gv_ref[...].astype(F32).T
            smalls.append(jnp.dot(pick, gv_t, preferred_element_type=F32))
        mu, _ = place((full, MUD * NU))
        lane = iota((full, MUD * NU), 1)
        live = (
            (mu == lane // NU)
            & (lane % NU < counts_ref[NB])
            & (mu + MUD * col < counts_ref[row])
        )
        for i, small in enumerate(smalls):
            big = jnp.concatenate([small] * MUD, axis=1)
            lhs[i] = jnp.where(live, big, 0.0).astype(BF)

    half, core = step // 2, step % 2

    def column(kind, which, t, wide, at):
        place = (which * 8 + 2 * t + core) * W + at
        mask = jnp.zeros((1, wide), F32)
        for k in range(wide // BS):
            on = screen_ref[row, place // BS + k] > 0
            mask = jnp.where(iota((1, wide), 1) // BS == k, on.astype(F32), mask)
        lanes = pl.ds(pl.multiple_of(place, H), wide)
        cells = refs[0][:, :, lanes].reshape(MUD * NU, wide)
        return jnp.dot(lhs[kind], cells, preferred_element_type=F32) * mask

    def pieces(outs, at):
        size = outs[0].shape[1]
        wide = len(outs) * size
        low = iota((LINES, size), 0) < MUD

        def lanes(first):
            return slice(first, first + size)

        for g in range(NG):
            for t, out in enumerate(outs):
                yield g, lanes(at + t * size), out[g * rows : g * rows + LINES].astype(BF)
            if per == 2:
                continue
            rest = [out[g * rows + LINES : (g + 1) * rows] for out in outs]
            if per == 3:
                count = len(outs) // 2
                rest = [jnp.where(low, rest[t], rest[t + count]) for t in range(count)]
            for t, piece in enumerate(rest):
                yield g, lanes(at + wide + t * size), piece.astype(BF)

    def spot(g):
        return g // 8, (g // 4) % 2, g % 4

    if part == 1:
        outs = [column(0, half, t, H, H) for t in range(4)]
        for g, at, piece in pieces(outs, 0):
            zlo, ylo, xx = spot(g)
            for copy in range(2):
                out_ref[zlo, ylo, copy, xx, :, at] = piece
        return

    outs = [column(1, half, t, W, 0) for t in range(4)]
    for g, at, piece in pieces(outs, 0):
        for copy in range(2):
            out_ref[(copy,) + spot(g) + (slice(None), at)] = piece
    base = WIDE + rest_of(per, WIDE)
    for copy in range(2):
        outs = [column(0, copy, t, H, 0) for t in range(4)]
        for g, at, piece in pieces(outs, base):
            out_ref[(copy,) + spot(g) + (slice(None), at)] = piece
    base += 2 * W + rest_of(per, 2 * W)
    green = refs[1][...]
    line, mu = iota((LINES, BS), 0), iota((LINES, BS), 1)
    left = ((mu == MUD * col + line) & (line < MUD)).astype(BF)
    right = ((mu == MUD * col + line - MUD) & (line >= MUD)).astype(BF)
    tail = jnp.dot(left, green[:, :TAIL], preferred_element_type=F32)
    lower = jnp.dot(right, green[:, TAIL:], preferred_element_type=F32)
    tail = (tail + jnp.concatenate([lower, jnp.zeros_like(lower)], axis=1)).astype(BF)
    for g in range(NG):
        for copy in range(2):
            out_ref[(copy,) + spot(g) + (slice(None), slice(base, base + TAIL))] = tail


def pack(per, part, pos, screen_mask, counts, green_virt, green_occ, cells):
    screened = 2 * W + rest_of(per, 2 * W)

    in_specs = [
        pl.BlockSpec((NU, NU), lambda s, *_: (0, 0)),
        pl.BlockSpec((MUD, NU, PSL), lambda s, *_: (0, 0, 0)),
    ]
    operands = [green_virt, cells]
    if part == 0:
        shape = (LINES, WIDE + rest_of(per, WIDE) + screened + TAIL)
        block = (2, 2, 2, None, 4, None) + shape
        index = lambda s, *_: (0, 0, 0, s // 2, 0, s % 2, 0, 0)
        in_specs.append(pl.BlockSpec((BS, 3 * BS), lambda s, *_: (0, 0)))
        operands.append(green_occ)
    else:
        shape = (LINES, screened)
        block = (None, 2, 2, 2, 4, None) + shape
        index = lambda s, *_: (s // 2, 0, 0, 0, 0, s % 2, 0, 0)
    rows = NG * LINES * halves_of(per)
    out = pl.pallas_call(
        functools.partial(pack_kernel, per, part),
        grid_spec=pltpu.PrefetchScalarGridSpec(
            num_scalar_prefetch=3,
            grid=(4,),
            in_specs=in_specs,
            out_specs=pl.BlockSpec(block, index),
            scratch_shapes=[pltpu.VMEM((2 - part, rows, MUD * NU), BF)],
        ),
        out_shape=pltpu.HBM(SIZES + shape, BF),
        compiler_params=PARAMS,
        cost_estimate=cost(2 * rows * 256 * PSL, 6 << 20),
        name=f"pack_{part}",
    )(pos, screen_mask, counts, *operands)
    return out.reshape((128,) + shape)


def band_kernel(per, mask_ref, c0, c1, c2, out_ref):
    step = pl.program_id(0)
    refs = (c0, c1, c2)
    lines = SRC * LINES
    halves = halves_of(per)
    count = lines * halves

    def place(shape, axis):
        at = iota(shape, axis)
        half, at = at // lines, at % lines
        line = at % LINES
        r = row_of(per, half, line)
        return half, line, (at // LINES) * MUD + r // per, r % per

    _, _, mu, _ = place((count, BS), 0)
    spread_rows = (mu == iota((count, BS), 1)).astype(BF)
    _, _, mu, _ = place((BS, count), 1)
    spread_cols = (mu == iota((BS, count), 0)).astype(BF)
    _, _, _, row_j = place((count, count), 0)
    col_half, col_line, _, col_j = place((count, count), 1)
    same = row_j == col_j
    cuts = 2 if per == 3 else 1
    wide = WIDE // cuts
    keeps = [same]
    if per == 3:
        keeps = [same & ((col_half == 0) | (col_line // MUD == cut)) for cut in range(cuts)]
    blocks = []
    for ref in refs:
        cells = []
        for cut in range(cuts):
            parts = [ref[:, cut * wide : (cut + 1) * wide]]
            if halves == 2:
                parts.append(ref[:, WIDE : WIDE + wide])
            cells.append(jnp.concatenate(parts, axis=0))
        blocks.append(cells)
    line, at = iota((BS, lines), 0), iota((BS, lines), 1)
    spot = (line // MUD) * LINES + line % MUD
    take_left = (spot == at).astype(BF)
    take_right = (spot + MUD == at).astype(BF)
    packed = c1[:, c1.shape[1] - TAIL :]
    left = jnp.dot(take_left, packed, preferred_element_type=F32).astype(BF)
    right = jnp.dot(take_right, packed, preferred_element_type=F32).astype(BF)
    left = jnp.dot(spread_rows, left, preferred_element_type=F32).astype(BF)
    right = jnp.dot(spread_rows, right, preferred_element_type=F32).astype(BF)
    totals = [jnp.zeros((count, wide), F32) for _ in range(cuts)]
    for k, part in enumerate((left[:, :BS], left[:, BS:], right[:, :BS])):
        part = jnp.dot(part, spread_cols, preferred_element_type=F32)
        part = part * mask_ref[step, k].astype(F32)
        for cut in range(cuts):
            used = jnp.where(keeps[cut], part, 0.0).astype(BF)
            totals[cut] += jnp.dot(used, blocks[k][cut], preferred_element_type=F32)
    for cut in range(cuts):
        virt = totals[cut].astype(BF)
        for h in range(halves):
            out_ref[h, cut * wide : (cut + 1) * wide, :] = virt[h * lines : (h + 1) * lines].T


def band(per, occ_mask, cells):
    lines, full = SRC * LINES, cells.shape[1]
    halves = halves_of(per)
    blk = lambda off: pl.BlockSpec((lines, full), lambda s, *_: ((s + off) % NB, 0))
    return pl.pallas_call(
        functools.partial(band_kernel, per),
        grid_spec=pltpu.PrefetchScalarGridSpec(
            num_scalar_prefetch=1,
            grid=(NB,),
            in_specs=[blk(off) for off in (NB - 1, 0, 1)],
            out_specs=pl.BlockSpec((halves, WIDE, lines), lambda s, *_: (0, 0, s)),
        ),
        out_shape=pltpu.HBM((halves, WIDE, NB * lines), BF),
        compiler_params=PARAMS,
        cost_estimate=cost(1 << 20, 1 << 16),
        name="band",
    )(occ_mask, cells, cells, cells)


def product_kernel(per, by_x, pos_ref, v_ref, s_ref, *refs):
    step = pl.program_id(0)
    if per == 3:
        rest_ref, cells, acc = refs[0], refs[-2], refs[-1]
        out_refs = refs[-6:-2]

        @pl.loop(0, s_ref.shape[0] // H)
        def _(n):
            rows = pl.ds(pl.multiple_of(n * H, H), H)
            rest = rest_ref[rows, :]
            low = iota(rest.shape, 0) % LINES < MUD
            none = jnp.zeros_like(rest)
            wide = [jnp.where(low, rest, none), jnp.where(low, none, rest)]
            cells[rows, :] = jnp.where(step == 0, s_ref[rows, :], jnp.concatenate(wide, axis=1))

    else:
        cells, acc = s_ref, refs[-1]
        out_refs = refs[-5:-1]

    tall = acc.shape[0] // 2

    @pl.loop(0, acc.shape[1] // W)
    def _(n):
        lanes = pl.ds(pl.multiple_of(n * W, W), W)

        @pl.loop(0, 2)
        def _(k):
            rows = pl.ds(pl.multiple_of(k * tall, tall), tall)
            before = jnp.where(step == 0, 0.0, acc[rows, lanes])
            acc[rows, lanes] = before + jnp.dot(
                v_ref[rows, :], cells[:, lanes], preferred_element_type=F32
            )

    @pl.when(step == halves_of(per) - 1)
    def _():
        @pl.loop(0, 4)
        def _(k):
            for i, out_ref in enumerate(out_refs):
                x, t = (pos_ref[3 + i], k) if by_x else (k, pos_ref[7 + i])
                rows = pl.ds(pl.multiple_of(x * W, W), W)
                lanes = pl.ds(pl.multiple_of(t * H, H), H)
                out_ref[k] = (acc[rows, lanes] * SCALE).astype(BF)


def product(per, by_x, mine, pos, virt, cells, at, before):
    wide = 4 * H
    halves = halves_of(per)
    rest = rest_of(per, wide)
    depth = virt.shape[2]
    operands = [virt, cells]
    in_specs = [
        pl.BlockSpec((None, WIDE, depth), lambda h, *_: (h, 0, 0)),
        pl.BlockSpec((depth, wide), lambda h, *_: (0, at // wide + (h if per == 4 else 0))),
    ]
    scratch = [pltpu.VMEM((WIDE, wide), F32)]
    if per == 3:
        scratch.insert(0, pltpu.VMEM((depth, wide), BF))
        operands.append(cells)
        in_specs.append(pl.BlockSpec((depth, rest), lambda h, *_: (0, (at + wide) // rest)))
    alias = {}
    if before is not None:
        alias = {len(operands) + 1 + i: i for i in range(4)}
        operands += before
        in_specs += [pl.BlockSpec(memory_space=pl.ANY)] * 4

    def index(h, pos_ref):
        return 0, 0, pos_ref[2] if mine else 1 - pos_ref[2]

    return pl.pallas_call(
        functools.partial(product_kernel, per, by_x),
        grid_spec=pltpu.PrefetchScalarGridSpec(
            num_scalar_prefetch=1,
            grid=(halves,),
            in_specs=in_specs,
            out_specs=[pl.BlockSpec((4, W, H), index)] * 4,
            scratch_shapes=scratch,
        ),
        out_shape=[pltpu.HBM((4, W, W), BF)] * 4,
        input_output_aliases=alias,
        compiler_params=SMALL,
        cost_estimate=cost(2 * halves * depth * WIDE * wide, 7 << 20),
        name="product",
    )(pos, *operands)


def middle_kernel(first, pos_ref, *refs):
    for i in range(4):
        at = pos_ref[first + i]
        value = refs[0][at].astype(F32)
        for ref in refs[1:4]:
            value += ref[at].astype(F32)
        refs[4 + i][...] = value.astype(refs[4 + i].dtype)


def middle(by_x, pos, parts):
    tile = W // 2
    return pl.pallas_call(
        functools.partial(middle_kernel, 7 if by_x else 3),
        grid_spec=pltpu.PrefetchScalarGridSpec(
            num_scalar_prefetch=1,
            grid=(W // tile,),
            in_specs=[pl.BlockSpec((4, tile, W), lambda i, *_: (0, i, 0))] * 4,
            out_specs=[pl.BlockSpec((tile, W), lambda i, *_: (i, 0))] * 4,
        ),
        out_shape=[jax.ShapeDtypeStruct((W, W), F32)] + [jax.ShapeDtypeStruct((W, W), BF)] * 3,
        compiler_params=SMALL,
        cost_estimate=cost(1 << 20, 3 << 20),
        name="middle",
    )(pos, in_hbm(parts[0]), *parts[1:])


def total_kernel(*refs):
    for group in range(2):
        value = refs[4 * group][...]
        for ref in refs[4 * group + 1 : 4 * group + 4]:
            value += ref[...].astype(F32)
        for core in range(2):
            at = core * W + group * H
            refs[8][:, at : at + H] = value[:, core * H : (core + 1) * H]


def total(parts):
    tile = W // 2
    return pl.pallas_call(
        total_kernel,
        grid=(W // tile,),
        in_specs=[pl.BlockSpec((tile, W), lambda i: (i, 0))] * 8,
        out_specs=pl.BlockSpec((tile, 2 * W), lambda i: (i, 0)),
        out_shape=pltpu.HBM((W, 2 * W), F32),
        compiler_params=SMALL,
        cost_estimate=cost(1 << 20, 2 << 20),
        name="total",
    )(*parts)


def along_x(parts):
    moved = [
        lax.ppermute(parts[s], "x", [(i, (i + s) % 4) for i in range(4)]) for s in range(1, 4)
    ]
    return [parts[0]] + moved


def along_t(parts):
    moved = [
        lax.ppermute(parts[d], ("zlo", "ylo"), [(i, i ^ d) for i in range(4)]) for d in range(1, 4)
    ]
    return [parts[0]] + moved


def exchange(value, axes):
    return lax.all_to_all(value, axes, split_axis=0, concat_axis=0, tiled=True)


def swapped(value):
    return lax.ppermute(value, "core", [(0, 1), (1, 0)])


def run(per, pos, cells, screen_mask, counts, green_occ, occ_mask, green_virt):
    cells, green_virt = in_hbm(cells), in_hbm(green_virt)
    first = pack(per, 0, pos, screen_mask, counts, green_virt, green_occ, cells)
    second = pack(per, 1, pos, screen_mask, counts, green_virt, green_occ, cells)
    first = exchange(first, AXES)
    second, first = lax.optimization_barrier((second, first))
    second = exchange(second, AXES)
    second = second.reshape(128 * LINES, second.shape[-1])
    first = first.reshape(128 * LINES, first.shape[-1])
    at = WIDE + rest_of(per, WIDE)
    virt = in_hbm(band(per, occ_mask, first))
    part_a = product(per, True, True, pos, virt, first, at, None)
    part_a = product(per, True, False, pos, virt, swapped(first), at, part_a)
    second, part_a = lax.optimization_barrier((second, part_a))
    sent_a = along_x(part_a)
    part_b = product(per, False, True, pos, virt, second, 0, None)
    part_b = product(per, False, False, pos, virt, swapped(second), 0, part_b)
    sent_b = along_t(part_b)
    sent_a = along_t(middle(True, pos, sent_a))
    sent_b = along_x(middle(False, pos, sent_b))
    return total(sent_a + sent_b)


def positions(row, col):
    x, t = lax.axis_index("x"), lax.axis_index(("zlo", "ylo"))
    receivers = [(x + s) % 4 for s in range(4)] + [t ^ d for d in range(4)]
    return jnp.stack([row, col, lax.axis_index("core")] + receivers).astype(jnp.int32)


def local(three_centre, screen_mask, block_counts, green_occ, occ_mask, green_virt):
    row = lax.axis_index(ROWS)
    col = lax.axis_index(COLS)
    pos = positions(row, col)
    live = block_counts[NB]
    branch = (live > 2 * NG).astype(jnp.int32) + (live > 3 * NG).astype(jnp.int32)
    return lax.switch(
        branch,
        [functools.partial(run, per) for per in (2, 3, 4)],
        pos,
        three_centre,
        screen_mask,
        block_counts,
        green_occ,
        occ_mask,
        green_virt,
    )


def solution(mesh):
    fine = Mesh(mesh.devices.reshape(SIZES), AXES)
    in_specs = (P(ROWS + COLS, None, None), P(), P(), P(ROWS, None), P(), P())
    return jax.shard_map(
        local, mesh=fine, in_specs=in_specs, out_specs=P(COLS, ROWS), check_vma=False
    )
```

```python
import functools
import math

import jax
import jax.numpy as jnp
from jax import lax
from jax.experimental import pallas as pl
from jax.experimental.pallas import tpu as pltpu
from jax.sharding import Mesh, PartitionSpec as P

AXES = ("zhi", "zlo", "ylo", "yhi", "x", "core")
SIZES = (2, 2, 2, 2, 4, 2)
ROWS = ("zhi", "zlo", "ylo")
COLS = ("yhi", "x", "core")
GROUP = ("zlo", "ylo", "x")
BS = 64
NU = 64
NB = 8
NG = 16
MUD = 4
SRC = 16
PSL = 4096
W = 256
H = W // 2
LINES = 8
TAIL = 128
WIDE = 4 * W
BF = jnp.bfloat16
F32 = jnp.float32
SCALE = -1.0 / math.sqrt(NB * BS * NU)
PARAMS = pltpu.CompilerParams(vmem_limit_bytes=48 * 1024 * 1024)
SMALL = pltpu.CompilerParams(vmem_limit_bytes=28 * 1024 * 1024)


def iota(shape, axis):
    return lax.broadcasted_iota(jnp.int32, shape, axis)


def cost(flops, size):
    return pl.CostEstimate(flops=flops, bytes_accessed=size, transcendentals=0)


def in_hbm(value):
    return pltpu.with_memory_space_constraint(value, pltpu.HBM)


def halves_of(per):
    return 1 if per == 2 else 2


def rest_of(per, width):
    return {2: 0, 3: width // 2, 4: width}[per]


def row_of(per, half, line):
    return line + LINES * half if per != 3 else jnp.where(half > 0, LINES + line % MUD, line)


def pack_kernel(per, part, pos_ref, screen_ref, counts_ref, gv_ref, *refs):
    out_ref, lhs = refs[-2:]
    step = pl.program_id(0)
    row = pos_ref[0]
    col = pos_ref[1]
    halves = halves_of(per)
    rows = LINES * halves
    full = NG * rows

    @pl.when(step == 0)
    def _():
        def place(shape):
            line = iota(shape, 0)
            group, half, line = line // rows, (line % rows) // LINES, line % LINES
            r = row_of(per, half, line)
            return r // per, group * per + r % per

        _, m = place((full, NU))
        pick = (m == iota((full, NU), 1)).astype(F32)
        smalls = [pick]
        if part == 0:
            gv_t = gv_ref[...].astype(F32).T
            smalls.append(jnp.dot(pick, gv_t, preferred_element_type=F32))
        mu, _ = place((full, MUD * NU))
        lane = iota((full, MUD * NU), 1)
        live = (
            (mu == lane // NU)
            & (lane % NU < counts_ref[NB])
            & (mu + MUD * col < counts_ref[row])
        )
        for i, small in enumerate(smalls):
            big = jnp.concatenate([small] * MUD, axis=1)
            lhs[i] = jnp.where(live, big, 0.0).astype(BF)

    half, core = step // 2, step % 2

    def column(kind, which, t, wide, at):
        place = (which * 8 + 2 * t + core) * W + at
        mask = jnp.zeros((1, wide), F32)
        for k in range(wide // BS):
            on = screen_ref[row, place // BS + k] > 0
            mask = jnp.where(iota((1, wide), 1) // BS == k, on.astype(F32), mask)
        lanes = pl.ds(pl.multiple_of(place, H), wide)
        cells = refs[0][:, :, lanes].reshape(MUD * NU, wide)
        return jnp.dot(lhs[kind], cells, preferred_element_type=F32) * mask

    def pieces(outs, at):
        size = outs[0].shape[1]
        wide = len(outs) * size
        low = iota((LINES, size), 0) < MUD

        def lanes(first):
            return slice(first, first + size)

        for g in range(NG):
            for t, out in enumerate(outs):
                yield g, lanes(at + t * size), out[g * rows : g * rows + LINES].astype(BF)
            if per == 2:
                continue
            rest = [out[g * rows + LINES : (g + 1) * rows] for out in outs]
            if per == 3:
                count = len(outs) // 2
                rest = [jnp.where(low, rest[t], rest[t + count]) for t in range(count)]
            for t, piece in enumerate(rest):
                yield g, lanes(at + wide + t * size), piece.astype(BF)

    def spot(g):
        return g // 8, (g // 4) % 2, g % 4

    if part == 1:
        outs = [column(0, half, t, H, H) for t in range(4)]
        for g, at, piece in pieces(outs, 0):
            zlo, ylo, xx = spot(g)
            for copy in range(2):
                out_ref[zlo, ylo, copy, xx, :, at] = piece
        return

    outs = [column(1, half, t, W, 0) for t in range(4)]
    for g, at, piece in pieces(outs, 0):
        for copy in range(2):
            out_ref[(copy,) + spot(g) + (slice(None), at)] = piece
    base = WIDE + rest_of(per, WIDE)
    for copy in range(2):
        outs = [column(0, copy, t, H, 0) for t in range(4)]
        for g, at, piece in pieces(outs, base):
            out_ref[(copy,) + spot(g) + (slice(None), at)] = piece
    base += 2 * W + rest_of(per, 2 * W)
    green = refs[1][...]
    line, mu = iota((LINES, BS), 0), iota((LINES, BS), 1)
    left = ((mu == MUD * col + line) & (line < MUD)).astype(BF)
    right = ((mu == MUD * col + line - MUD) & (line >= MUD)).astype(BF)
    tail = jnp.dot(left, green[:, :TAIL], preferred_element_type=F32)
    lower = jnp.dot(right, green[:, TAIL:], preferred_element_type=F32)
    tail = (tail + jnp.concatenate([lower, jnp.zeros_like(lower)], axis=1)).astype(BF)
    for g in range(NG):
        for copy in range(2):
            out_ref[(copy,) + spot(g) + (slice(None), slice(base, base + TAIL))] = tail


def pack(per, part, pos, screen_mask, counts, green_virt, green_occ, cells):
    screened = 2 * W + rest_of(per, 2 * W)

    in_specs = [
        pl.BlockSpec((NU, NU), lambda s, *_: (0, 0)),
        pl.BlockSpec((MUD, NU, PSL), lambda s, *_: (0, 0, 0)),
    ]
    operands = [green_virt, cells]
    if part == 0:
        shape = (LINES, WIDE + rest_of(per, WIDE) + screened + TAIL)
        block = (2, 2, 2, None, 4, None) + shape
        index = lambda s, *_: (0, 0, 0, s // 2, 0, s % 2, 0, 0)
        in_specs.append(pl.BlockSpec((BS, 3 * BS), lambda s, *_: (0, 0)))
        operands.append(green_occ)
    else:
        shape = (LINES, screened)
        block = (None, 2, 2, 2, 4, None) + shape
        index = lambda s, *_: (s // 2, 0, 0, 0, 0, s % 2, 0, 0)
    rows = NG * LINES * halves_of(per)
    out = pl.pallas_call(
        functools.partial(pack_kernel, per, part),
        grid_spec=pltpu.PrefetchScalarGridSpec(
            num_scalar_prefetch=3,
            grid=(4,),
            in_specs=in_specs,
            out_specs=pl.BlockSpec(block, index),
            scratch_shapes=[pltpu.VMEM((2 - part, rows, MUD * NU), BF)],
        ),
        out_shape=pltpu.HBM(SIZES + shape, BF),
        compiler_params=PARAMS,
        cost_estimate=cost(2 * rows * 256 * PSL, 6 << 20),
        name=f"pack_{part}",
    )(pos, screen_mask, counts, *operands)
    return out.reshape((128,) + shape)


def band_kernel(per, mask_ref, c0, c1, c2, out_ref, *scratch):
    step = pl.program_id(0)
    refs = (c0, c1, c2)
    spread_rows, spread_cols, keeps, takes = scratch
    lines = SRC * LINES
    halves = halves_of(per)
    count = lines * halves

    def place(shape, axis):
        at = iota(shape, axis)
        half, at = at // lines, at % lines
        line = at % LINES
        r = row_of(per, half, line)
        return half, line, (at // LINES) * MUD + r // per, r % per

    cuts = 2 if per == 3 else 1
    wide = WIDE // cuts

    @pl.when(step == 0)
    def _():
        _, _, mu, _ = place((count, BS), 0)
        spread_rows[...] = (mu == iota((count, BS), 1)).astype(BF)
        _, _, mu, _ = place((BS, count), 1)
        spread_cols[...] = (mu == iota((BS, count), 0)).astype(BF)
        _, _, _, row_j = place((count, count), 0)
        half, line, _, col_j = place((count, count), 1)
        for cut in range(cuts):
            keep = row_j == col_j
            if per == 3:
                keep = keep & ((half == 0) | (line // MUD == cut))
            keeps[cut] = keep.astype(F32)
        line, at = iota((BS, lines), 0), iota((BS, lines), 1)
        spot = (line // MUD) * LINES + line % MUD
        takes[0] = (spot == at).astype(BF)
        takes[1] = (spot + MUD == at).astype(BF)

    blocks = []
    for ref in refs:
        cells = []
        for cut in range(cuts):
            parts = [ref[:, cut * wide : (cut + 1) * wide]]
            if halves == 2:
                parts.append(ref[:, WIDE : WIDE + wide])
            cells.append(jnp.concatenate(parts, axis=0))
        blocks.append(cells)
    packed = c1[:, c1.shape[1] - TAIL :]
    left = jnp.dot(takes[0], packed, preferred_element_type=F32).astype(BF)
    right = jnp.dot(takes[1], packed, preferred_element_type=F32).astype(BF)
    left = jnp.dot(spread_rows[...], left, preferred_element_type=F32).astype(BF)
    right = jnp.dot(spread_rows[...], right, preferred_element_type=F32).astype(BF)
    totals = [jnp.zeros((count, wide), F32) for _ in range(cuts)]
    for k, part in enumerate((left[:, :BS], left[:, BS:], right[:, :BS])):
        part = jnp.dot(part, spread_cols[...], preferred_element_type=F32)
        part = part * mask_ref[step, k].astype(F32)
        for cut in range(cuts):
            used = (part * keeps[cut]).astype(BF)
            totals[cut] += jnp.dot(used, blocks[k][cut], preferred_element_type=F32)
    for cut in range(cuts):
        virt = totals[cut].astype(BF)
        for h in range(halves):
            out_ref[h, cut * wide : (cut + 1) * wide, :] = virt[h * lines : (h + 1) * lines].T


def band(per, occ_mask, cells):
    lines, full = SRC * LINES, cells.shape[1]
    halves = halves_of(per)
    count = lines * halves
    blk = lambda off: pl.BlockSpec((lines, full), lambda s, *_: ((s + off) % NB, 0))
    return pl.pallas_call(
        functools.partial(band_kernel, per),
        grid_spec=pltpu.PrefetchScalarGridSpec(
            num_scalar_prefetch=1,
            grid=(NB,),
            in_specs=[blk(off) for off in (NB - 1, 0, 1)],
            out_specs=pl.BlockSpec((halves, WIDE, lines), lambda s, *_: (0, 0, s)),
            scratch_shapes=[
                pltpu.VMEM((count, BS), BF),
                pltpu.VMEM((BS, count), BF),
                pltpu.VMEM((2 if per == 3 else 1, count, count), F32),
                pltpu.VMEM((2, BS, lines), BF),
            ],
        ),
        out_shape=pltpu.HBM((halves, WIDE, NB * lines), BF),
        compiler_params=PARAMS,
        cost_estimate=cost(1 << 20, 1 << 16),
        name="band",
    )(occ_mask, cells, cells, cells)


def product_kernel(per, by_x, pos_ref, v_ref, s_ref, *refs):
    half, tile = pl.program_id(0), pl.program_id(1)
    out_refs, acc = refs[-5:-1], refs[-1]
    cells = s_ref[...]
    if per == 3:
        low = iota(cells.shape, 0) % LINES < MUD
        keep = (half == 0) | (low == (tile == 0))
        cells = jnp.where(keep, cells, jnp.zeros_like(cells))
    lanes = pl.ds(pl.multiple_of(tile * W, W), W)
    before = jnp.where(half == 0, 0.0, acc[:, lanes])
    acc[:, lanes] = before + jnp.dot(v_ref[...], cells, preferred_element_type=F32)

    @pl.when((half == halves_of(per) - 1) & (tile == 1))
    def _():
        @pl.loop(0, 4)
        def _(k):
            for i, out_ref in enumerate(out_refs):
                x, t = (pos_ref[3 + i], k) if by_x else (k, pos_ref[7 + i])
                rows = pl.ds(pl.multiple_of(x * W, W), W)
                lanes = pl.ds(pl.multiple_of(t * H, H), H)
                out_ref[k] = (acc[rows, lanes] * SCALE).astype(BF)


def product(per, by_x, mine, pos, virt, cells, at, before):
    wide = 2 * W
    halves = halves_of(per)
    depth = virt.shape[2]

    def column(h, n, *_):
        if per == 3:
            return 0, at // W + jnp.where(h == 0, n, 2)
        return 0, at // W + 2 * h + n

    operands = [virt, cells]
    in_specs = [
        pl.BlockSpec((None, WIDE, depth), lambda h, n, *_: (h, 0, 0)),
        pl.BlockSpec((depth, W), column),
    ]
    alias = {}
    if before is not None:
        alias = {len(operands) + 1 + i: i for i in range(4)}
        operands += before
        in_specs += [pl.BlockSpec(memory_space=pl.ANY)] * 4

    def index(h, n, pos_ref):
        return 0, 0, pos_ref[2] if mine else 1 - pos_ref[2]

    return pl.pallas_call(
        functools.partial(product_kernel, per, by_x),
        grid_spec=pltpu.PrefetchScalarGridSpec(
            num_scalar_prefetch=1,
            grid=(halves, 2),
            in_specs=in_specs,
            out_specs=[pl.BlockSpec((4, W, H), index)] * 4,
            scratch_shapes=[pltpu.VMEM((WIDE, wide), F32)],
        ),
        out_shape=[pltpu.HBM((4, W, W), BF)] * 4,
        input_output_aliases=alias,
        compiler_params=SMALL,
        cost_estimate=cost(2 * halves * depth * WIDE * wide, 7 << 20),
        name="product",
    )(pos, *operands)


def middle_kernel(first, pos_ref, *refs):
    for i in range(4):
        at = pos_ref[first + i]
        value = refs[0][at].astype(F32)
        for ref in refs[1:4]:
            value += ref[at].astype(F32)
        refs[4 + i][...] = value.astype(refs[4 + i].dtype)


def middle(by_x, pos, parts):
    tile = W // 2
    return pl.pallas_call(
        functools.partial(middle_kernel, 7 if by_x else 3),
        grid_spec=pltpu.PrefetchScalarGridSpec(
            num_scalar_prefetch=1,
            grid=(W // tile,),
            in_specs=[pl.BlockSpec((4, tile, W), lambda i, *_: (0, i, 0))] * 4,
            out_specs=[pl.BlockSpec((tile, W), lambda i, *_: (i, 0))] * 4,
        ),
        out_shape=[jax.ShapeDtypeStruct((W, W), F32)] + [jax.ShapeDtypeStruct((W, W), BF)] * 3,
        compiler_params=SMALL,
        cost_estimate=cost(1 << 20, 3 << 20),
        name="middle",
    )(pos, in_hbm(parts[0]), *parts[1:])


def total_kernel(*refs):
    for group in range(2):
        value = refs[4 * group][...]
        for ref in refs[4 * group + 1 : 4 * group + 4]:
            value += ref[...].astype(F32)
        for core in range(2):
            at = core * W + group * H
            refs[8][:, at : at + H] = value[:, core * H : (core + 1) * H]


def total(parts):
    tile = W // 2
    return pl.pallas_call(
        total_kernel,
        grid=(W // tile,),
        in_specs=[pl.BlockSpec((tile, W), lambda i: (i, 0))] * 8,
        out_specs=pl.BlockSpec((tile, 2 * W), lambda i: (i, 0)),
        out_shape=pltpu.HBM((W, 2 * W), F32),
        compiler_params=SMALL,
        cost_estimate=cost(1 << 20, 2 << 20),
        name="total",
    )(*parts)


def along_x(parts):
    moved = [
        lax.ppermute(parts[s], "x", [(i, (i + s) % 4) for i in range(4)]) for s in range(1, 4)
    ]
    return [parts[0]] + moved


def along_t(parts):
    moved = [
        lax.ppermute(parts[d], ("zlo", "ylo"), [(i, i ^ d) for i in range(4)]) for d in range(1, 4)
    ]
    return [parts[0]] + moved


def exchange(value, axes):
    return lax.all_to_all(value, axes, split_axis=0, concat_axis=0, tiled=True)


def swapped(value):
    return lax.ppermute(value, "core", [(0, 1), (1, 0)])


def run(per, pos, cells, screen_mask, counts, green_occ, occ_mask, green_virt):
    cells, green_virt = in_hbm(cells), in_hbm(green_virt)
    first = pack(per, 0, pos, screen_mask, counts, green_virt, green_occ, cells)
    second = pack(per, 1, pos, screen_mask, counts, green_virt, green_occ, cells)
    first = exchange(first, AXES)
    second, first = lax.optimization_barrier((second, first))
    second = exchange(second, AXES)
    second = second.reshape(128 * LINES, second.shape[-1])
    first = first.reshape(128 * LINES, first.shape[-1])
    at = WIDE + rest_of(per, WIDE)
    virt = in_hbm(band(per, occ_mask, first))
    part_a = product(per, True, True, pos, virt, first, at, None)
    part_a = product(per, True, False, pos, virt, swapped(first), at, part_a)
    second, part_a = lax.optimization_barrier((second, part_a))
    sent_a = along_x(part_a)
    part_b = product(per, False, True, pos, virt, second, 0, None)
    part_b = product(per, False, False, pos, virt, swapped(second), 0, part_b)
    sent_b = along_t(part_b)
    sent_a = along_t(middle(True, pos, sent_a))
    sent_b = along_x(middle(False, pos, sent_b))
    return total(sent_a + sent_b)


def positions(row, col):
    x, t = lax.axis_index("x"), lax.axis_index(("zlo", "ylo"))
    receivers = [(x + s) % 4 for s in range(4)] + [t ^ d for d in range(4)]
    return jnp.stack([row, col, lax.axis_index("core")] + receivers).astype(jnp.int32)


def local(three_centre, screen_mask, block_counts, green_occ, occ_mask, green_virt):
    row = lax.axis_index(ROWS)
    col = lax.axis_index(COLS)
    pos = positions(row, col)
    live = block_counts[NB]
    branch = (live > 2 * NG).astype(jnp.int32) + (live > 3 * NG).astype(jnp.int32)
    return lax.switch(
        branch,
        [functools.partial(run, per) for per in (2, 3, 4)],
        pos,
        three_centre,
        screen_mask,
        block_counts,
        green_occ,
        occ_mask,
        green_virt,
    )


def solution(mesh):
    fine = Mesh(mesh.devices.reshape(SIZES), AXES)
    in_specs = (P(ROWS + COLS, None, None), P(), P(), P(ROWS, None), P(), P())
    return jax.shard_map(
        local, mesh=fine, in_specs=in_specs, out_specs=P(COLS, ROWS), check_vma=False
    )
```

```python
import functools
import math

import jax
import jax.numpy as jnp
from jax import lax
from jax.experimental import pallas as pl
from jax.experimental.pallas import tpu as pltpu
from jax.sharding import Mesh, PartitionSpec as P

AXES = ("zhi", "zlo", "ylo", "yhi", "x", "core")
SIZES = (2, 2, 2, 2, 4, 2)
ROWS = ("zhi", "zlo", "ylo")
COLS = ("yhi", "x", "core")
GROUP = ("zlo", "ylo", "x")
BS = 64
NU = 64
NB = 8
NG = 16
MUD = 4
SRC = 16
PSL = 4096
W = 256
H = W // 2
LINES = 8
TAIL = 128
WIDE = 4 * W
BF = jnp.bfloat16
F32 = jnp.float32
SCALE = -1.0 / math.sqrt(NB * BS * NU)
PARAMS = pltpu.CompilerParams(vmem_limit_bytes=48 * 1024 * 1024)
SMALL = pltpu.CompilerParams(vmem_limit_bytes=28 * 1024 * 1024)


def iota(shape, axis):
    return lax.broadcasted_iota(jnp.int32, shape, axis)


def cost(flops, size):
    return pl.CostEstimate(flops=flops, bytes_accessed=size, transcendentals=0)


def in_hbm(value):
    return pltpu.with_memory_space_constraint(value, pltpu.HBM)


def halves_of(per):
    return 1 if per == 2 else 2


def rest_of(per, width):
    return {2: 0, 3: width // 2, 4: width}[per]


def row_of(per, half, line):
    return line + LINES * half if per != 3 else jnp.where(half > 0, LINES + line % MUD, line)


def pack_kernel(per, part, pos_ref, screen_ref, counts_ref, gv_ref, *refs):
    out_ref, lhs = refs[-2:]
    step = pl.program_id(0)
    row = pos_ref[0]
    col = pos_ref[1]
    halves = halves_of(per)
    rows = LINES * halves
    full = NG * rows

    @pl.when(step == 0)
    def _():
        def place(shape):
            line = iota(shape, 0)
            group, half, line = line // rows, (line % rows) // LINES, line % LINES
            r = row_of(per, half, line)
            return r // per, group * per + r % per

        _, m = place((full, NU))
        pick = (m == iota((full, NU), 1)).astype(F32)
        smalls = [pick]
        if part == 0:
            gv_t = gv_ref[...].astype(F32).T
            smalls.append(jnp.dot(pick, gv_t, preferred_element_type=F32))
        mu, _ = place((full, MUD * NU))
        lane = iota((full, MUD * NU), 1)
        live = (
            (mu == lane // NU)
            & (lane % NU < counts_ref[NB])
            & (mu + MUD * col < counts_ref[row])
        )
        for i, small in enumerate(smalls):
            big = jnp.concatenate([small] * MUD, axis=1)
            lhs[i] = jnp.where(live, big, 0.0).astype(BF)

    half, core = step // 2, step % 2

    def column(kind, which, t, wide, at):
        place = (which * 8 + 2 * t + core) * W + at
        mask = jnp.zeros((1, wide), F32)
        for k in range(wide // BS):
            on = screen_ref[row, place // BS + k] > 0
            mask = jnp.where(iota((1, wide), 1) // BS == k, on.astype(F32), mask)
        lanes = pl.ds(pl.multiple_of(place, H), wide)
        cells = refs[0][:, :, lanes].reshape(MUD * NU, wide)
        return jnp.dot(lhs[kind], cells, preferred_element_type=F32) * mask

    def pieces(outs, at):
        size = outs[0].shape[1]
        wide = len(outs) * size
        low = iota((LINES, size), 0) < MUD

        def lanes(first):
            return slice(first, first + size)

        for g in range(NG):
            for t, out in enumerate(outs):
                yield g, lanes(at + t * size), out[g * rows : g * rows + LINES].astype(BF)
            if per == 2:
                continue
            rest = [out[g * rows + LINES : (g + 1) * rows] for out in outs]
            if per == 3:
                count = len(outs) // 2
                rest = [jnp.where(low, rest[t], rest[t + count]) for t in range(count)]
            for t, piece in enumerate(rest):
                yield g, lanes(at + wide + t * size), piece.astype(BF)

    def spot(g):
        return g // 8, (g // 4) % 2, g % 4

    if part == 1:
        outs = [column(0, half, t, H, H) for t in range(4)]
        for g, at, piece in pieces(outs, 0):
            zlo, ylo, xx = spot(g)
            for copy in range(2):
                out_ref[zlo, ylo, copy, xx, :, at] = piece
        return

    outs = [column(1, half, t, W, 0) for t in range(4)]
    for g, at, piece in pieces(outs, 0):
        for copy in range(2):
            out_ref[(copy,) + spot(g) + (slice(None), at)] = piece
    base = WIDE + rest_of(per, WIDE)
    for copy in range(2):
        outs = [column(0, copy, t, H, 0) for t in range(4)]
        for g, at, piece in pieces(outs, base):
            out_ref[(copy,) + spot(g) + (slice(None), at)] = piece
    base += 2 * W + rest_of(per, 2 * W)
    green = refs[1][...]
    line, mu = iota((LINES, BS), 0), iota((LINES, BS), 1)
    left = ((mu == MUD * col + line) & (line < MUD)).astype(BF)
    right = ((mu == MUD * col + line - MUD) & (line >= MUD)).astype(BF)
    tail = jnp.dot(left, green[:, :TAIL], preferred_element_type=F32)
    lower = jnp.dot(right, green[:, TAIL:], preferred_element_type=F32)
    tail = (tail + jnp.concatenate([lower, jnp.zeros_like(lower)], axis=1)).astype(BF)
    for g in range(NG):
        for copy in range(2):
            out_ref[(copy,) + spot(g) + (slice(None), slice(base, base + TAIL))] = tail


def pack(per, part, pos, screen_mask, counts, green_virt, green_occ, cells):
    screened = 2 * W + rest_of(per, 2 * W)

    in_specs = [
        pl.BlockSpec((NU, NU), lambda s, *_: (0, 0)),
        pl.BlockSpec((MUD, NU, PSL), lambda s, *_: (0, 0, 0)),
    ]
    operands = [green_virt, cells]
    if part == 0:
        shape = (LINES, WIDE + rest_of(per, WIDE) + screened + TAIL)
        block = (2, 2, 2, None, 4, None) + shape
        index = lambda s, *_: (0, 0, 0, s // 2, 0, s % 2, 0, 0)
        in_specs.append(pl.BlockSpec((BS, 3 * BS), lambda s, *_: (0, 0)))
        operands.append(green_occ)
    else:
        shape = (LINES, screened)
        block = (None, 2, 2, 2, 4, None) + shape
        index = lambda s, *_: (s // 2, 0, 0, 0, 0, s % 2, 0, 0)
    rows = NG * LINES * halves_of(per)
    out = pl.pallas_call(
        functools.partial(pack_kernel, per, part),
        grid_spec=pltpu.PrefetchScalarGridSpec(
            num_scalar_prefetch=3,
            grid=(4,),
            in_specs=in_specs,
            out_specs=pl.BlockSpec(block, index),
            scratch_shapes=[pltpu.VMEM((2 - part, rows, MUD * NU), BF)],
        ),
        out_shape=pltpu.HBM(SIZES + shape, BF),
        compiler_params=PARAMS,
        cost_estimate=cost(2 * rows * 256 * PSL, 6 << 20),
        name=f"pack_{part}",
    )(pos, screen_mask, counts, *operands)
    return out.reshape((128,) + shape)


def band_kernel(per, mask_ref, c0, c1, c2, c3, out_ref):
    step = pl.program_id(0)
    refs = (c0, c1, c2, c3)
    lines = SRC * LINES
    halves = halves_of(per)
    count = lines * halves

    def place(shape, axis):
        at = iota(shape, axis)
        half, at = at // lines, at % lines
        line = at % LINES
        r = row_of(per, half, line)
        return half, line, (at // LINES) * MUD + r // per, r % per

    _, _, mu, _ = place((count, BS), 0)
    spread_rows = (mu == iota((count, BS), 1)).astype(BF)
    _, _, mu, _ = place((BS, count), 1)
    spread_cols = (mu == iota((BS, count), 0)).astype(BF)
    _, _, _, row_j = place((count, count), 0)
    col_half, col_line, _, col_j = place((count, count), 1)
    same = row_j == col_j
    cuts = 2 if per == 3 else 1
    wide = WIDE // cuts
    keeps = [same]
    if per == 3:
        keeps = [same & ((col_half == 0) | (col_line // MUD == cut)) for cut in range(cuts)]
    blocks = []
    for ref in refs:
        cells = []
        for cut in range(cuts):
            parts = [ref[:, cut * wide : (cut + 1) * wide]]
            if halves == 2:
                parts.append(ref[:, WIDE : WIDE + wide])
            cells.append(jnp.concatenate(parts, axis=0))
        blocks.append(cells)
    line, at = iota((BS, lines), 0), iota((BS, lines), 1)
    spot = (line // MUD) * LINES + line % MUD
    take_left = (spot == at).astype(BF)
    take_right = (spot + MUD == at).astype(BF)
    end = c0.shape[1] - TAIL
    for u in range(2):
        packed = refs[u + 1][:, end:]
        left = jnp.dot(take_left, packed, preferred_element_type=F32).astype(BF)
        right = jnp.dot(take_right, packed, preferred_element_type=F32).astype(BF)
        left = jnp.dot(spread_rows, left, preferred_element_type=F32).astype(BF)
        right = jnp.dot(spread_rows, right, preferred_element_type=F32).astype(BF)
        totals = [jnp.zeros((count, wide), F32) for _ in range(cuts)]
        for k, part in enumerate((left[:, :BS], left[:, BS:], right[:, :BS])):
            part = jnp.dot(part, spread_cols, preferred_element_type=F32)
            part = part * mask_ref[2 * step + u, k].astype(F32)
            for cut in range(cuts):
                used = jnp.where(keeps[cut], part, 0.0).astype(BF)
                totals[cut] += jnp.dot(used, blocks[u + k][cut], preferred_element_type=F32)
        for cut in range(cuts):
            virt = totals[cut].astype(BF)
            for h in range(halves):
                out_ref[h, cut * wide : (cut + 1) * wide, u * lines : (u + 1) * lines] = virt[
                    h * lines : (h + 1) * lines
                ].T


def band(per, occ_mask, cells):
    lines, full = SRC * LINES, cells.shape[1]
    halves = halves_of(per)
    blk = lambda off: pl.BlockSpec((lines, full), lambda s, *_: ((2 * s + off) % NB, 0))
    return pl.pallas_call(
        functools.partial(band_kernel, per),
        grid_spec=pltpu.PrefetchScalarGridSpec(
            num_scalar_prefetch=1,
            grid=(NB // 2,),
            in_specs=[blk(off) for off in (NB - 1, 0, 1, 2)],
            out_specs=pl.BlockSpec((halves, WIDE, 2 * lines), lambda s, *_: (0, 0, s)),
        ),
        out_shape=pltpu.HBM((halves, WIDE, NB * lines), BF),
        compiler_params=PARAMS,
        cost_estimate=cost(1 << 20, 1 << 16),
        name="band",
    )(occ_mask, cells, cells, cells, cells)


def product_kernel(per, by_x, pos_ref, v_ref, *refs):
    out_refs, acc = refs[-5:-1], refs[-1]
    step = pl.program_id(0)
    last = halves_of(per) - 1

    def finish(value):
        acc[...] = value * SCALE
        for i, out_ref in enumerate(out_refs):
            if by_x:
                part = acc[pl.ds(pl.multiple_of(pos_ref[3 + i] * W, W), W), :].astype(BF)
                for t in range(4):
                    out_ref[t] = part[:, t * H : (t + 1) * H]
            else:
                part = acc[:, pl.ds(pl.multiple_of(pos_ref[7 + i] * H, H), H)].astype(BF)
                for x in range(4):
                    out_ref[x] = part[x * W : (x + 1) * W]

    @pl.when(step == 0)
    def _():
        value = jnp.dot(v_ref[...], refs[0][...], preferred_element_type=F32)
        if last == 0:
            finish(value)
        else:
            acc[...] = value

    if last == 1:

        @pl.when(step == 1)
        def _():
            cells = refs[1][...]
            if per == 3:
                low = iota(cells.shape, 0) % LINES < MUD
                none = jnp.zeros_like(cells)
                cells = jnp.concatenate(
                    [jnp.where(low, cells, none), jnp.where(low, none, cells)], axis=1
                )
            finish(acc[...] + jnp.dot(v_ref[...], cells, preferred_element_type=F32))


def product(per, by_x, mine, pos, virt, cells, at, before):
    wide = 4 * H
    halves = halves_of(per)
    rest = rest_of(per, wide)
    depth = virt.shape[2]
    operands = [virt, cells]
    in_specs = [
        pl.BlockSpec((None, WIDE, depth), lambda h, *_: (h, 0, 0)),
        pl.BlockSpec((depth, wide), lambda h, *_: (0, at // wide)),
    ]
    if rest:
        operands.append(cells)
        in_specs.append(pl.BlockSpec((depth, rest), lambda h, *_: (0, (at + wide) // rest)))
    alias = {}
    if before is not None:
        alias = {len(operands) + 1 + i: i for i in range(4)}
        operands += before
        in_specs += [pl.BlockSpec(memory_space=pl.ANY)] * 4

    def index(h, pos_ref):
        return 0, 0, pos_ref[2] if mine else 1 - pos_ref[2]

    return pl.pallas_call(
        functools.partial(product_kernel, per, by_x),
        grid_spec=pltpu.PrefetchScalarGridSpec(
            num_scalar_prefetch=1,
            grid=(halves,),
            in_specs=in_specs,
            out_specs=[pl.BlockSpec((4, W, H), index)] * 4,
            scratch_shapes=[pltpu.VMEM((WIDE, wide), F32)],
        ),
        out_shape=[pltpu.HBM((4, W, W), BF)] * 4,
        input_output_aliases=alias,
        compiler_params=SMALL,
        cost_estimate=cost(2 * halves * depth * WIDE * wide, 7 << 20),
        name="product",
    )(pos, *operands)


def middle_kernel(first, pos_ref, *refs):
    for i in range(4):
        at = pos_ref[first + i]
        value = refs[0][at].astype(F32)
        for ref in refs[1:4]:
            value += ref[at].astype(F32)
        refs[4 + i][...] = value.astype(refs[4 + i].dtype)


def middle(by_x, pos, parts):
    tile = W // 2
    return pl.pallas_call(
        functools.partial(middle_kernel, 7 if by_x else 3),
        grid_spec=pltpu.PrefetchScalarGridSpec(
            num_scalar_prefetch=1,
            grid=(W // tile,),
            in_specs=[pl.BlockSpec((4, tile, W), lambda i, *_: (0, i, 0))] * 4,
            out_specs=[pl.BlockSpec((tile, W), lambda i, *_: (i, 0))] * 4,
        ),
        out_shape=[jax.ShapeDtypeStruct((W, W), F32)] + [jax.ShapeDtypeStruct((W, W), BF)] * 3,
        compiler_params=SMALL,
        cost_estimate=cost(1 << 20, 3 << 20),
        name="middle",
    )(pos, in_hbm(parts[0]), *parts[1:])


def total_kernel(*refs):
    for group in range(2):
        value = refs[4 * group][...]
        for ref in refs[4 * group + 1 : 4 * group + 4]:
            value += ref[...].astype(F32)
        for core in range(2):
            at = core * W + group * H
            refs[8][:, at : at + H] = value[:, core * H : (core + 1) * H]


def total(parts):
    tile = W // 2
    return pl.pallas_call(
        total_kernel,
        grid=(W // tile,),
        in_specs=[pl.BlockSpec((tile, W), lambda i: (i, 0))] * 8,
        out_specs=pl.BlockSpec((tile, 2 * W), lambda i: (i, 0)),
        out_shape=pltpu.HBM((W, 2 * W), F32),
        compiler_params=SMALL,
        cost_estimate=cost(1 << 20, 2 << 20),
        name="total",
    )(*parts)


def along_x(parts):
    moved = [
        lax.ppermute(parts[s], "x", [(i, (i + s) % 4) for i in range(4)]) for s in range(1, 4)
    ]
    return [parts[0]] + moved


def along_t(parts):
    moved = [
        lax.ppermute(parts[d], ("zlo", "ylo"), [(i, i ^ d) for i in range(4)]) for d in range(1, 4)
    ]
    return [parts[0]] + moved


def exchange(value, axes):
    return lax.all_to_all(value, axes, split_axis=0, concat_axis=0, tiled=True)


def swapped(value):
    return lax.ppermute(value, "core", [(0, 1), (1, 0)])


def run(per, pos, cells, screen_mask, counts, green_occ, occ_mask, green_virt):
    cells, green_virt = in_hbm(cells), in_hbm(green_virt)
    first = pack(per, 0, pos, screen_mask, counts, green_virt, green_occ, cells)
    second = pack(per, 1, pos, screen_mask, counts, green_virt, green_occ, cells)
    first = exchange(first, AXES)
    second, first = lax.optimization_barrier((second, first))
    second = exchange(second, AXES)
    second = second.reshape(128 * LINES, second.shape[-1])
    first = first.reshape(128 * LINES, first.shape[-1])
    at = WIDE + rest_of(per, WIDE)
    virt = in_hbm(band(per, occ_mask, first))
    part_a = product(per, True, True, pos, virt, first, at, None)
    part_a = product(per, True, False, pos, virt, swapped(first), at, part_a)
    second, part_a = lax.optimization_barrier((second, part_a))
    sent_a = along_x(part_a)
    part_b = product(per, False, True, pos, virt, second, 0, None)
    part_b = product(per, False, False, pos, virt, swapped(second), 0, part_b)
    sent_b = along_t(part_b)
    sent_a = along_t(middle(True, pos, sent_a))
    sent_b = along_x(middle(False, pos, sent_b))
    return total(sent_a + sent_b)


def positions(row, col):
    x, t = lax.axis_index("x"), lax.axis_index(("zlo", "ylo"))
    receivers = [(x + s) % 4 for s in range(4)] + [t ^ d for d in range(4)]
    return jnp.stack([row, col, lax.axis_index("core")] + receivers).astype(jnp.int32)


def local(three_centre, screen_mask, block_counts, green_occ, occ_mask, green_virt):
    row = lax.axis_index(ROWS)
    col = lax.axis_index(COLS)
    pos = positions(row, col)
    return lax.cond(
        block_counts[NB] > 3 * NG,
        functools.partial(run, 4),
        functools.partial(run, 3),
        pos,
        three_centre,
        screen_mask,
        block_counts,
        green_occ,
        occ_mask,
        green_virt,
    )


def solution(mesh):
    fine = Mesh(mesh.devices.reshape(SIZES), AXES)
    in_specs = (P(ROWS + COLS, None, None), P(), P(), P(ROWS, None), P(), P())
    return jax.shard_map(
        local, mesh=fine, in_specs=in_specs, out_specs=P(COLS, ROWS), check_vma=False
    )
```

```python
import functools
import math

import jax
import jax.numpy as jnp
from jax import lax
from jax.experimental import pallas as pl
from jax.experimental.pallas import tpu as pltpu
from jax.sharding import Mesh, PartitionSpec as P

AXES = ("zhi", "zlo", "ylo", "yhi", "x", "core")
SIZES = (2, 2, 2, 2, 4, 2)
ROWS = ("zhi", "zlo", "ylo")
COLS = ("yhi", "x", "core")
GROUP = ("zlo", "ylo", "x")
BS = 64
NU = 64
NB = 8
NG = 16
MUD = 4
SRC = 16
PSL = 4096
W = 256
H = W // 2
LINES = 8
TAIL = 128
WIDE = 4 * W
BF = jnp.bfloat16
F32 = jnp.float32
SCALE = -1.0 / math.sqrt(NB * BS * NU)
PARAMS = pltpu.CompilerParams(vmem_limit_bytes=48 * 1024 * 1024)
SMALL = pltpu.CompilerParams(vmem_limit_bytes=28 * 1024 * 1024)


def iota(shape, axis):
    return lax.broadcasted_iota(jnp.int32, shape, axis)


def cost(flops, size):
    return pl.CostEstimate(flops=flops, bytes_accessed=size, transcendentals=0)


def in_hbm(value):
    return pltpu.with_memory_space_constraint(value, pltpu.HBM)


def halves_of(per):
    return 1 if per == 2 else 2


def rest_of(per, width):
    return {2: 0, 3: width // 2, 4: width}[per]


def row_of(per, half, line):
    return line + LINES * half if per != 3 else jnp.where(half > 0, LINES + line % MUD, line)


def pack_kernel(per, part, pos_ref, screen_ref, counts_ref, gv_ref, *refs):
    out_ref, lhs = refs[-2:]
    step = pl.program_id(0)
    row = pos_ref[0]
    col = pos_ref[1]
    halves = halves_of(per)
    rows = LINES * halves
    full = NG * rows

    @pl.when(step == 0)
    def _():
        def place(shape):
            line = iota(shape, 0)
            group, half, line = line // rows, (line % rows) // LINES, line % LINES
            r = row_of(per, half, line)
            return r // per, group * per + r % per

        _, m = place((full, NU))
        pick = (m == iota((full, NU), 1)).astype(F32)
        smalls = [pick]
        if part == 0:
            gv_t = gv_ref[...].astype(F32).T
            smalls.append(jnp.dot(pick, gv_t, preferred_element_type=F32))
        mu, _ = place((full, MUD * NU))
        lane = iota((full, MUD * NU), 1)
        live = (
            (mu == lane // NU)
            & (lane % NU < counts_ref[NB])
            & (mu + MUD * col < counts_ref[row])
        )
        for i, small in enumerate(smalls):
            big = jnp.concatenate([small] * MUD, axis=1)
            lhs[i] = jnp.where(live, big, 0.0).astype(BF)

    half, core = step // 2, step % 2

    def column(kind, which, t, wide, at):
        place = (which * 8 + 2 * t + core) * W + at
        mask = jnp.zeros((1, wide), F32)
        for k in range(wide // BS):
            on = screen_ref[row, place // BS + k] > 0
            mask = jnp.where(iota((1, wide), 1) // BS == k, on.astype(F32), mask)
        lanes = pl.ds(pl.multiple_of(place, H), wide)
        cells = refs[0][:, :, lanes].reshape(MUD * NU, wide)
        return jnp.dot(lhs[kind], cells, preferred_element_type=F32) * mask

    def pieces(outs, at):
        size = outs[0].shape[1]
        wide = len(outs) * size
        low = iota((LINES, size), 0) < MUD

        def lanes(first):
            return slice(first, first + size)

        for g in range(NG):
            for t, out in enumerate(outs):
                yield g, lanes(at + t * size), out[g * rows : g * rows + LINES].astype(BF)
            if per == 2:
                continue
            rest = [out[g * rows + LINES : (g + 1) * rows] for out in outs]
            if per == 3:
                count = len(outs) // 2
                rest = [jnp.where(low, rest[t], rest[t + count]) for t in range(count)]
            for t, piece in enumerate(rest):
                yield g, lanes(at + wide + t * size), piece.astype(BF)

    def spot(g):
        return g // 8, (g // 4) % 2, g % 4

    if part == 1:
        outs = [column(0, half, t, H, H) for t in range(4)]
        for g, at, piece in pieces(outs, 0):
            zlo, ylo, xx = spot(g)
            for copy in range(2):
                out_ref[zlo, ylo, copy, xx, :, at] = piece
        return

    outs = [column(1, half, t, W, 0) for t in range(4)]
    for g, at, piece in pieces(outs, 0):
        for copy in range(2):
            out_ref[(copy,) + spot(g) + (slice(None), at)] = piece
    base = WIDE + rest_of(per, WIDE)
    for copy in range(2):
        outs = [column(0, copy, t, H, 0) for t in range(4)]
        for g, at, piece in pieces(outs, base):
            out_ref[(copy,) + spot(g) + (slice(None), at)] = piece
    base += 2 * W + rest_of(per, 2 * W)
    green = refs[1][...]
    line, mu = iota((LINES, BS), 0), iota((LINES, BS), 1)
    left = ((mu == MUD * col + line) & (line < MUD)).astype(BF)
    right = ((mu == MUD * col + line - MUD) & (line >= MUD)).astype(BF)
    tail = jnp.dot(left, green[:, :TAIL], preferred_element_type=F32)
    lower = jnp.dot(right, green[:, TAIL:], preferred_element_type=F32)
    tail = (tail + jnp.concatenate([lower, jnp.zeros_like(lower)], axis=1)).astype(BF)
    for g in range(NG):
        for copy in range(2):
            out_ref[(copy,) + spot(g) + (slice(None), slice(base, base + TAIL))] = tail


def pack(per, part, pos, screen_mask, counts, green_virt, green_occ, cells):
    screened = 2 * W + rest_of(per, 2 * W)

    in_specs = [
        pl.BlockSpec((NU, NU), lambda s, *_: (0, 0)),
        pl.BlockSpec((MUD, NU, PSL), lambda s, *_: (0, 0, 0)),
    ]
    operands = [green_virt, cells]
    if part == 0:
        shape = (LINES, WIDE + rest_of(per, WIDE) + screened + TAIL)
        block = (2, 2, 2, None, 4, None) + shape
        index = lambda s, *_: (0, 0, 0, s // 2, 0, s % 2, 0, 0)
        in_specs.append(pl.BlockSpec((BS, 3 * BS), lambda s, *_: (0, 0)))
        operands.append(green_occ)
    else:
        shape = (LINES, screened)
        block = (None, 2, 2, 2, 4, None) + shape
        index = lambda s, *_: (s // 2, 0, 0, 0, 0, s % 2, 0, 0)
    rows = NG * LINES * halves_of(per)
    out = pl.pallas_call(
        functools.partial(pack_kernel, per, part),
        grid_spec=pltpu.PrefetchScalarGridSpec(
            num_scalar_prefetch=3,
            grid=(4,),
            in_specs=in_specs,
            out_specs=pl.BlockSpec(block, index),
            scratch_shapes=[pltpu.VMEM((2 - part, rows, MUD * NU), BF)],
        ),
        out_shape=pltpu.HBM(SIZES + shape, BF),
        compiler_params=PARAMS,
        cost_estimate=cost(2 * rows * 256 * PSL, 6 << 20),
        name=f"pack_{part}",
    )(pos, screen_mask, counts, *operands)
    return out.reshape((128,) + shape)


def band_kernel(per, mask_ref, c0, c1, c2, c3, out_ref):
    step = pl.program_id(0)
    refs = (c0, c1, c2, c3)
    lines = SRC * LINES
    halves = halves_of(per)
    count = lines * halves

    def place(shape, axis):
        at = iota(shape, axis)
        half, at = at // lines, at % lines
        line = at % LINES
        r = row_of(per, half, line)
        return half, line, (at // LINES) * MUD + r // per, r % per

    _, _, mu, _ = place((count, BS), 0)
    spread_rows = (mu == iota((count, BS), 1)).astype(BF)
    _, _, mu, _ = place((BS, count), 1)
    spread_cols = (mu == iota((BS, count), 0)).astype(BF)
    _, _, _, row_j = place((count, count), 0)
    col_half, col_line, _, col_j = place((count, count), 1)
    same = row_j == col_j
    cuts = 2 if per == 3 else 1
    wide = WIDE // cuts
    keeps = [same]
    if per == 3:
        keeps = [same & ((col_half == 0) | (col_line // MUD == cut)) for cut in range(cuts)]
    blocks = []
    for ref in refs:
        cells = []
        for cut in range(cuts):
            parts = [ref[:, cut * wide : (cut + 1) * wide]]
            if halves == 2:
                parts.append(ref[:, WIDE : WIDE + wide])
            cells.append(jnp.concatenate(parts, axis=0))
        blocks.append(cells)
    line, at = iota((BS, lines), 0), iota((BS, lines), 1)
    spot = (line // MUD) * LINES + line % MUD
    take_left = (spot == at).astype(BF)
    take_right = (spot + MUD == at).astype(BF)
    end = c0.shape[1] - TAIL
    for u in range(2):
        packed = refs[u + 1][:, end:]
        left = jnp.dot(take_left, packed, preferred_element_type=F32).astype(BF)
        right = jnp.dot(take_right, packed, preferred_element_type=F32).astype(BF)
        left = jnp.dot(spread_rows, left, preferred_element_type=F32).astype(BF)
        right = jnp.dot(spread_rows, right, preferred_element_type=F32).astype(BF)
        totals = [jnp.zeros((count, wide), F32) for _ in range(cuts)]
        for k, part in enumerate((left[:, :BS], left[:, BS:], right[:, :BS])):
            part = jnp.dot(part, spread_cols, preferred_element_type=F32)
            part = part * mask_ref[2 * step + u, k].astype(F32)
            for cut in range(cuts):
                used = jnp.where(keeps[cut], part, 0.0).astype(BF)
                totals[cut] += jnp.dot(used, blocks[u + k][cut], preferred_element_type=F32)
        for cut in range(cuts):
            virt = totals[cut].astype(BF)
            for h in range(halves):
                out_ref[h, cut * wide : (cut + 1) * wide, u * lines : (u + 1) * lines] = virt[
                    h * lines : (h + 1) * lines
                ].T


def band(per, occ_mask, cells):
    lines, full = SRC * LINES, cells.shape[1]
    halves = halves_of(per)
    blk = lambda off: pl.BlockSpec((lines, full), lambda s, *_: ((2 * s + off) % NB, 0))
    return pl.pallas_call(
        functools.partial(band_kernel, per),
        grid_spec=pltpu.PrefetchScalarGridSpec(
            num_scalar_prefetch=1,
            grid=(NB // 2,),
            in_specs=[blk(off) for off in (NB - 1, 0, 1, 2)],
            out_specs=pl.BlockSpec((halves, WIDE, 2 * lines), lambda s, *_: (0, 0, s)),
        ),
        out_shape=pltpu.HBM((halves, WIDE, NB * lines), BF),
        compiler_params=PARAMS,
        cost_estimate=cost(1 << 20, 1 << 16),
        name="band",
    )(occ_mask, cells, cells, cells, cells)


def product_kernel(per, by_x, pos_ref, v_ref, *refs):
    out_refs, acc = refs[-5:-1], refs[-1]
    step = pl.program_id(0)
    last = halves_of(per) - 1

    def finish(value):
        acc[...] = value * SCALE
        for i, out_ref in enumerate(out_refs):
            if by_x:
                part = acc[pl.ds(pl.multiple_of(pos_ref[3 + i] * W, W), W), :].astype(BF)
                for t in range(4):
                    out_ref[t] = part[:, t * H : (t + 1) * H]
            else:
                part = acc[:, pl.ds(pl.multiple_of(pos_ref[7 + i] * H, H), H)].astype(BF)
                for x in range(4):
                    out_ref[x] = part[x * W : (x + 1) * W]

    @pl.when(step == 0)
    def _():
        value = jnp.dot(v_ref[...], refs[0][...], preferred_element_type=F32)
        if last == 0:
            finish(value)
        else:
            acc[...] = value

    if last == 1:

        @pl.when(step == 1)
        def _():
            cells = refs[1][...]
            if per == 3:
                low = iota(cells.shape, 0) % LINES < MUD
                none = jnp.zeros_like(cells)
                cells = jnp.concatenate(
                    [jnp.where(low, cells, none), jnp.where(low, none, cells)], axis=1
                )
            finish(acc[...] + jnp.dot(v_ref[...], cells, preferred_element_type=F32))


def product(per, by_x, mine, pos, virt, cells, at, before):
    wide = 4 * H
    halves = halves_of(per)
    rest = rest_of(per, wide)
    depth = virt.shape[2]
    operands = [virt, cells]
    in_specs = [
        pl.BlockSpec((None, WIDE, depth), lambda h, *_: (h, 0, 0)),
        pl.BlockSpec((depth, wide), lambda h, *_: (0, at // wide)),
    ]
    if rest:
        operands.append(cells)
        in_specs.append(pl.BlockSpec((depth, rest), lambda h, *_: (0, (at + wide) // rest)))
    alias = {}
    if before is not None:
        alias = {len(operands) + 1 + i: i for i in range(4)}
        operands += before
        in_specs += [pl.BlockSpec(memory_space=pl.ANY)] * 4

    def index(h, pos_ref):
        return 0, 0, pos_ref[2] if mine else 1 - pos_ref[2]

    return pl.pallas_call(
        functools.partial(product_kernel, per, by_x),
        grid_spec=pltpu.PrefetchScalarGridSpec(
            num_scalar_prefetch=1,
            grid=(halves,),
            in_specs=in_specs,
            out_specs=[pl.BlockSpec((4, W, H), index)] * 4,
            scratch_shapes=[pltpu.VMEM((WIDE, wide), F32)],
        ),
        out_shape=[pltpu.HBM((4, W, W), BF)] * 4,
        input_output_aliases=alias,
        compiler_params=SMALL,
        cost_estimate=cost(2 * halves * depth * WIDE * wide, 7 << 20),
        name="product",
    )(pos, *operands)


def middle_kernel(first, pos_ref, *refs):
    for i in range(4):
        at = pos_ref[first + i]
        value = refs[0][at].astype(F32)
        for ref in refs[1:4]:
            value += ref[at].astype(F32)
        refs[4 + i][...] = value.astype(refs[4 + i].dtype)


def middle(by_x, pos, parts):
    tile = W // 2
    return pl.pallas_call(
        functools.partial(middle_kernel, 7 if by_x else 3),
        grid_spec=pltpu.PrefetchScalarGridSpec(
            num_scalar_prefetch=1,
            grid=(W // tile,),
            in_specs=[pl.BlockSpec((4, tile, W), lambda i, *_: (0, i, 0))] * 4,
            out_specs=[pl.BlockSpec((tile, W), lambda i, *_: (i, 0))] * 4,
        ),
        out_shape=[jax.ShapeDtypeStruct((W, W), F32)] + [jax.ShapeDtypeStruct((W, W), BF)] * 3,
        compiler_params=SMALL,
        cost_estimate=cost(1 << 20, 3 << 20),
        name="middle",
    )(pos, in_hbm(parts[0]), *parts[1:])


def total_kernel(*refs):
    for group in range(2):
        value = refs[4 * group][...]
        for ref in refs[4 * group + 1 : 4 * group + 4]:
            value += ref[...].astype(F32)
        for core in range(2):
            at = core * W + group * H
            refs[8][:, at : at + H] = value[:, core * H : (core + 1) * H]


def total(parts):
    tile = W // 2
    return pl.pallas_call(
        total_kernel,
        grid=(W // tile,),
        in_specs=[pl.BlockSpec((tile, W), lambda i: (i, 0))] * 8,
        out_specs=pl.BlockSpec((tile, 2 * W), lambda i: (i, 0)),
        out_shape=pltpu.HBM((W, 2 * W), F32),
        compiler_params=SMALL,
        cost_estimate=cost(1 << 20, 2 << 20),
        name="total",
    )(*parts)


def along_x(parts):
    moved = [
        lax.ppermute(parts[s], "x", [(i, (i + s) % 4) for i in range(4)]) for s in range(1, 4)
    ]
    return [parts[0]] + moved


def along_t(parts):
    moved = [
        lax.ppermute(parts[d], ("zlo", "ylo"), [(i, i ^ d) for i in range(4)]) for d in range(1, 4)
    ]
    return [parts[0]] + moved


def exchange(value, axes):
    return lax.all_to_all(value, axes, split_axis=0, concat_axis=0, tiled=True)


def swapped(value):
    return lax.ppermute(value, "core", [(0, 1), (1, 0)])


def run(per, pos, cells, screen_mask, counts, green_occ, occ_mask, green_virt):
    cells, green_virt = in_hbm(cells), in_hbm(green_virt)
    first = pack(per, 0, pos, screen_mask, counts, green_virt, green_occ, cells)
    second = pack(per, 1, pos, screen_mask, counts, green_virt, green_occ, cells)
    first = exchange(first, AXES)
    second, first = lax.optimization_barrier((second, first))
    second = exchange(second, AXES)
    second = second.reshape(128 * LINES, second.shape[-1])
    first = first.reshape(128 * LINES, first.shape[-1])
    at = WIDE + rest_of(per, WIDE)
    virt = in_hbm(band(per, occ_mask, first))
    part_a = product(per, True, True, pos, virt, first, at, None)
    part_a = product(per, True, False, pos, virt, swapped(first), at, part_a)
    sent_a = along_x(part_a)
    second, _ = lax.optimization_barrier((second, part_a))
    part_b = product(per, False, True, pos, virt, second, 0, None)
    part_b = product(per, False, False, pos, virt, swapped(second), 0, part_b)
    sent_b = along_t(part_b)
    sent_a = along_t(middle(True, pos, sent_a))
    sent_b = along_x(middle(False, pos, sent_b))
    return total(sent_a + sent_b)


def positions(row, col):
    x, t = lax.axis_index("x"), lax.axis_index(("zlo", "ylo"))
    receivers = [(x + s) % 4 for s in range(4)] + [t ^ d for d in range(4)]
    return jnp.stack([row, col, lax.axis_index("core")] + receivers).astype(jnp.int32)


def local(three_centre, screen_mask, block_counts, green_occ, occ_mask, green_virt):
    row = lax.axis_index(ROWS)
    col = lax.axis_index(COLS)
    pos = positions(row, col)
    return lax.cond(
        block_counts[NB] > 3 * NG,
        functools.partial(run, 4),
        functools.partial(run, 3),
        pos,
        three_centre,
        screen_mask,
        block_counts,
        green_occ,
        occ_mask,
        green_virt,
    )


def solution(mesh):
    fine = Mesh(mesh.devices.reshape(SIZES), AXES)
    in_specs = (P(ROWS + COLS, None, None), P(), P(), P(ROWS, None), P(), P())
    return jax.shard_map(
        local, mesh=fine, in_specs=in_specs, out_specs=P(COLS, ROWS), check_vma=False
    )
```
